32 devices in a mesh: dp: 16 (over z, y, x), tensor: 2 (over core).
Axes of the slice: x: 2, y: 2, z: 4, core: 2. Of those that a mesh axis runs over, the one named last changes fastest.
Arguments:
- tokens: bfloat16 [16384, 768], P('dp'), may hold values from -6 to 6
- upper_delta: bfloat16 [16384, 768], P(('dp', 'tensor')), may hold values from -0.119628906 to 0.119628906
- segments: int32 [32, 512], P('dp'), may hold values from 0 to 3, as said below
- summary_index: int32 [32, 4], P('dp'), may hold values from 0 to 419, as said below
- validity: int32 [32, 512], P('dp'), may hold values from 0 to 1, as said below
- queries: bfloat16 [128, 768], P('dp'), may hold values from -15 to 15
- positives: int32 [128], P('dp'), may hold values from 0 to 127
- query_weight: bfloat16 [768, 768], P(None, 'tensor'), may hold values from -0.21875 to 0.21875
- key_weight: bfloat16 [768, 768], P(None, 'tensor'), may hold values from -0.21875 to 0.21875
- value_weight: bfloat16 [768, 768], P(None, 'tensor'), may hold values from -0.21875 to 0.21875
- query_bias: bfloat16 [768], P('tensor'), may hold values from -3 to 3
- value_bias: bfloat16 [768], P('tensor'), may hold values from -3 to 3
- output_weight: bfloat16 [768, 768], P('tensor'), may hold values from -1.25 to 1.25
- output_bias: bfloat16 [768], replicated, may hold values from -3 to 3
- first_gain: bfloat16 [768], replicated, may hold values from 0.25 to 1.75
- first_shift: bfloat16 [768], replicated, may hold values from -3 to 3
- up_weight: bfloat16 [768, 3072], P(None, 'tensor'), may hold values from -0.21875 to 0.21875
- up_bias: bfloat16 [3072], P('tensor'), may hold values from -3 to 3
- down_weight: bfloat16 [3072, 768], P('tensor'), may hold values from -0.109375 to 0.109375
- down_bias: bfloat16 [768], replicated, may hold values from -3 to 3
- second_gain: bfloat16 [768], replicated, may hold values from 0.25 to 1.75
Outputs:
- loss_terms: float32 [128], P('dp')
- query_gradient: float32 [128, 768], P('dp')
- token_gradient: bfloat16 [16384, 768], P(('dp', 'tensor'))
- query_weight_gradient: float32 [768, 768], P(None, 'tensor')
- key_weight_gradient: float32 [768, 768], P(None, 'tensor')
- value_weight_gradient: float32 [768, 768], P(None, 'tensor')
- query_bias_gradient: float32 [768], P('tensor')
- value_bias_gradient: float32 [768], P('tensor')
- output_weight_gradient: float32 [768, 768], P('tensor')
- output_bias_gradient: float32 [768], replicated
- first_gain_gradient: float32 [768], replicated
- first_shift_gradient: float32 [768], replicated
- up_weight_gradient: float32 [768, 3072], P(None, 'tensor')
- up_bias_gradient: float32 [3072], P('tensor')
- down_weight_gradient: float32 [3072, 768], P('tensor')
- down_bias_gradient: float32 [768], replicated
- second_gain_gradient: float32 [768], replicated
The draws below stay inside these ranges and needn't reach their ends.
Inputs may be any that keep to these rules, and one draw needn't show every extreme that they name: `segments`: along each row the numbers never fall; every one of the 4 passages of a row holds at least an eighth of 512 consecutive tokens, and padding tokens carry the last passage's number. `summary_index`: each entry is a valid token of passage k of its row, among that passage's first four tokens. `validity`: each row ends in a run of 1 to 64 padding tokens that lies inside its last passage; all other tokens are 1.
All inputs are finite; a program needn't handle non-finite values.
Results may differ from the reference program's by a relative error of at most 0.04.
Values may be sent and summed in bfloat16 or wider, within the bound.
No kernel may reach another device: no remote copies, remote signals or barrier semaphores. Data moves between devices by JAX's collectives and lax.ppermute only.
A program may use at most 192 MiB of HBM per device.

```python
import math
from functools import partial
import jax
import jax.numpy as jnp
from jax import lax

D = 768
HEADS = 12
HD = 64
FF = 3072
SEQ = 512
P_ROW = 4
ROWS = 32
TOKENS = 16384
PASS = 128
QUERIES = 128
N_TENSOR = 2


def row_starts(key):
    jitter = SEQ // (4 * P_ROW)
    stride = SEQ // P_ROW
    moves = jax.random.randint(key, (ROWS, P_ROW), -jitter, jitter + 1)
    order = jnp.arange(P_ROW, dtype=jnp.int32)[None, :]
    row_ids = jnp.arange(ROWS, dtype=jnp.int32)[:, None]
    farthest = (row_ids == ROWS - 1) & (order == P_ROW - 1)
    moves = jnp.where(farthest, jitter, moves)
    return jnp.where(order == 0, 0, order * stride + moves).astype(jnp.int32)


def draw_segments(key, part):
    starts = row_starts(key)
    places = jnp.arange(SEQ, dtype=jnp.int32)
    crossed = (places[None, :, None] >= starts[:, None, 1:]).astype(jnp.int32)
    return jnp.sum(crossed, -1).astype(jnp.int32)


def draw_summary_index(key, part):
    starts = row_starts(key)
    key = jax.random.fold_in(key, 5)
    offsets = jax.random.randint(key, (ROWS, P_ROW), 0, 4)
    order = jnp.arange(P_ROW, dtype=jnp.int32)[None, :]
    row_ids = jnp.arange(ROWS, dtype=jnp.int32)[:, None]
    offsets = jnp.where((row_ids == 0) & (order == 0), 0, offsets)
    offsets = jnp.where((row_ids == ROWS - 1) & (order == P_ROW - 1), 3, offsets)
    return (starts + offsets).astype(jnp.int32)


def draw_validity(key, part):
    key = jax.random.fold_in(key, 7)
    padding = jax.random.randint(key, (ROWS, 1), 1, SEQ // 8 + 1)
    places = jnp.arange(SEQ, dtype=jnp.int32)[None, :]
    return (places < SEQ - padding).astype(jnp.int32)


def with_ends(result, key, low, top_value):
    extent = result.shape
    place = [jax.random.randint(jax.random.fold_in(key, axis), (), 0, extent[axis]) for axis in range(len(extent))]
    result = result.at[tuple(place)].set(low)
    longest = extent.index(max(extent))
    place[longest] = (place[longest] + 1) % extent[longest]
    return result.at[tuple(place)].set(top_value)


def block_levels(stream_key, shape, pieces, least, top_value):
    level, own = 1.0, jax.random.fold_in(stream_key, 6)
    for axis_at, shards_of in pieces:
        heights = jnp.exp(jax.random.uniform(jax.random.fold_in(own, axis_at), (shards_of,), jnp.float32, least / len(pieces), top_value / len(pieces)))
        level = level * jnp.repeat(heights, shape[axis_at] // shards_of).reshape([-1 if axis == axis_at else 1 for axis in range(len(shape))])
    return level


def gaussian(key, dims, scale, most, cuts=(), held_as=jnp.bfloat16):
    level = block_levels(key, dims, cuts, -0.22, 0.18) if cuts else 1.0
    array = jax.random.normal(key, dims, jnp.float32) * scale * level
    return jnp.minimum(jnp.maximum(array, -most), most).astype(held_as)


def setup_inputs(seed: int = 0) -> dict:
    key_list = jax.random.split(jax.random.key(seed), 22)
    tokens = gaussian(key_list[0], (TOKENS, D), 1.0, 6.0, ((0, 16),))
    upper_delta = gaussian(key_list[1], (TOKENS, D), 0.02, 0.119628906, ((0, 32),))
    segments = draw_segments(jax.random.fold_in(key_list[21], 71), 0)
    summary_index = draw_summary_index(jax.random.fold_in(key_list[21], 71), 0)
    validity = draw_validity(jax.random.fold_in(key_list[21], 71), 0)
    queries = gaussian(key_list[5], (QUERIES, D), 2.5, 15.0, ((0, 16),))
    positives = with_ends(jax.random.randint(key_list[6], (QUERIES,), 0, PASS), jax.random.fold_in(key_list[6], 1), 0, PASS - 1).astype(jnp.int32)
    query_weight = gaussian(key_list[7], (D, D), D ** -0.5, 0.21875, ((1, 2),))
    key_weight = gaussian(key_list[8], (D, D), D ** -0.5, 0.21875, ((1, 2),))
    value_weight = gaussian(key_list[9], (D, D), D ** -0.5, 0.21875, ((1, 2),))
    query_bias = gaussian(key_list[10], (D,), 0.5, 3.0, ((0, 2),))
    value_bias = gaussian(key_list[11], (D,), 0.5, 3.0, ((0, 2),))
    output_weight = gaussian(key_list[12], (D, D), (D * 4 * P_ROW // SEQ) ** -0.5, 1.25, ((0, 2),))
    output_bias = gaussian(key_list[13], (D,), 0.5, 3.0)
    first_gain = jnp.clip(1.0 + 0.15 * jax.random.normal(key_list[14], (D,), jnp.float32), 0.25, 1.75).astype(jnp.bfloat16)
    first_shift = gaussian(key_list[15], (D,), 0.5, 3.0)
    up_weight = gaussian(key_list[16], (D, FF), D ** -0.5, 0.21875, ((1, 2),))
    up_bias = gaussian(key_list[17], (FF,), 0.5, 3.0, ((0, 2),))
    down_weight = gaussian(key_list[18], (FF, D), FF ** -0.5, 0.109375, ((0, 2),))
    down_bias = gaussian(key_list[19], (D,), 0.5, 3.0)
    second_gain = jnp.clip(1.0 + 0.15 * jax.random.normal(key_list[20], (D,), jnp.float32), 0.25, 1.75).astype(jnp.bfloat16)
    return dict(tokens=tokens, upper_delta=upper_delta, segments=segments, summary_index=summary_index, validity=validity, queries=queries, positives=positives, query_weight=query_weight, key_weight=key_weight, value_weight=value_weight, query_bias=query_bias, value_bias=value_bias, output_weight=output_weight, output_bias=output_bias, first_gain=first_gain, first_shift=first_shift, up_weight=up_weight, up_bias=up_bias, down_weight=down_weight, down_bias=down_bias, second_gain=second_gain)


@jax.custom_vjp
def low(v):
    return lax.optimization_barrier(v.astype(jnp.bfloat16)).astype(jnp.float32)

@jax.custom_vjp
def low_back(v):
    return v

def low_keep(v):
    return (low(v), None)

def low_pass(kept, grad):
    return (grad,)

def back_keep(v):
    return (v, None)

def back_low(kept, grad):
    return (low(grad),)
low.defvjp(low_keep, low_pass)
low_back.defvjp(back_keep, back_low)
norm_eps = 1e-05
neg_large = -1e+30

def matmul(left, right):
    return jnp.dot(left, right, precision=lax.Precision.HIGHEST, preferred_element_type=jnp.float32)

def layer_norm(inputs, norm_gain, norm_shift):
    center = inputs - lax.optimization_barrier(jnp.mean(inputs, -1, keepdims=True))
    spread = lax.optimization_barrier(jnp.mean(center * center, -1, keepdims=True))
    return center * lax.rsqrt(spread + norm_eps) * norm_gain + norm_shift

def gelu_exact(inputs):
    return 0.5 * inputs * (1.0 + lax.erf(inputs * (1.0 / math.sqrt(2.0))))

def encode_group(params, group_data):
    query_weight, key_weight, value_weight, query_bias, value_bias, output_weight, output_bias, first_gain, first_shift, up_weight, up_bias, down_weight, down_bias, second_gain = params
    inputs, segment_rows, validity_rows, summary_rows = group_data
    group_rows = segment_rows.shape[0]
    length = segment_rows.shape[1]
    visible = (segment_rows[:, :, None] == segment_rows[:, None, :]) & (validity_rows[:, None, :] > 0)
    width_part = D // N_TENSOR
    heads_part = HEADS // N_TENSOR
    units_part = FF // N_TENSOR
    scaling = 1.0 / math.sqrt(HD)
    head_shape = (group_rows, length, heads_part, HD)
    head_sum = jnp.zeros((group_rows * length, D), jnp.float32)
    for member in range(N_TENSOR):
        offset = member * width_part
        finish = offset + width_part
        query_heads = low_back(low(matmul(inputs, query_weight[:, offset:finish]) + query_bias[offset:finish])).reshape(head_shape)
        key_heads = low_back(low(matmul(inputs, key_weight[:, offset:finish]))).reshape(head_shape)
        value_heads = low_back(low(matmul(inputs, value_weight[:, offset:finish]) + value_bias[offset:finish])).reshape(head_shape)
        logits = low_back(jnp.einsum('gqhd,gkhd->ghqk', query_heads, key_heads, precision=lax.Precision.HIGHEST) * scaling)
        masked = jnp.where(visible[:, None], logits, neg_large)
        row_peak = lax.optimization_barrier(jnp.max(masked, -1, keepdims=True))
        row_exp = jnp.exp(masked - row_peak)
        weights = row_exp / lax.optimization_barrier(jnp.sum(row_exp, -1, keepdims=True))
        context = jnp.einsum('ghqk,gkhd->gqhd', low(weights), value_heads, precision=lax.Precision.HIGHEST)
        context = low_back(low(context.reshape(group_rows * length, width_part)))
        head_sum = head_sum + low(matmul(context, output_weight[offset:finish, :]))
    attended = low_back(head_sum) + output_bias
    first_out = layer_norm(inputs + attended, first_gain, first_shift)
    first_low = low(first_out)
    unit_sum = jnp.zeros((group_rows * length, D), jnp.float32)
    for member in range(N_TENSOR):
        offset = member * units_part
        finish = offset + units_part
        hidden = low_back(matmul(first_low, up_weight[:, offset:finish]) + up_bias[offset:finish])
        unit_sum = unit_sum + low(matmul(low(gelu_exact(hidden)), down_weight[offset:finish, :]))
    second_in = first_out + (low_back(unit_sum) + down_bias)
    encoded = layer_norm(second_in, second_gain, 0.0)
    flat_index = (jnp.arange(group_rows, dtype=jnp.int32)[:, None] * length + summary_rows.astype(jnp.int32)).reshape(-1)
    return (low(encoded[flat_index]), encoded)

def reference(tokens, upper_delta, segments, summary_index, validity, queries, positives, query_weight, key_weight, value_weight, query_bias, value_bias, output_weight, output_bias, first_gain, first_shift, up_weight, up_bias, down_weight, down_bias, second_gain):
    params = tuple((weight.astype(jnp.float32) for weight in (query_weight, key_weight, value_weight, query_bias, value_bias, output_weight, output_bias, first_gain, first_shift, up_weight, up_bias, down_weight, down_bias, second_gain)))
    length = segments.shape[1]
    group_rows = math.gcd(ROWS, max(1, 4096 // length))
    groups = ROWS // group_rows

    def forward(weights_in, inputs, query_rows):
        group_data = (inputs.reshape(groups, group_rows * length, D), segments.reshape(groups, group_rows, length), validity.reshape(groups, group_rows, length), summary_index.reshape(groups, group_rows, P_ROW))
        encoded, layer_out = lax.map(jax.checkpoint(partial(encode_group, weights_in)), group_data)
        passages = encoded.reshape(PASS, D)
        scores = low_back(matmul(query_rows, passages.T) * (1.0 / math.sqrt(D)))
        row_peak = lax.optimization_barrier(jnp.max(scores, -1, keepdims=True))
        log_total = row_peak[:, 0] + jnp.log(lax.optimization_barrier(jnp.sum(jnp.exp(scores - row_peak), -1)))
        chosen = jnp.arange(PASS, dtype=jnp.int32)[None, :] == positives.astype(jnp.int32)[:, None]
        picked = lax.optimization_barrier(jnp.sum(jnp.where(chosen, scores, 0.0), -1))
        return (log_total - picked, layer_out.reshape(TOKENS, D))
    (loss_terms, layer_out), pullback = jax.vjp(forward, params, tokens.astype(jnp.float32), queries.astype(jnp.float32))
    weight_gradients, token_gradient, query_gradient = pullback((jnp.ones_like(loss_terms), upper_delta.astype(jnp.float32)))
    return (loss_terms, query_gradient, token_gradient.astype(jnp.bfloat16), weight_gradients[0], weight_gradients[1], weight_gradients[2], weight_gradients[3], weight_gradients[4], weight_gradients[5], weight_gradients[6], weight_gradients[7], weight_gradients[8], weight_gradients[9], weight_gradients[10], weight_gradients[11], weight_gradients[12], weight_gradients[13])
```

```python
import math

import jax
import jax.numpy as jnp
from jax import lax
from jax.sharding import PartitionSpec as P

D = 768
HD = 64


norm_eps = 1e-05
neg_large = -1e30
root_half = 0.7071067811865476
inv_root_tau = 0.3989422804014327


def bits_of(axis):
    return lax.axis_size(axis).bit_length() - 1


def flip(value, axis, bit):
    size = lax.axis_size(axis)
    return lax.ppermute(value, axis, [(i, i ^ (1 << bit)) for i in range(size)])


def swap(value):
    return flip(value, "tensor", 0)


def own_bit(axis, bit):
    return (lax.axis_index(axis) >> bit) & 1


def join(value, other, high):
    return jnp.where(
        high == 1, jnp.concatenate([other, value], 0), jnp.concatenate([value, other], 0)
    )


def gather_dp(value):
    for bit in range(bits_of("dp")):
        value = join(value, flip(value, "dp", bit), own_bit("dp", bit))
    return value


def gather_all(value):
    value = join(value, swap(value), own_bit("tensor", 0))
    return gather_dp(value)


def reduce_small(value):
    for bit in range(bits_of("dp")):
        value = value + flip(value, "dp", bit)
    return value


def reduce_rows(value, order):
    for bit in order:
        half = value.shape[0] // 2
        mine = own_bit("dp", bit)
        sent = lax.dynamic_slice_in_dim(value, (1 - mine) * half, half, 0)
        kept = lax.dynamic_slice_in_dim(value, mine * half, half, 0)
        arrived = flip(sent, "dp", bit)
        value = (kept.astype(jnp.float32) + arrived.astype(jnp.float32)).astype(jnp.bfloat16)
    for bit in reversed(order):
        value = join(value, flip(value, "dp", bit), own_bit("dp", bit))
    return value


def reduce_halves(value):
    count = bits_of("dp")
    first = list(range(count))
    second = [1, 0] + first[2:]
    half = value.shape[0] // 2
    return jnp.concatenate(
        [reduce_rows(value[:half], first), reduce_rows(value[half:], second)], 0
    ).astype(jnp.float32)


def layer_norm(inputs, norm_gain, norm_shift):
    center = inputs - jnp.mean(inputs, -1, keepdims=True)
    spread = jnp.mean(center * center, -1, keepdims=True)
    row_scale = lax.rsqrt(spread + norm_eps)
    normed = center * row_scale
    return (normed * norm_gain + norm_shift, normed, row_scale)


def norm_back(out_delta, normed, row_scale, norm_gain):
    scaled = out_delta * norm_gain
    first_mean = jnp.mean(scaled, -1, keepdims=True)
    second_mean = jnp.mean(scaled * normed, -1, keepdims=True)
    in_delta = row_scale * (scaled - first_mean - normed * second_mean)
    return (in_delta, jnp.sum(out_delta * normed, 0), jnp.sum(out_delta, 0))


def dot(left, right):
    return jnp.dot(left, right, preferred_element_type=jnp.float32)


def dot_t(left, right):
    return lax.dot_general(left, right, (((1,), (1,)), ((), ())), preferred_element_type=jnp.float32)


def t_dot(left, right):
    return lax.dot_general(left, right, (((0,), (0,)), ((), ())), preferred_element_type=jnp.float32)


def shards(
    tokens,
    upper_delta,
    segments,
    summary_index,
    validity,
    queries,
    positives,
    query_weight,
    key_weight,
    value_weight,
    query_bias,
    value_bias,
    output_weight,
    output_bias,
    first_gain,
    first_shift,
    up_weight,
    up_bias,
    down_weight,
    down_bias,
    second_gain,
):
    f32, bf16 = jnp.float32, jnp.bfloat16
    row_count, length = segments.shape
    token_count = row_count * length
    members = lax.axis_size("tensor")
    place = lax.axis_index("tensor")
    own_count = token_count // members
    width_local = query_weight.shape[1]
    heads_local = width_local // HD
    head_shape = (row_count, length, heads_local, HD)
    scaling = 1.0 / math.sqrt(HD)
    score_scale = 1.0 / math.sqrt(D)

    def own(value):
        part = value.shape[0] // members
        return lax.dynamic_slice_in_dim(value, place * part, part, 0)

    def others(value):
        part = value.shape[0] // members
        return lax.dynamic_slice_in_dim(value, (1 - place) * part, part, 0)

    output_other = swap(output_weight)
    up_other = swap(up_weight)
    up_bias_other = swap(up_bias.reshape(1, -1))
    down_other = swap(down_weight)
    all_queries = gather_dp(queries)
    all_positives = gather_dp(positives.reshape(-1, 1)).reshape(-1)

    visible = ((segments[:, :, None] == segments[:, None, :]) & (validity[:, None, :] > 0))[:, None]
    query_heads = (
        (dot(tokens, query_weight) + query_bias.astype(f32)).astype(bf16).reshape(head_shape)
    )
    key_heads = dot(tokens, key_weight).astype(bf16).reshape(head_shape)
    value_heads = (
        (dot(tokens, value_weight) + value_bias.astype(f32)).astype(bf16).reshape(head_shape)
    )

    def masked_logits():
        product = (
            jnp.einsum("rqhd,rkhd->rhqk", query_heads, key_heads, preferred_element_type=f32)
            * scaling
        )
        return jnp.where(visible, product, neg_large)

    logits = masked_logits()
    row_peak = jnp.max(logits, -1, keepdims=True)
    row_exp = jnp.exp(logits - row_peak)
    row_total = jnp.sum(row_exp, -1, keepdims=True)
    weights_low = (row_exp / row_total).astype(bf16)
    log_total = row_peak + jnp.log(row_total)
    context = jnp.einsum("rhqk,rkhd->rqhd", weights_low, value_heads, preferred_element_type=f32)
    context = context.astype(bf16).reshape(token_count, width_local)

    context_in = swap(others(context))
    head_sum = dot(own(context), output_weight) + dot(context_in, output_other)
    own_tokens = own(tokens)
    first_out, first_normed, first_scale = layer_norm(
        own_tokens.astype(f32) + (head_sum + output_bias.astype(f32)),
        first_gain.astype(f32),
        first_shift.astype(f32),
    )
    first_low = first_out.astype(bf16)
    first_in = swap(first_low)

    def gelu(hidden):
        return (0.5 * hidden * (1.0 + lax.erf(hidden * root_half))).astype(bf16)

    def gelu_slope(hidden):
        return (
            0.5 * (1.0 + lax.erf(hidden * root_half))
            + hidden * jnp.exp(-0.5 * hidden * hidden) * inv_root_tau
        )

    hidden_other = dot(first_low, up_other) + up_bias_other.astype(f32)
    active_other = gelu(hidden_other)
    active_in = swap(active_other)
    hidden = dot(first_low, up_weight) + up_bias.astype(f32)
    active = gelu(hidden)
    unit_sum = dot(active, down_weight) + dot(active_other, down_other)
    second_out, second_normed, second_scale = layer_norm(
        first_out + (unit_sum + down_bias.astype(f32)), second_gain.astype(f32), 0.0
    )

    positions = own(summary_index).reshape(-1)
    at_summary = jnp.arange(own_count, dtype=jnp.int32)[None, :] == (
        positions + jnp.arange(own_count // length, dtype=jnp.int32).repeat(summary_index.shape[1]) * length
    )[:, None]
    summary_low = dot(at_summary.astype(bf16), second_out.astype(bf16)).astype(bf16)
    passages = gather_all(summary_low)
    scores = dot_t(all_queries, passages) * score_scale
    score_peak = jnp.max(scores, -1, keepdims=True)
    score_exp = jnp.exp(scores - score_peak)
    score_total = jnp.sum(score_exp, -1, keepdims=True)
    chosen = jnp.arange(scores.shape[1], dtype=jnp.int32)[None, :] == all_positives[:, None]
    losses = (
        score_peak[:, 0] + jnp.log(score_total[:, 0]) - jnp.sum(jnp.where(chosen, scores, 0.0), -1)
    )
    score_delta = (score_exp / score_total - chosen.astype(f32)).astype(bf16)
    query_count = queries.shape[0]
    query_start = lax.axis_index("dp") * query_count
    row_losses = lax.dynamic_slice_in_dim(losses, query_start, query_count, 0)
    query_gradient = (
        dot(lax.dynamic_slice_in_dim(score_delta, query_start, query_count, 0), passages)
        * score_scale
    )
    own_passages = summary_low.shape[0]
    passage_start = (lax.axis_index("dp") * members + place) * own_passages
    passage_delta = (
        t_dot(lax.dynamic_slice_in_dim(score_delta, passage_start, own_passages, 1), all_queries)
        * score_scale
    )

    out_delta = upper_delta.astype(f32)
    for k in range(own_passages):
        out_delta = out_delta + jnp.where(at_summary[k][:, None], passage_delta[k][None, :], 0.0)
    second_delta, second_gain_gradient, _ = norm_back(
        out_delta, second_normed, second_scale, second_gain.astype(f32)
    )
    down_bias_gradient = jnp.sum(second_delta, 0)
    unit_delta = second_delta.astype(bf16)
    unit_in = swap(unit_delta)
    delta_other = (dot_t(unit_delta, down_other) * gelu_slope(hidden_other)).astype(bf16)
    delta_in = swap(delta_other)
    hidden_delta = (dot_t(unit_delta, down_weight) * gelu_slope(hidden)).astype(bf16)
    down_weight_gradient = (t_dot(active, unit_delta) + t_dot(active_in, unit_in)).astype(bf16)
    up_weight_gradient = (t_dot(first_low, hidden_delta) + t_dot(first_in, delta_in)).astype(bf16)
    up_bias_gradient = jnp.sum(hidden_delta, 0, dtype=f32) + jnp.sum(delta_in, 0, dtype=f32)
    back_sum = dot_t(hidden_delta, up_weight) + dot_t(delta_other, up_other)
    first_delta, first_gain_gradient, first_shift_gradient = norm_back(
        second_delta + back_sum, first_normed, first_scale, first_gain.astype(f32)
    )
    output_bias_gradient = jnp.sum(first_delta, 0)
    branch_own = first_delta.astype(bf16)
    branch_delta = join(branch_own, swap(branch_own), place)

    output_weight_gradient = t_dot(branch_delta, context).astype(bf16)
    context_delta = dot_t(branch_delta, output_weight).astype(bf16).reshape(head_shape)
    weights_again = jnp.exp(masked_logits() - log_total)
    weight_delta = jnp.einsum(
        "rqhd,rkhd->rhqk", context_delta, value_heads, preferred_element_type=f32
    )
    inner_sum = jnp.sum(weights_again * weight_delta, -1, keepdims=True)
    logit_delta = (weights_again * (weight_delta - inner_sum)).astype(bf16)
    query_delta = (
        (
            jnp.einsum("rhqk,rkhd->rqhd", logit_delta, key_heads, preferred_element_type=f32)
            * scaling
        )
        .astype(bf16)
        .reshape(token_count, width_local)
    )
    key_delta = (
        (
            jnp.einsum("rhqk,rqhd->rkhd", logit_delta, query_heads, preferred_element_type=f32)
            * scaling
        )
        .astype(bf16)
        .reshape(token_count, width_local)
    )
    value_delta = (
        jnp.einsum(
            "rhqk,rqhd->rkhd",
            weights_again.astype(bf16),
            context_delta,
            preferred_element_type=f32,
        )
        .astype(bf16)
        .reshape(token_count, width_local)
    )
    query_bias_gradient = jnp.sum(query_delta, 0, dtype=f32)
    value_bias_gradient = jnp.sum(value_delta, 0, dtype=f32)

    def input_part(rows):
        return (
            dot_t(rows(query_delta), query_weight)
            + dot_t(rows(key_delta), key_weight)
            + dot_t(rows(value_delta), value_weight)
        )

    input_in = swap(input_part(others).astype(bf16))
    token_gradient = (first_delta + input_part(own) + input_in.astype(f32)).astype(bf16)

    head_gradients = jnp.concatenate(
        [
            t_dot(tokens, query_delta).astype(bf16),
            t_dot(tokens, key_delta).astype(bf16),
            t_dot(tokens, value_delta).astype(bf16),
            output_weight_gradient,
        ],
        1,
    )
    down_total = reduce_halves(down_weight_gradient)
    up_total = reduce_halves(up_weight_gradient)
    head_total = reduce_halves(head_gradients)

    shared = jnp.stack(
        [
            output_bias_gradient,
            first_gain_gradient,
            first_shift_gradient,
            down_bias_gradient,
            second_gain_gradient,
        ]
    )
    shared = shared + swap(shared)
    small = reduce_small(
        jnp.concatenate(
            [
                shared.reshape(-1),
                up_bias_gradient,
                query_bias_gradient,
                value_bias_gradient,
            ]
        ).reshape(1, -1)
    ).reshape(-1)
    width = D
    units = up_bias.shape[0]
    parts = [small[i * width : (i + 1) * width] for i in range(5)]
    rest = small[5 * width :]
    return (
        row_losses,
        query_gradient,
        token_gradient,
        head_total[:, :width_local],
        head_total[:, width_local : 2 * width_local],
        head_total[:, 2 * width_local : 3 * width_local],
        rest[units : units + width_local],
        rest[units + width_local :],
        head_total[:, 3 * width_local :].T,
        parts[0],
        parts[1],
        parts[2],
        up_total,
        rest[:units],
        down_total,
        parts[3],
        parts[4],
    )


def solution(mesh):
    in_specs = (
        P("dp", None),
        P(("dp", "tensor"), None),
        P("dp", None),
        P("dp", None),
        P("dp", None),
        P("dp", None),
        P("dp"),
        P(None, "tensor"),
        P(None, "tensor"),
        P(None, "tensor"),
        P("tensor"),
        P("tensor"),
        P("tensor", None),
        P(),
        P(),
        P(),
        P(None, "tensor"),
        P("tensor"),
        P("tensor", None),
        P(),
        P(),
    )
    out_specs = (
        P("dp"),
        P("dp", None),
        P(("dp", "tensor"), None),
        P(None, "tensor"),
        P(None, "tensor"),
        P(None, "tensor"),
        P("tensor"),
        P("tensor"),
        P("tensor", None),
        P(),
        P(),
        P(),
        P(None, "tensor"),
        P("tensor"),
        P("tensor", None),
        P(),
        P(),
    )
    return jax.shard_map(shards, mesh=mesh, in_specs=in_specs, out_specs=out_specs, check_vma=False)
```

```python
import functools
import math

import jax
import jax.numpy as jnp
from jax import lax
from jax.experimental import pallas as pl
from jax.experimental.pallas import tpu as pltpu
from jax.sharding import PartitionSpec as P

D = 768
HD = 64
LANES = 128

norm_eps = 1e-05
neg_large = -1e30
root_half = 0.7071067811865476
inv_root_tau = 0.3989422804014327
log2_e = 1.4426950408889634

f32, bf16 = jnp.float32, jnp.bfloat16
COSTS = dict(
    attend_far=9, attend_near=9, forward=17, loss_back=6, unit_back_far=6, unit_back_near=6, down_gradient=7,
    up_gradient=7, first_back=9, attend_back_near=10, attend_back_far=10, head_gradients=8, add_halves=3,
    add_chunks=2, add_four=2, join_chunks=2, join_quarters=2, finish_down=4, finish_up=4, finish_heads=4,
)
FLOPS = int(2.3e9)
VMEM_GRANT = 63 << 20
SMALL = 16


def bits_of(axis):
    return lax.axis_size(axis).bit_length() - 1


def flip_by(value, axis, mask):
    size = lax.axis_size(axis)
    return lax.ppermute(value, axis, [(i, i ^ mask) for i in range(size)])


def swap(value):
    return flip_by(value, "tensor", 1)


def own_bit(axis, bit):
    return (lax.axis_index(axis) >> bit) & 1


def join(value, other, high):
    return jnp.where(
        high == 1, jnp.concatenate([other, value], 0), jnp.concatenate([value, other], 0)
    )


def gather_dp(value):
    for bit in range(bits_of("dp")):
        value = join(value, flip_by(value, "dp", 1 << bit), own_bit("dp", bit))
    return value


def gather_all(value):
    value = join(value, swap(value), own_bit("tensor", 0))
    return gather_dp(value)


def dot(left, right):
    return jnp.dot(left, right, preferred_element_type=f32)


def dot_t(left, right):
    return lax.dot_general(left, right, (((1,), (1,)), ((), ())), preferred_element_type=f32)


def t_dot(left, right):
    return lax.dot_general(left, right, (((0,), (0,)), ((), ())), preferred_element_type=f32)


class Late:
    def __init__(self, source, held, semaphore):
        self.held, self.waited = held, False
        self.shape, self.dtype = held.shape, held.dtype
        self.copy = pltpu.make_async_copy(source, held, semaphore)
        self.copy.start()

    def wait(self):
        if not self.waited:
            self.copy.wait()
        self.waited = True
        return self.held


class Early:
    def __init__(self, held, target, semaphore):
        self.held, self.target, self.semaphore, self.sent = held, target, semaphore, False
        self.shape, self.dtype = held.shape, held.dtype

    def __getitem__(self, at):
        return self.held[at]

    def __setitem__(self, at, value):
        self.held[at] = value

    def send(self, *at):
        source, target = (self.held.at[at], self.target.at[at]) if at else (self.held, self.target)
        pltpu.make_async_copy(source, target, self.semaphore).start()
        self.sent = True

    def finish(self):
        if not self.sent:
            self.send()
        pltpu.make_async_copy(self.held, self.target, self.semaphore).wait()


def ready(*values):
    return [value.wait() if isinstance(value, Late) else value for value in values]


def call(kernel, name, outs, *args, scratch=(), late=(), early=(), order=None, parts=None):
    parts, after = parts or {}, order or []
    count, waits, made = len(args), len(after), len(outs)
    held = [
        pltpu.VMEM(parts[i][0] if i in parts else args[i].shape, args[i].dtype) for i in late
    ] + [pltpu.VMEM(*outs[i]) for i in early]

    def body(*refs):
        inputs = list(refs[:count])
        results = list(refs[count + waits : count + waits + made])
        rest = refs[count + waits + made :]
        scratches, rest = rest[: len(scratch)], rest[len(scratch) :]
        for k, i in enumerate(late):
            source = parts[i][1](inputs[0], inputs[i]) if i in parts else inputs[i]
            inputs[i] = Late(source, rest[k], rest[-1].at[k])
        for k, i in enumerate(early):
            k += len(late)
            results[i] = Early(rest[k], results[i], rest[-1].at[k])
        kernel(*inputs, *results, *scratches)
        for i in late:
            inputs[i].wait()
        for i in early:
            results[i].finish()

    specs = [pl.BlockSpec(memory_space=pltpu.SMEM)]
    specs += [pl.BlockSpec(memory_space=pl.ANY if i in late else pltpu.VMEM) for i in range(1, count)]
    specs += [pl.BlockSpec(memory_space=pl.ANY)] * waits
    own = [pltpu.SemaphoreType.DMA((len(held),))] if held else []
    made_by = pl.pallas_call(
        body,
        name=name,
        out_shape=[jax.ShapeDtypeStruct(s, t) for s, t in outs],
        in_specs=specs,
        out_specs=[pl.BlockSpec(memory_space=pl.ANY if i in early else pltpu.VMEM) for i in range(made)],
        scratch_shapes=[*scratch, *held, *own],
        compiler_params=pltpu.CompilerParams(vmem_limit_bytes=VMEM_GRANT),
        cost_estimate=pl.CostEstimate(
            flops=int(COSTS[name] * FLOPS), bytes_accessed=1, transcendentals=0
        ),
    )(*args, *after)
    if order is not None:
        order[:] = [made_by[-1]]
    return made_by


def rows_at(index, size):
    return pl.ds(pl.multiple_of(index * size, size), size)


def add_low(left, right):
    return (left.astype(f32) + right.astype(f32)).astype(bf16)


BX, BY, BZ, BT, BD, PLACES = range(6)


def add_halves(info, keep_a, came_a, keep_b, came_b, send_a, kept_a, send_b, kept_b):
    quarter = keep_b.shape[0] // 2
    for bit, keep, came, send, kept in (
        (info[BY], keep_a, came_a, send_a, kept_a),
        (info[BX], keep_b, came_b, send_b, kept_b),
    ):
        mine, other = rows_at(bit, quarter), rows_at(1 - bit, quarter)
        send[:quarter] = add_low(keep[other], came[other])
        kept[:quarter] = add_low(keep[mine], came[mine])
        if keep.shape[0] > 2 * quarter:
            extra = add_low(keep[2 * quarter :], came[2 * quarter :])
            send[quarter:] = extra
            kept[quarter:] = extra


def add_chunks(info, keep_a, came_a, keep_b, came_b, own, one, two, three):
    quarter = keep_b.shape[0]
    chunk = quarter // 4
    for step, out in enumerate((own, one, two, three)):
        at = rows_at(info[BZ] ^ step, chunk)
        out[:chunk] = add_low(keep_a[at], came_a[at])
        out[chunk : 2 * chunk] = add_low(keep_b[at], came_b[at])
        if keep_a.shape[0] > quarter:
            out[2 * chunk :] = add_low(keep_a[quarter:], came_a[quarter:])


def add_four(info, own, one, two, three, total):
    total[...] = (
        (own[...].astype(f32) + one[...].astype(f32))
        + (two[...].astype(f32) + three[...].astype(f32))
    ).astype(bf16)


def join_chunks(info, own, one, two, three, quarter_a, quarter_b):
    chunk = quarter_a.shape[0] // 4
    for step, part in enumerate((own, one, two, three)):
        at = rows_at(info[BZ] ^ step, chunk)
        quarter_a[at] = part[:chunk]
        quarter_b[at] = part[chunk : 2 * chunk]


def join_quarters(info, own_a, came_a, own_b, came_b, half_a, half_b):
    size = own_a.shape[0]
    for bit, own, came, half in (
        (info[BY], own_a, came_a, half_a),
        (info[BX], own_b, came_b, half_b),
    ):
        half[rows_at(bit, size)] = own[...]
        half[rows_at(1 - bit, size)] = came[...]


def finish_down(info, own_a, came_a, own_b, came_b, out):
    size = own_a.shape[0]
    for part, bit, own, came in ((0, info[BX], own_a, came_a), (1, info[BY], own_b, came_b)):
        out[rows_at(2 * part + bit, size)] = own[...].astype(f32)
        out[rows_at(2 * part + 1 - bit, size)] = came[...].astype(f32)


def finish_up(info, own_a, came_a, own_b, came_b, out):
    size, width = own_a.shape
    for part, bit, own, came in ((0, info[BX], own_a, came_a), (1, info[BY], own_b, came_b)):
        columns = pl.ds(part * width, width)
        out[rows_at(bit, size), columns] = own[...].astype(f32)
        out[rows_at(1 - bit, size), columns] = came[...].astype(f32)


def finish_heads(info, own_a, came_a, own_b, came_b, query, key, value, output):
    size, width = own_a.shape
    half = width // 2
    for part, bit, own, came in ((0, info[BX], own_a, came_a), (1, info[BY], own_b, came_b)):
        left, right = ((query, key), (value, None))[part]
        for at, source in ((bit, own), (1 - bit, came)):
            left[rows_at(at, size)] = source[:, :half].astype(f32)
            if right is None:
                output[:, rows_at(at, size)] = source[:, half:].astype(f32).T
            else:
                right[rows_at(at, size)] = source[:, half:].astype(f32)


class Reduction:
    def __init__(self, info, order, halves):
        self.info, self.order = info, order
        self.made = halves
        send_a, send_b, self.keep_a, self.keep_b = halves
        self.came = [flip_by(send_a, "dp", 1), flip_by(send_b, "dp", 2)]

    def staged(self, kernel, outs, *args):
        self.made = call(kernel, kernel.__name__, outs, self.info, *args, order=self.order)
        return self.made

    def quarters(self):
        (first, width), half = self.keep_a.shape, self.keep_b.shape[0]
        self.extra, self.quarter = first - half, half // 2
        a, b = ((self.quarter + self.extra, width), bf16), ((self.quarter, width), bf16)
        send_a, keep_a, send_b, keep_b = self.staged(
            add_halves, [a, a, b, b], self.keep_a, self.came[0], self.keep_b, self.came[1]
        )
        self.keep_a, self.keep_b, self.width = keep_a, keep_b, width
        self.came = [flip_by(send_a, "dp", 2), flip_by(send_b, "dp", 1)]

    def chunks(self):
        self.piece = ((self.quarter // 2 + self.extra, self.width), bf16)
        self.own, *sent = self.staged(
            add_chunks, [self.piece] * 4, self.keep_a, self.came[0], self.keep_b, self.came[1]
        )
        self.came = [flip_by(s, "dp", 4 * (k + 1)) for k, s in enumerate(sent)]

    def total(self):
        (total,) = self.staged(add_four, [self.piece], self.own, *self.came)
        for bit in range(4, bits_of("dp")):
            total = add_low(total, flip_by(total, "dp", 1 << bit))
        rows = self.quarter // 2
        self.small = total[rows:] if self.extra else None
        self.own = total[:rows] if self.extra else total
        self.came = [flip_by(self.own, "dp", 4 * (k + 1)) for k in range(3)]

    def join_four(self):
        whole = ((self.quarter, self.width), bf16)
        self.keep_a, self.keep_b = self.staged(join_chunks, [whole] * 2, self.own, *self.came)
        self.came = [flip_by(self.keep_a, "dp", 2), flip_by(self.keep_b, "dp", 1)]

    def join_two(self):
        whole = ((2 * self.quarter, self.width), bf16)
        self.keep_a, self.keep_b = self.staged(
            join_quarters, [whole] * 2, self.keep_a, self.came[0], self.keep_b, self.came[1]
        )
        self.came = [flip_by(self.keep_a, "dp", 1), flip_by(self.keep_b, "dp", 2)]

    def finish(self, kernel, outs):
        return self.staged(kernel, outs, self.keep_a, self.came[0], self.keep_b, self.came[1])


def down_gradient(info, unit, active, unit_in, active_in, send_a, send_b, keep_a, keep_b):
    size = send_a.shape[0]
    unit, active, unit_in, active_in = ready(unit, active, unit_in, active_in)
    for side in range(2):
        for part, bit, outs in ((0, info[BX], (send_a, keep_a)), (1, info[BY], (send_b, keep_b))):
            at = rows_at(2 * part + (bit if side else 1 - bit), size)
            outs[side][...] = (
                t_dot(active[:, at], unit[...]) + t_dot(active_in[:, at], unit_in[...])
            ).astype(bf16)
            outs[side].send()


def up_gradient(info, delta, first, delta_in, first_in, send_a, send_b, keep_a, keep_b, bias):
    size, width = send_a.shape
    delta, first, delta_in, first_in = ready(delta, first, delta_in, first_in)
    for side in range(2):
        for part, bit, outs in ((0, info[BX], (send_a, keep_a)), (1, info[BY], (send_b, keep_b))):
            columns = pl.ds(part * width, width)
            at = rows_at(bit if side else 1 - bit, size)
            outs[side][...] = (
                t_dot(first[:, at], delta[:, columns]) + t_dot(first_in[:, at], delta_in[:, columns])
            ).astype(bf16)
            outs[side].send()
    ones = jnp.ones((8, delta.shape[0]), bf16)
    bias[...] = dot(ones, delta[...]) + dot(ones, delta_in[...])


def head_gradients(
    info, tokens, query, query_far, key, key_far, value, value_far, branch, branch_far,
    context, context_far, shared, shared_in, bias, send_a, send_b, keep_a, keep_b,
):
    half, width = send_b.shape
    tokens, branch, branch_far, context, context_far = ready(tokens, branch, branch_far, context, context_far)
    value, value_far, query, query_far, key, key_far = ready(value, value_far, query, query_far, key, key_far)
    narrow = query.shape[1]
    length = query.shape[0]
    near, far = rows_at(info[BT], length), rows_at(1 - info[BT], length)
    for side in range(2):
        for part, bit, outs in ((1, info[BY], (send_b, keep_b)), (0, info[BX], (send_a, keep_a))):
            out = outs[side]
            at = rows_at(bit if side else 1 - bit, half)
            tokens_near, tokens_far = tokens[near, at], tokens[far, at]
            if part == 0:
                left = t_dot(tokens_near, query[...]) + t_dot(tokens_far, query_far[...])
                right = t_dot(tokens_near, key[...]) + t_dot(tokens_far, key_far[...])
            else:
                left = t_dot(tokens_near, value[...]) + t_dot(tokens_far, value_far[...])
                right = t_dot(branch[:, at], context[...]) + t_dot(branch_far[:, at], context_far[...])
            out[:half, :narrow] = left.astype(bf16)
            out[:half, narrow:] = right.astype(bf16)
            out.send(pl.ds(0, half))
    ones = jnp.ones((8, length), bf16)
    query_sum = dot(ones, query[...]) + dot(ones, query_far[...])
    value_sum = dot(ones, value[...]) + dot(ones, value_far[...])
    last = jnp.concatenate([query_sum, value_sum], 1)
    rows = lax.broadcasted_iota(jnp.int32, (8, width), 0)
    block = shared[...] + shared_in[...]
    block = jnp.where(rows == 5, bias[:, :width], jnp.where(rows == 6, bias[:, width:], block))
    block = jnp.where(rows == 7, last, block)
    block = jnp.concatenate([block, jnp.zeros_like(block)], 0).astype(bf16)
    for out in (send_a, keep_a):
        out[half:] = block
        out.send(pl.ds(half, SMALL))


def pair_columns(pair):
    return pl.ds(pl.multiple_of(pair * LANES, LANES), LANES)


def attend(
    info, tokens, query_weight, key_weight, value_weight, query_bias, value_bias, segments, validity,
    context, query, key, value, weights, shade, *, far,
):
    length = context.shape[0]
    row = 1 - info[BT] if far else info[BT]
    mark = segments[pl.ds(row, 1)]
    seen = jnp.where(validity[pl.ds(row, 1)] > 0, mark, -1)
    column = jnp.broadcast_to(mark.astype(f32), (8, length)).T[:, :1]
    shade[...] = jnp.where(column == seen.astype(f32), 0.0, neg_large)
    x, query_weight = ready(tokens, query_weight)
    query[...] = (dot(x[...], query_weight[...]) + query_bias[...].astype(f32)[None]).astype(bf16)
    query.send()
    (key_weight,) = ready(key_weight)
    key[...] = dot(x[...], key_weight[...]).astype(bf16)
    key.send()
    (value_weight,) = ready(value_weight)
    value[...] = (dot(x[...], value_weight[...]) + value_bias[...].astype(f32)[None]).astype(bf16)
    value.send()
    low = lax.broadcasted_iota(jnp.int32, (length, LANES), 1) < HD
    scale = log2_e / math.sqrt(HD)

    def body(pair, _):
        at = pair_columns(pair)
        q, k, v = query[:, at], key[:, at], value[:, at]
        parts = []
        for member in range(2):
            side = jnp.where(low if member == 0 else ~low, q, jnp.zeros_like(q))
            logits = dot_t(side, k) * scale + shade[...]
            peak = jnp.max(logits, -1, keepdims=True)
            raised = jnp.exp2(logits - peak)
            total = jnp.sum(raised, -1, keepdims=True)
            share = (raised * (1.0 / total)).astype(bf16)
            weights[2 * pair + member] = share
            weights.send(2 * pair + member)
            parts.append(dot(share, v))
        context[:, at] = jnp.where(low, parts[0], parts[1]).astype(bf16)
        return 0

    lax.fori_loop(0, context.shape[1] // LANES, body, 0)


def attend_back(
    info, branch, output_weight, value, context, weights, key, query, query_weight, key_weight, value_weight,
    query_delta, key_delta, value_delta, part, context_delta,
):
    length = part.shape[0]
    branch, output_weight = ready(branch, output_weight)
    context_delta[...] = dot_t(branch[...], output_weight[...]).astype(bf16)
    value, context, weights, key, query = ready(value, context, weights, key, query)
    low = lax.broadcasted_iota(jnp.int32, (length, LANES), 1) < HD
    scale = 1.0 / math.sqrt(HD)

    def body(pair, _):
        at = pair_columns(pair)
        q, k, v, delta = query[:, at], key[:, at], value[:, at], context_delta[:, at]
        product = delta.astype(f32) * context[:, at].astype(f32)
        queries, keys, values = [], [], []
        for member in range(2):
            mine = low if member == 0 else ~low
            inner = jnp.sum(jnp.where(mine, product, 0.0), -1, keepdims=True)
            side = jnp.where(mine, delta, jnp.zeros_like(delta))
            share = weights[2 * pair + member]
            logit_delta = (share.astype(f32) * (dot_t(side, v) - inner)).astype(bf16)
            queries.append(dot(logit_delta, k))
            keys.append(t_dot(logit_delta, q))
            values.append(t_dot(share, delta))
        query_delta[:, at] = (jnp.where(low, queries[0], queries[1]) * scale).astype(bf16)
        key_delta[:, at] = (jnp.where(low, keys[0], keys[1]) * scale).astype(bf16)
        value_delta[:, at] = jnp.where(low, values[0], values[1]).astype(bf16)
        return 0

    lax.fori_loop(0, query.shape[1] // LANES, body, 0)
    query_delta.send()
    key_delta.send()
    value_delta.send()
    query_weight, key_weight, value_weight = ready(query_weight, key_weight, value_weight)
    part[...] = (
        dot_t(query_delta[...], query_weight[...])
        + dot_t(key_delta[...], key_weight[...])
        + dot_t(value_delta[...], value_weight[...])
    ).astype(part.dtype)


OB, FG, FS, DB, SG = range(5)


def center(inputs):
    shifted = inputs - jnp.mean(inputs, -1, keepdims=True)
    spread = jnp.mean(shifted * shifted, -1, keepdims=True)
    row_scale = lax.rsqrt(spread + norm_eps)
    return shifted * row_scale, row_scale


def norm_back(out_delta, normed, row_scale, norm_gain):
    scaled = out_delta * norm_gain
    first_mean = jnp.mean(scaled, -1, keepdims=True)
    second_mean = jnp.mean(scaled * normed, -1, keepdims=True)
    return row_scale * (scaled - first_mean - normed * second_mean)


def forward(
    info, context, output_near, x, context_in, output_far, up_far, down_far, up_near, down_near, vectors,
    bias_near, bias_far, first_low, first_normed, first_scale, active_near, active_far, slope_near, slope_far,
    second_normed, second_scale, summary, total,
):
    length = total.shape[0]
    step = length // 2
    halves = (pl.ds(0, step), pl.ds(step, step))
    context, output_near, x, context_in, output_far = ready(context, output_near, x, context_in, output_far)
    for at in halves:
        heads = dot(context[at], output_near[...]) + dot(context_in[at], output_far[...])
        normed, scale = center(x[at].astype(f32) + (heads + vectors[OB : OB + 1]))
        out = normed * vectors[FG : FG + 1] + vectors[FS : FS + 1]
        first_normed[at] = normed.astype(bf16)
        first_scale[at] = scale
        first_low[at] = out.astype(bf16)
        total[at] = out + vectors[DB : DB + 1]
    first_low.send()
    first_normed.send()

    width = 3 * LANES
    for up, down, bias, active, slope in (
        (up_far, down_far, bias_far, active_far, slope_far),
        (up_near, down_near, bias_near, active_near, slope_near),
    ):
        up, down = ready(up, down)

        def body(index, _, up=up, down=down, bias=bias, active=active, slope=slope):
            units = rows_at(index, width)
            for at in halves:
                hidden = dot(first_low[at], up[:, units]) + bias[:, units]
                share = 0.5 * (1.0 + lax.erf(hidden * root_half))
                low = (hidden * share).astype(bf16)
                active[at, units] = low
                slope[at, units] = (
                    share + hidden * jnp.exp(-0.5 * hidden * hidden) * inv_root_tau
                ).astype(bf16)
                total[at] += dot(low, down[units])
            active.send(slice(None), units)
            slope.send(slice(None), units)
            return 0

        lax.fori_loop(0, up.shape[1] // width, body, 0)

    for at in halves:
        normed, scale = center(total[at])
        second_normed[at] = normed.astype(bf16)
        second_scale[at] = scale
        total[at] = normed * vectors[SG : SG + 1]
    second_normed.send()
    rows = [total[pl.ds(info[PLACES + k], 1)] for k in range(summary.shape[0])]
    summary[...] = jnp.concatenate(rows, 0).astype(bf16)


def loss_back(*refs, pieces):
    info, *sources = refs[: 1 + pieces]
    (
        upper, normed, scale, vectors, losses, query_gradient, second_delta, unit_delta, sums, all_rows, deltas,
        lost, out_delta,
    ) = refs[1 + pieces :]
    width = upper.shape[1]
    size = sources[0].shape[0]
    for step, source in enumerate(sources):
        all_rows[rows_at(info[BZ] ^ step, size) if pieces > 1 else pl.ds(0, size)] = source[...]
    count = all_rows.shape[0]
    block = min(256, count)
    score_scale = 1.0 / math.sqrt(width)
    own_passages = 4
    upper, normed = ready(upper, normed)
    out_delta[...] = upper[...].astype(f32)

    def body(index, sums_in):
        at = rows_at(index, block)
        rows = all_rows[at, :width]
        digits = all_rows[at, width:].astype(f32)
        scores = dot_t(rows, all_rows[:, :width]) * score_scale
        columns = lax.broadcasted_iota(jnp.int32, (block, count), 1)
        numbers = lax.broadcasted_iota(jnp.int32, (block, 1), 0)
        scores = jnp.where((columns & 15) < 8, scores, neg_large)
        peak = jnp.max(scores, -1, keepdims=True)
        raised = jnp.exp(scores - peak)
        total = jnp.sum(raised, -1, keepdims=True)
        target = (digits[:, 0:1] * 16.0 + digits[:, 1:2]).astype(jnp.int32)
        chosen = columns == target
        lost[at] = peak + jnp.log(total) - jnp.sum(jnp.where(chosen, scores, 0.0), -1, keepdims=True)
        delta = (raised / total - chosen.astype(f32)).astype(bf16)
        delta = jnp.where((numbers & 15) >= 8, delta, jnp.zeros_like(delta))
        deltas[at] = delta
        wide = delta.astype(f32)
        results = []
        for k in range(own_passages):
            column = info[BD] * 16 + info[BT] * own_passages + k
            share = jnp.sum(jnp.where(columns == column, wide, 0.0), -1, keepdims=True)
            results.append(sums_in[k] + jnp.sum(share * rows.astype(f32), 0, keepdims=True))
        return tuple(results)

    zero = jnp.zeros((1, width), f32)
    passage_delta = lax.fori_loop(0, count // block, body, (zero,) * own_passages)
    for k in range(own_passages):
        out_delta[pl.ds(info[PLACES + k], 1)] += passage_delta[k] * score_scale
    own = pl.multiple_of(info[BD] * 16, 16)
    own_delta = deltas[pl.ds(own, 16)]
    query_gradient[...] = (dot(own_delta, all_rows[:, :width]) * score_scale)[8:]
    losses[...] = lost[pl.ds(pl.multiple_of(own + 8, 8), 8)]

    length = upper.shape[0]
    step = length // 4
    bias_sum = gain_sum = zero
    for start in range(0, length, step):
        at = pl.ds(start, step)
        n = normed[at].astype(f32)
        delta = norm_back(out_delta[at], n, scale[at], vectors[SG : SG + 1])
        unit_delta[at] = delta.astype(bf16)
        second_delta[at] = delta
        unit_delta.send(at)
        second_delta.send(at)
        bias_sum += jnp.sum(delta, 0, keepdims=True)
        gain_sum += jnp.sum(out_delta[at] * n, 0, keepdims=True)
    sums[...] = jnp.concatenate(
        [jnp.zeros((DB, width), f32), bias_sum, gain_sum, jnp.zeros((7 - SG, width), f32)], 0
    )


def unit_back(info, unit_delta, down_weight, slope, hidden_delta):
    width = 3 * LANES
    unit_delta, down_weight, slope = ready(unit_delta, down_weight, slope)

    def body(index, _):
        units = rows_at(index, width)
        delta = dot_t(unit_delta[...], down_weight[units])
        hidden_delta[:, units] = (delta * slope[:, units].astype(f32)).astype(bf16)
        hidden_delta.send(slice(None), units)
        return 0

    lax.fori_loop(0, down_weight.shape[0] // width, body, 0)


def first_back(
    info, delta_far, up_far, delta_near, up_near, second_delta, normed, scale, vectors, sums_in, first_delta,
    branch, sums, total,
):
    length, width = total.shape
    delta_far, up_far = ready(delta_far, up_far)
    total[...] = dot_t(delta_far[...], up_far[...])
    delta_near, up_near = ready(delta_near, up_near)
    total[...] += dot_t(delta_near[...], up_near[...])
    second_delta, normed = ready(second_delta, normed)
    step = length // 4
    zero = jnp.zeros((1, width), f32)
    bias_sum = gain_sum = shift_sum = zero
    for start in range(0, length, step):
        at = pl.ds(start, step)
        out_delta = second_delta[at] + total[at]
        n = normed[at].astype(f32)
        delta = norm_back(out_delta, n, scale[at], vectors[FG : FG + 1])
        branch[at] = delta.astype(bf16)
        first_delta[at] = delta
        branch.send(at)
        first_delta.send(at)
        bias_sum += jnp.sum(delta, 0, keepdims=True)
        gain_sum += jnp.sum(out_delta * n, 0, keepdims=True)
        shift_sum += jnp.sum(out_delta, 0, keepdims=True)
    sums[...] = sums_in[...] + jnp.concatenate(
        [bias_sum, gain_sum, shift_sum, jnp.zeros((7 - FS, width), f32)], 0
    )


def shards(
    tokens,
    upper_delta,
    segments,
    summary_index,
    validity,
    queries,
    positives,
    query_weight,
    key_weight,
    value_weight,
    query_bias,
    value_bias,
    output_weight,
    output_bias,
    first_gain,
    first_shift,
    up_weight,
    up_bias,
    down_weight,
    down_bias,
    second_gain,
):
    row_count, length = segments.shape
    token_count = row_count * length
    members = lax.axis_size("tensor")
    place = lax.axis_index("tensor")
    own_count = token_count // members
    width_local = query_weight.shape[1]
    heads_local = width_local // HD
    at_dp = lax.axis_index("dp")
    half_rows = D // 2

    def own(value):
        part = value.shape[0] // members
        return lax.dynamic_slice_in_dim(value, place * part, part, 0)

    info = jnp.concatenate(
        [
            jnp.stack([at_dp & 1, (at_dp >> 1) & 1, (at_dp >> 2) & 3, place, at_dp]).astype(jnp.int32),
            own(summary_index).reshape(-1),
        ]
    )
    vectors = jnp.stack([output_bias, first_gain, first_shift, down_bias, second_gain]).astype(f32)
    vectors = jnp.concatenate([vectors, jnp.zeros((3, D), f32)], 0)
    output_far = swap(output_weight)
    up_far = swap(up_weight)
    bias_far = swap(up_bias.reshape(1, -1))
    down_far = swap(down_weight)

    context_shape = ((length, width_local), bf16)

    def near_rows(info, ref):
        return ref.at[rows_at(info[BT], length)]

    def far_rows(info, ref):
        return ref.at[rows_at(1 - info[BT], length)]

    def attention(far):
        return call(
            functools.partial(attend, far=far),
            "attend_far" if far else "attend_near",
            [context_shape] * 4 + [((heads_local, length, length), bf16)],
            info, tokens, query_weight, key_weight, value_weight, query_bias, value_bias, segments, validity,
            scratch=[pltpu.VMEM((length, length), f32)],
            late=(1, 2, 3, 4),
            early=(1, 2, 3, 4),
            parts={1: ((length, D), far_rows if far else near_rows)},
        )

    context_far, query_far, key_far, value_far, weights_far = attention(True)
    context_in = swap(context_far)
    context, query, key, value, weights = attention(False)

    row, units = ((length, D), bf16), ((length, up_weight.shape[1]), bf16)
    scale_shape = ((length, 1), f32)
    own_passages = summary_index.shape[1]
    (
        first_low, first_normed, first_scale, active, active_far, slope, slope_far, second_normed, second_scale,
        summary,
    ) = call(
        forward, "forward",
        [row, row, scale_shape, units, units, units, units, row, scale_shape, ((own_passages, D), bf16)],
        info, context, output_weight, tokens, context_in, output_far, up_far, down_far, up_weight, down_weight,
        vectors, up_bias.reshape(1, -1).astype(f32), bias_far.astype(f32),
        late=range(1, 10),
        early=(0, 1, 3, 4, 5, 6, 7),
        parts={3: ((length, D), near_rows)},
        scratch=[pltpu.VMEM((length, D), f32)],
    )
    first_in = swap(first_low)
    active_in = swap(active_far)

    pairs = jnp.concatenate([summary, swap(summary)], 0)
    pairs = jnp.where(place == 0, pairs, jnp.roll(pairs, own_passages, 0))
    column = (positives // 8) * 16 + positives % 8
    digits = jnp.stack([column // 16, column % 16], 1).astype(bf16)
    bundle = jnp.concatenate(
        [
            jnp.pad(pairs, ((0, 0), (0, LANES))),
            jnp.concatenate([queries, jnp.pad(digits, ((0, 0), (0, LANES - 2)))], 1),
        ],
        0,
    )
    for bit in (0, 1):
        bundle = join(bundle, flip_by(bundle, "dp", 1 << bit), own_bit("dp", bit))
    pieces = [bundle, *[flip_by(bundle, "dp", 4 * k) for k in (1, 2, 3)]]
    if bits_of("dp") > 4:
        place_z = (at_dp >> 2) & 3
        joined = jnp.zeros((4, *bundle.shape), bf16)
        for k, piece in enumerate(pieces):
            joined = lax.dynamic_update_slice(joined, piece[None], (place_z ^ k, 0, 0))
        bundle = joined.reshape(-1, bundle.shape[1])
        for bit in range(4, bits_of("dp")):
            bundle = join(bundle, flip_by(bundle, "dp", 1 << bit), own_bit("dp", bit))
        pieces = [bundle]
    gathered = 16 * lax.axis_size("dp")
    query_count = queries.shape[0]
    losses, query_gradient, second_delta, unit_delta, sums = call(
        functools.partial(loss_back, pieces=len(pieces)), "loss_back",
        [((query_count, 1), f32), ((query_count, D), f32), ((length, D), f32), row, ((8, D), f32)],
        info, *pieces, upper_delta, second_normed, second_scale, vectors,
        late=(len(pieces) + 1, len(pieces) + 2), early=(2, 3),
        scratch=[
            pltpu.VMEM((gathered, D + LANES), bf16),
            pltpu.VMEM((gathered, gathered), bf16),
            pltpu.VMEM((gathered, 1), f32),
            pltpu.VMEM((length, D), f32),
        ],
    )
    unit_in = swap(unit_delta)
    order = []

    def through_units(name, weight, slope):
        return call(
            unit_back, name, [units], info, unit_delta, weight, slope, late=(1, 2, 3), early=(0,), order=order
        )[0]

    delta_far = through_units("unit_back_far", down_far, slope_far)
    delta_in = swap(delta_far)
    half = ((half_rows, D), bf16)
    down = Reduction(
        info, order,
        call(
            down_gradient, "down_gradient", [half] * 4, info, unit_delta, active, unit_in, active_in,
            late=(1, 2, 3, 4), early=(0, 1, 2, 3), order=order,
        ),
    )
    hidden_delta = through_units("unit_back_near", down_weight, slope)
    *halves, up_bias_sum = call(
        up_gradient, "up_gradient", [half] * 4 + [((8, up_weight.shape[1]), f32)], info, hidden_delta, first_low,
        delta_in, first_in, late=(1, 2, 3, 4), early=(0, 1, 2, 3), order=order,
    )
    up = Reduction(info, order, halves)
    down.quarters()
    first_delta, branch, shared = call(
        first_back, "first_back", [((length, D), f32), row, ((8, D), f32)], info, delta_far, up_far,
        hidden_delta, up_weight, second_delta, first_normed, first_scale, vectors, sums,
        late=range(1, 7), early=(0, 1), scratch=[pltpu.VMEM((length, D), f32)], order=order,
    )
    branch_far = swap(branch)
    shared_in = swap(shared)

    def attention_back(name, branch, weights, query, key, value, context, kind):
        return call(
            attend_back,
            name,
            [context_shape] * 3 + [((length, D), kind)],
            info, branch, output_weight, value, context, weights, key, query, query_weight, key_weight, value_weight,
            scratch=[pltpu.VMEM((length, width_local), bf16)],
            late=range(1, 11),
            early=(0, 1, 2),
            order=order,
        )

    query_delta, key_delta, value_delta, part = attention_back(
        "attend_back_near", branch, weights, query, key, value, context, f32
    )
    down.chunks()
    up.quarters()
    query_delta_far, key_delta_far, value_delta_far, part_far = attention_back(
        "attend_back_far", branch_far, weights_far, query_far, key_far, value_far, context_far, bf16,
    )
    part_in = swap(part_far)
    down.total()
    up.chunks()

    tall = ((half_rows + SMALL, D), bf16)
    heads = Reduction(
        info, order,
        call(
            head_gradients, "head_gradients", [tall, half, tall, half], info, tokens, query_delta, query_delta_far,
            key_delta, key_delta_far, value_delta, value_delta_far, branch, branch_far, context, context_far,
            shared, shared_in, up_bias_sum, late=(1, 8, 9, 10, 11, 6, 7, 2, 3, 4, 5), early=(0, 1, 2, 3), order=order,
        ),
    )
    down.join_four()
    up.total()
    heads.quarters()
    down.join_two()
    heads.chunks()
    up.join_four()
    (down_total,) = down.finish(finish_down, [(down_weight.shape, f32)])
    heads.total()
    up.join_two()
    heads.join_four()
    (up_total,) = up.finish(finish_up, [(up_weight.shape, f32)])
    heads.join_two()
    wide = (query_weight.shape, f32)
    heads_total = heads.finish(finish_heads, [wide] * 3 + [(output_weight.shape, f32)])
    small_total = heads.small.astype(f32)
    token_gradient = (first_delta + part + part_in.astype(f32)).astype(bf16)

    return (
        losses.reshape(-1),
        query_gradient,
        token_gradient,
        heads_total[0],
        heads_total[1],
        heads_total[2],
        small_total[7, :width_local],
        small_total[7, width_local:],
        heads_total[3],
        small_total[OB],
        small_total[FG],
        small_total[FS],
        up_total,
        small_total[5:7].reshape(-1),
        down_total,
        small_total[DB],
        small_total[SG],
    )


def solution(mesh):
    in_specs = (
        P("dp", None),
        P(("dp", "tensor"), None),
        P("dp", None),
        P("dp", None),
        P("dp", None),
        P("dp", None),
        P("dp"),
        P(None, "tensor"),
        P(None, "tensor"),
        P(None, "tensor"),
        P("tensor"),
        P("tensor"),
        P("tensor", None),
        P(),
        P(),
        P(),
        P(None, "tensor"),
        P("tensor"),
        P("tensor", None),
        P(),
        P(),
    )
    out_specs = (
        P("dp"),
        P("dp", None),
        P(("dp", "tensor"), None),
        P(None, "tensor"),
        P(None, "tensor"),
        P(None, "tensor"),
        P("tensor"),
        P("tensor"),
        P("tensor", None),
        P(),
        P(),
        P(),
        P(None, "tensor"),
        P("tensor"),
        P("tensor", None),
        P(),
        P(),
    )
    return jax.shard_map(shards, mesh=mesh, in_specs=in_specs, out_specs=out_specs, check_vma=False)
```

```python
import functools
import math

import jax
import jax.numpy as jnp
from jax import lax
from jax.experimental import pallas as pl
from jax.experimental.pallas import tpu as pltpu
from jax.sharding import PartitionSpec as P

D = 768
HD = 64
LANES = 128

norm_eps = 1e-05
neg_large = -1e30
root_half = 0.7071067811865476
inv_root_tau = 0.3989422804014327
log2_e = 1.4426950408889634

f32, bf16 = jnp.float32, jnp.bfloat16
COSTS = dict(
    attend_far=9, attend_near=9, forward=17, loss_back=6, unit_back_far=6, unit_back_near=6, down_gradient=7,
    up_gradient=7, first_back=9, attend_back_near=10, attend_back_far=10, head_gradients=8, add_halves=3,
    add_quarters=2, add_eighths=2, add_last=2, join_pieces=2, join_eighths=2, join_quarters=2, finish_down=4, finish_up=4, finish_heads=4,
)
FLOPS = int(2.3e9)
SMALL = 16


def bits_of(axis):
    return lax.axis_size(axis).bit_length() - 1


def flip_by(value, axis, mask):
    size = lax.axis_size(axis)
    return lax.ppermute(value, axis, [(i, i ^ mask) for i in range(size)])


def swap(value):
    return flip_by(value, "tensor", 1)


def own_bit(axis, bit):
    return (lax.axis_index(axis) >> bit) & 1


def join(value, other, high):
    return jnp.where(
        high == 1, jnp.concatenate([other, value], 0), jnp.concatenate([value, other], 0)
    )


def gather_dp(value):
    for bit in range(bits_of("dp")):
        value = join(value, flip_by(value, "dp", 1 << bit), own_bit("dp", bit))
    return value


def gather_all(value):
    value = join(value, swap(value), own_bit("tensor", 0))
    return gather_dp(value)


def dot(left, right):
    return jnp.dot(left, right, preferred_element_type=f32)


def dot_t(left, right):
    return lax.dot_general(left, right, (((1,), (1,)), ((), ())), preferred_element_type=f32)


def t_dot(left, right):
    return lax.dot_general(left, right, (((0,), (0,)), ((), ())), preferred_element_type=f32)


class Late:
    def __init__(self, source, held, semaphore):
        self.held, self.waited = held, False
        self.shape, self.dtype = held.shape, held.dtype
        self.copy = pltpu.make_async_copy(source, held, semaphore)
        self.copy.start()

    def wait(self):
        if not self.waited:
            self.copy.wait()
        self.waited = True
        return self.held


class Early:
    def __init__(self, held, target, semaphore):
        self.held, self.target, self.semaphore, self.sent = held, target, semaphore, False
        self.shape, self.dtype = held.shape, held.dtype

    def __getitem__(self, at):
        return self.held[at]

    def __setitem__(self, at, value):
        self.held[at] = value

    def send(self, *at):
        source, target = (self.held.at[at], self.target.at[at]) if at else (self.held, self.target)
        pltpu.make_async_copy(source, target, self.semaphore).start()
        self.sent = True

    def finish(self):
        if not self.sent:
            self.send()
        pltpu.make_async_copy(self.held, self.target, self.semaphore).wait()


def ready(*values):
    return [value.wait() if isinstance(value, Late) else value for value in values]


def call(kernel, name, outs, *args, scratch=(), late=(), early=(), order=None, grant=20, final=()):
    after = order or []
    count, waits, made = len(args), len(after), len(outs)
    held = [pltpu.VMEM(args[i].shape, args[i].dtype) for i in late] + [pltpu.VMEM(*outs[i]) for i in early]
    args = [pltpu.with_memory_space_constraint(a, pltpu.HBM) if i in late else a for i, a in enumerate(args)]

    def body(*refs):
        inputs = list(refs[:count])
        results = list(refs[count + waits : count + waits + made])
        rest = refs[count + waits + made :]
        scratches, rest = rest[: len(scratch)], rest[len(scratch) :]
        for k, i in enumerate(late):
            inputs[i] = Late(inputs[i], rest[k], rest[-1].at[k])
        for k, i in enumerate(early, len(late)):
            results[i] = Early(rest[k], results[i], rest[-1].at[k])
        kernel(*inputs, *results, *scratches)
        for i in early:
            results[i].finish()

    specs = [pl.BlockSpec(memory_space=pltpu.SMEM)]
    specs += [pl.BlockSpec(memory_space=pltpu.HBM if i in late else pltpu.VMEM) for i in range(1, count)]
    specs += [pl.BlockSpec(memory_space=pl.ANY)] * waits
    own = [pltpu.SemaphoreType.DMA((len(held),))] if held else []
    made_by = pl.pallas_call(
        body,
        name=name,
        out_shape=[
            jax.ShapeDtypeStruct(*out) if i in final else (pltpu.HBM if i in early else pltpu.VMEM)(*out)
            for i, out in enumerate(outs)
        ],
        in_specs=specs,
        out_specs=[pl.BlockSpec(memory_space=pltpu.HBM if i in early else pltpu.VMEM) for i in range(made)],
        scratch_shapes=[*scratch, *held, *own],
        compiler_params=pltpu.CompilerParams(vmem_limit_bytes=grant << 20),
        cost_estimate=pl.CostEstimate(
            flops=int(COSTS[name] * FLOPS), bytes_accessed=1, transcendentals=0
        ),
    )(*args, *after)
    if order is not None:
        order[:] = [made_by[-1]]
    return made_by


def rows_at(index, size):
    return pl.ds(pl.multiple_of(index * size, size), size)


def add_low(left, right):
    return (left.astype(f32) + right.astype(f32)).astype(bf16)


BX, BY, BZ, BT, BD, PLACES = range(6)


def add_halves(info, keep_a, came_a, keep_b, came_b, send_a, kept_a, send_b, kept_b):
    quarter = keep_b.shape[0] // 2
    for bit, keep, came, send, kept in (
        (info[BY], keep_a, came_a, send_a, kept_a),
        (info[BX], keep_b, came_b, send_b, kept_b),
    ):
        mine, other = rows_at(bit, quarter), rows_at(1 - bit, quarter)
        send[:quarter] = add_low(keep[other], came[other])
        kept[:quarter] = add_low(keep[mine], came[mine])
        if keep.shape[0] > 2 * quarter:
            extra = add_low(keep[2 * quarter :], came[2 * quarter :])
            send[quarter:] = extra
            kept[quarter:] = extra


def add_quarters(info, keep_a, came_a, keep_b, came_b, send, kept):
    quarter = keep_b.shape[0]
    half = quarter // 2
    bit = info[BZ] & 1
    for out, side in ((send, 1 - bit), (kept, bit)):
        at = rows_at(side, half)
        out[:half] = add_low(keep_a[at], came_a[at])
        out[half:quarter] = add_low(keep_b[at], came_b[at])
        if keep_a.shape[0] > quarter:
            out[quarter:] = add_low(keep_a[quarter:], came_a[quarter:])


def add_eighths(info, keep, came, send, kept):
    half = kept.shape[0] // 32 * 16
    bit = info[BZ] >> 1
    for out, side in ((send, 1 - bit), (kept, bit)):
        for part in range(2):
            at = rows_at(2 * part + side, half)
            out[part * half : part * half + half] = add_low(keep[at], came[at])
        if kept.shape[0] > 2 * half:
            out[2 * half :] = add_low(keep[4 * half :], came[4 * half :])


def add_last(info, keep, came, total, *small):
    size = total.shape[0]
    total[...] = add_low(keep[:size], came[:size])
    if small:
        small[0][...] = add_low(keep[size:], came[size:])


def join_pieces(info, own, came, eighth):
    half = own.shape[0] // 2
    bit = info[BZ] >> 1
    for source, side in ((own, bit), (came, 1 - bit)):
        for part in range(2):
            eighth[rows_at(2 * part + side, half)] = source[part * half : part * half + half]


def join_eighths(info, own, came, quarter_a, quarter_b):
    half = own.shape[0] // 2
    bit = info[BZ] & 1
    for source, side in ((own, bit), (came, 1 - bit)):
        quarter_a[rows_at(side, half)] = source[:half]
        quarter_b[rows_at(side, half)] = source[half:]


def join_quarters(info, own_a, came_a, own_b, came_b, half_a, half_b):
    size = own_a.shape[0]
    for bit, own, came, half in (
        (info[BY], own_a, came_a, half_a),
        (info[BX], own_b, came_b, half_b),
    ):
        half[rows_at(bit, size)] = own[...]
        half[rows_at(1 - bit, size)] = came[...]


def finish_down(info, own_a, came_a, own_b, came_b, out, mark):
    mark[...] = jnp.zeros_like(mark)
    size = own_a.shape[0]
    for part, bit, own, came in ((0, info[BX], own_a, came_a), (1, info[BY], own_b, came_b)):
        for side, source in ((bit, own), (1 - bit, came)):
            at = rows_at(2 * part + side, size)
            out[at] = source[...].astype(f32)
            out.send(at)


def finish_up(info, own_a, came_a, own_b, came_b, out, mark):
    mark[...] = jnp.zeros_like(mark)
    size, width = own_a.shape
    for part, bit, own, came in ((0, info[BX], own_a, came_a), (1, info[BY], own_b, came_b)):
        for side, source in ((bit, own), (1 - bit, came)):
            at = rows_at(side, size), pl.ds(part * width, width)
            out[at] = source[...].astype(f32)
            out.send(*at)


def finish_heads(info, own_a, came_a, own_b, came_b, query, key, value, output):
    size, width = own_a.shape
    half = width // 2
    for part, bit, own, came in ((0, info[BX], own_a, came_a), (1, info[BY], own_b, came_b)):
        left, right = ((query, key), (value, output))[part]
        for side, source in ((bit, own), (1 - bit, came)):
            at = rows_at(side, size)
            left[at] = source[:, :half].astype(f32)
            left.send(at)
            at = (slice(None), at) if right is output else (at,)
            right[at] = source[:, half:].astype(f32)
            right.send(*at)


class Reduction:
    def __init__(self, info, order, halves):
        self.info, self.order = info, order
        self.made = halves
        send_a, send_b, self.keep_a, self.keep_b = halves
        self.came = [flip_by(send_a, "dp", 1), flip_by(send_b, "dp", 2)]

    def staged(self, kernel, outs, *args, early=()):
        self.made = call(kernel, kernel.__name__, outs, self.info, *args, order=self.order, early=early)
        return self.made

    def quarters(self):
        (first, width), half = self.keep_a.shape, self.keep_b.shape[0]
        self.extra, self.quarter = first - half, half // 2
        a, b = ((self.quarter + self.extra, width), bf16), ((self.quarter, width), bf16)
        send_a, keep_a, send_b, keep_b = self.staged(
            add_halves, [a, a, b, b], self.keep_a, self.came[0], self.keep_b, self.came[1]
        )
        self.keep_a, self.keep_b, self.width = keep_a, keep_b, width
        self.came = [flip_by(send_a, "dp", 2), flip_by(send_b, "dp", 1)]

    def eighths(self):
        piece = ((self.quarter + self.extra, self.width), bf16)
        send, self.own = self.staged(
            add_quarters, [piece] * 2, self.keep_a, self.came[0], self.keep_b, self.came[1]
        )
        self.came = flip_by(send, "dp", 4)

    def pieces(self):
        piece = ((self.quarter // 2 + self.extra, self.width), bf16)
        send, self.own = self.staged(add_eighths, [piece] * 2, self.own, self.came)
        self.came = flip_by(send, "dp", 8)

    def total(self):
        outs = [((self.quarter // 2, self.width), bf16)]
        outs += [((self.extra, self.width), bf16)] if self.extra else []
        self.own, *small = [
            functools.reduce(
                lambda value, bit: add_low(value, flip_by(value, "dp", 1 << bit)),
                range(4, bits_of("dp")),
                made,
            )
            for made in self.staged(add_last, outs, self.own, self.came)
        ]
        self.small = small[0] if small else None
        self.came = flip_by(self.own, "dp", 8)

    def join_two_z(self):
        (self.own,) = self.staged(join_pieces, [((self.quarter, self.width), bf16)], self.own, self.came)
        self.came = flip_by(self.own, "dp", 4)

    def join_z(self):
        whole = ((self.quarter, self.width), bf16)
        self.keep_a, self.keep_b = self.staged(join_eighths, [whole] * 2, self.own, self.came)
        self.came = [flip_by(self.keep_a, "dp", 2), flip_by(self.keep_b, "dp", 1)]

    def join_two(self):
        whole = ((2 * self.quarter, self.width), bf16)
        self.keep_a, self.keep_b = self.staged(
            join_quarters, [whole] * 2, self.keep_a, self.came[0], self.keep_b, self.came[1]
        )
        self.came = [flip_by(self.keep_a, "dp", 1), flip_by(self.keep_b, "dp", 2)]

    def finish(self, kernel, outs):
        return self.staged(
            kernel, outs, self.keep_a, self.came[0], self.keep_b, self.came[1],
            early=[i for i, out in enumerate(outs) if out[0][0] > 8],
        )


def down_gradient(info, unit, active, unit_in, active_in, send_a, send_b, keep_a, keep_b):
    size = send_a.shape[0]
    unit, active, unit_in, active_in = ready(unit, active, unit_in, active_in)
    for side in range(2):
        for part, bit, outs in ((0, info[BX], (send_a, keep_a)), (1, info[BY], (send_b, keep_b))):
            at = rows_at(2 * part + (bit if side else 1 - bit), size)
            outs[side][...] = (
                t_dot(active[:, at], unit[...]) + t_dot(active_in[:, at], unit_in[...])
            ).astype(bf16)


def up_gradient(info, delta, first, delta_in, first_in, send_a, send_b, keep_a, keep_b, bias):
    size, width = send_a.shape
    delta, first, delta_in, first_in = ready(delta, first, delta_in, first_in)
    for side in range(2):
        for part, bit, outs in ((0, info[BX], (send_a, keep_a)), (1, info[BY], (send_b, keep_b))):
            columns = pl.ds(part * width, width)
            at = rows_at(bit if side else 1 - bit, size)
            outs[side][...] = (
                t_dot(first[:, at], delta[:, columns]) + t_dot(first_in[:, at], delta_in[:, columns])
            ).astype(bf16)
    ones = jnp.ones((8, delta.shape[0]), bf16)
    bias[...] = dot(ones, delta[...]) + dot(ones, delta_in[...])


def head_gradients(
    info, tokens, query, query_far, key, key_far, value, value_far, branch, branch_far,
    context, context_far, shared, shared_in, bias, send_a, send_b, keep_a, keep_b,
):
    half, width = send_b.shape
    tokens, branch, branch_far, context, context_far = ready(tokens, branch, branch_far, context, context_far)
    value, value_far, query, query_far, key, key_far = ready(value, value_far, query, query_far, key, key_far)
    narrow = query.shape[1]
    length = query.shape[0]
    near, far = rows_at(info[BT], length), rows_at(1 - info[BT], length)
    for side in range(2):
        for part, bit, outs in ((1, info[BY], (send_b, keep_b)), (0, info[BX], (send_a, keep_a))):
            out = outs[side]
            at = rows_at(bit if side else 1 - bit, half)
            tokens_near, tokens_far = tokens[near, at], tokens[far, at]
            if part == 0:
                left = t_dot(tokens_near, query[...]) + t_dot(tokens_far, query_far[...])
                right = t_dot(tokens_near, key[...]) + t_dot(tokens_far, key_far[...])
            else:
                left = t_dot(tokens_near, value[...]) + t_dot(tokens_far, value_far[...])
                right = dot(context[...], branch[:, at]) + dot(context_far[...], branch_far[:, at])
            out[:half, :narrow] = left.astype(bf16)
            out[:half, narrow:] = right.astype(bf16)
    ones = jnp.ones((8, length), bf16)
    query_sum = dot(ones, query[...]) + dot(ones, query_far[...])
    value_sum = dot(ones, value[...]) + dot(ones, value_far[...])
    last = jnp.concatenate([query_sum, value_sum], 1)
    rows = lax.broadcasted_iota(jnp.int32, (8, width), 0)
    block = shared[...] + shared_in[...]
    block = jnp.where(rows == 5, bias[:, :width], jnp.where(rows == 6, bias[:, width:], block))
    block = jnp.where(rows == 7, last, block)
    block = jnp.concatenate([block, jnp.zeros_like(block)], 0).astype(bf16)
    for out in (send_a, keep_a):
        out[half:] = block


def pair_columns(pair):
    return pl.ds(pl.multiple_of(pair * LANES, LANES), LANES)


def attend(
    info, tokens, query_weight, key_weight, value_weight, query_bias, value_bias, segments, validity,
    context, query, key, value, raised, shares, shade, *, far,
):
    length = context.shape[1]
    row = 1 - info[BT] if far else info[BT]
    segments, validity = ready(segments, validity)
    mark = segments[pl.ds(row, 1)]
    seen = jnp.where(validity[pl.ds(row, 1)] > 0, mark, -1)
    column = jnp.broadcast_to(seen.astype(f32), (8, length)).T[:, :1]
    shade[...] = jnp.where(column == mark.astype(f32), 0.0, neg_large)
    tokens, query_weight, query_bias, value_bias = ready(tokens, query_weight, query_bias, value_bias)
    x = tokens[rows_at(row, length)]
    scale = 1.0 / math.sqrt(HD)
    query[...] = (
        (dot(x, query_weight[...]) + query_bias[...].astype(f32)[None]).astype(bf16) * bf16(scale)
    )
    query.send()
    (key_weight,) = ready(key_weight)
    key[...] = dot(x, key_weight[...]).astype(bf16)
    key.send()
    (value_weight,) = ready(value_weight)
    value[...] = (dot(x, value_weight[...]) + value_bias[...].astype(f32)[None]).astype(bf16)
    value.send()
    low = lax.broadcasted_iota(jnp.int32, (length, LANES), 1) < HD

    def body(pair, _):
        at = pair_columns(pair)
        q, k, v = query[:, at], key[:, at], value[:, at]
        for member in range(2):
            mine = low if member == 0 else ~low
            logits = dot_t(k, jnp.where(mine, q, jnp.zeros_like(q))) + shade[...]
            peak = jnp.max(logits, 0, keepdims=True)
            lifted = jnp.exp(logits - peak).astype(bf16)
            raised[2 * pair + member] = lifted
            raised.send(2 * pair + member)
            sums = t_dot(jnp.where(mine, v, jnp.ones_like(v)), lifted)
            own, other = pl.ds(member * HD, HD), (1 - member) * HD
            share = 1.0 / sums[other : other + 1]
            shares[pl.ds(2 * pair + member, 1)] = share
            context[pl.ds(pl.multiple_of(pair * LANES + member * HD, HD), HD)] = (
                sums[member * HD : member * HD + HD] * share
            ).astype(bf16)
        return 0

    lax.fori_loop(0, context.shape[0] // LANES, body, 0)


def attend_back(
    info, branch, output_weight, shares, value, context, raised, key, query, query_weight, key_weight, value_weight,
    query_delta, key_delta, value_delta, part, context_delta,
):
    length = part.shape[0]
    branch, output_weight = ready(branch, output_weight)
    context_delta[...] = dot_t(output_weight[...], branch[...]).astype(bf16)
    value, context, raised, key, query = ready(value, context, raised, key, query)
    low = lax.broadcasted_iota(jnp.int32, (length, LANES), 1) < HD
    scale = 1.0 / math.sqrt(HD)

    def body(pair, _):
        at = pair_columns(pair)
        q, k, v = query[:, at], key[:, at], value[:, at]
        queries, keys, values = [], [], []
        for member in range(2):
            rows = pl.ds(pl.multiple_of(pair * LANES + member * HD, HD), HD)
            delta = context_delta[rows].astype(f32) * shares[pl.ds(2 * pair + member, 1)]
            inner = jnp.sum(delta * context[rows].astype(f32), 0, keepdims=True)
            delta = delta.astype(bf16)
            none = jnp.zeros_like(delta)
            delta = jnp.concatenate([none, delta] if member else [delta, none], 0)
            lifted = raised[2 * pair + member]
            logit_delta = (lifted.astype(f32) * (dot(v, delta) - inner)).astype(bf16)
            values.append(dot_t(lifted, delta))
            keys.append(dot(logit_delta, q))
            queries.append(t_dot(k, logit_delta)[member * HD : member * HD + HD])
        query_delta[:, at] = (jnp.concatenate(queries, 0) * scale).T.astype(bf16)
        key_delta[:, at] = jnp.where(low, keys[0], keys[1]).astype(bf16)
        value_delta[:, at] = (values[0] + values[1]).astype(bf16)
        return 0

    lax.fori_loop(0, query.shape[1] // LANES, body, 0)
    query_weight, key_weight, value_weight = ready(query_weight, key_weight, value_weight)
    part[...] = (
        dot_t(query_delta[...], query_weight[...])
        + dot_t(key_delta[...], key_weight[...])
        + dot_t(value_delta[...], value_weight[...])
    ).astype(part.dtype)


OB, FG, FS, DB, SG = range(5)


def center(inputs):
    shifted = inputs - jnp.mean(inputs, -1, keepdims=True)
    spread = jnp.mean(shifted * shifted, -1, keepdims=True)
    row_scale = lax.rsqrt(spread + norm_eps)
    return shifted * row_scale, row_scale


def norm_back(out_delta, normed, row_scale, norm_gain):
    scaled = out_delta * norm_gain
    first_mean = jnp.mean(scaled, -1, keepdims=True)
    second_mean = jnp.mean(scaled * normed, -1, keepdims=True)
    return row_scale * (scaled - first_mean - normed * second_mean)


def forward(
    info, context, output_near, tokens, context_in, output_far, up_far, down_far, up_near, down_near, vectors,
    bias_near, bias_far, first_low, first_normed, first_scale, active_near, active_far, slope_near, slope_far,
    second_normed, second_scale, summary, total,
):
    length = total.shape[0]
    step = length // 2
    halves = (pl.ds(0, step), pl.ds(step, step))
    base = info[BT] * length
    for at in halves:
        heads = t_dot(context[:, at], output_near[...]) + t_dot(context_in[:, at], output_far[...])
        x = tokens[pl.ds(pl.multiple_of(base + at.start, step), step)].astype(f32)
        normed, scale = center(x + (heads + vectors[OB : OB + 1]))
        out = normed * vectors[FG : FG + 1] + vectors[FS : FS + 1]
        first_normed[at] = normed.astype(bf16)
        first_scale[at] = scale
        first_low[at] = out.astype(bf16)
        total[at] = out + vectors[DB : DB + 1]
    first_low.send()
    first_normed.send()
    first_scale.send()

    width = 4 * LANES
    for up, down, bias, active, slope in (
        (up_far, down_far, bias_far, active_far, slope_far),
        (up_near, down_near, bias_near, active_near, slope_near),
    ):
        up, down = ready(up, down)

        def body(index, _, up=up, down=down, bias=bias, active=active, slope=slope):
            units = rows_at(index, width)
            for at in halves:
                hidden = dot(first_low[at], up[:, units]) + bias[:, units]
                share = 0.5 * (1.0 + lax.erf(hidden * root_half))
                low = (hidden * share).astype(bf16)
                active[at, units] = low
                slope[at, units] = (
                    share + hidden * jnp.exp(-0.5 * hidden * hidden) * inv_root_tau
                ).astype(bf16)
                total[at] += dot(low, down[units])
            active.send(slice(None), units)
            slope.send(slice(None), units)
            return 0

        lax.fori_loop(0, up.shape[1] // width, body, 0)

    for at in halves:
        normed, scale = center(total[at])
        second_normed[at] = normed.astype(bf16)
        second_scale[at] = scale
        total[at] = normed * vectors[SG : SG + 1]
    rows = [total[pl.ds(info[PLACES + k], 1)] for k in range(summary.shape[0])]
    summary[...] = jnp.concatenate(rows, 0).astype(bf16)


def loss_back(*refs, pieces):
    info, *sources = refs[: 1 + pieces]
    (
        upper, normed, scale, vectors, losses, query_gradient, second_delta, unit_delta, sums, all_rows, deltas,
        lost, out_delta,
    ) = refs[1 + pieces :]
    width = upper.shape[1]
    size = sources[0].shape[0]
    for step, source in enumerate(sources):
        all_rows[rows_at(info[BZ] ^ step, size) if pieces > 1 else pl.ds(0, size)] = source[...]
    count = all_rows.shape[0]
    block = min(256, count)
    score_scale = 1.0 / math.sqrt(width)
    own_passages = 4
    upper, normed, scale = ready(upper, normed, scale)
    out_delta[...] = upper[...].astype(f32)

    def body(index, sums_in):
        at = rows_at(index, block)
        rows = all_rows[at, :width]
        digits = all_rows[at, width:].astype(f32)
        scores = dot_t(rows, all_rows[:, :width]) * score_scale
        columns = lax.broadcasted_iota(jnp.int32, (block, count), 1)
        numbers = lax.broadcasted_iota(jnp.int32, (block, 1), 0)
        scores = jnp.where((columns & 15) < 8, scores, neg_large)
        peak = jnp.max(scores, -1, keepdims=True)
        raised = jnp.exp(scores - peak)
        total = jnp.sum(raised, -1, keepdims=True)
        target = (digits[:, 0:1] * 16.0 + digits[:, 1:2]).astype(jnp.int32)
        chosen = columns == target
        lost[at] = peak + jnp.log(total) - jnp.sum(jnp.where(chosen, scores, 0.0), -1, keepdims=True)
        delta = (raised / total - chosen.astype(f32)).astype(bf16)
        delta = jnp.where((numbers & 15) >= 8, delta, jnp.zeros_like(delta))
        deltas[at] = delta
        wide = delta.astype(f32)
        results = []
        for k in range(own_passages):
            column = info[BD] * 16 + info[BT] * own_passages + k
            share = jnp.sum(jnp.where(columns == column, wide, 0.0), -1, keepdims=True)
            results.append(sums_in[k] + jnp.sum(share * rows.astype(f32), 0, keepdims=True))
        return tuple(results)

    zero = jnp.zeros((1, width), f32)
    passage_delta = lax.fori_loop(0, count // block, body, (zero,) * own_passages)
    for k in range(own_passages):
        out_delta[pl.ds(info[PLACES + k], 1)] += passage_delta[k] * score_scale
    own = pl.multiple_of(info[BD] * 16, 16)
    own_delta = deltas[pl.ds(own, 16)]
    query_gradient[...] = (dot(own_delta, all_rows[:, :width]) * score_scale)[8:]
    losses[...] = lost[pl.ds(pl.multiple_of(own + 8, 8), 8)]

    length = upper.shape[0]
    step = length // 4
    bias_sum = gain_sum = zero
    for start in range(0, length, step):
        at = pl.ds(start, step)
        n = normed[at].astype(f32)
        delta = norm_back(out_delta[at], n, scale[at], vectors[SG : SG + 1])
        unit_delta[at] = delta.astype(bf16)
        second_delta[at] = delta
        bias_sum += jnp.sum(delta, 0, keepdims=True)
        gain_sum += jnp.sum(out_delta[at] * n, 0, keepdims=True)
    sums[...] = jnp.concatenate(
        [jnp.zeros((DB, width), f32), bias_sum, gain_sum, jnp.zeros((7 - SG, width), f32)], 0
    )


def unit_back(info, unit_delta, down_weight, slope, hidden_delta):
    width = 4 * LANES
    unit_delta, down_weight, slope = ready(unit_delta, down_weight, slope)

    def body(index, _):
        units = rows_at(index, width)
        delta = dot_t(unit_delta[...], down_weight[units])
        hidden_delta[:, units] = (delta * slope[:, units].astype(f32)).astype(bf16)
        return 0

    lax.fori_loop(0, down_weight.shape[0] // width, body, 0)


def first_back(
    info, delta_far, up_far, delta_near, up_near, second_delta, normed, scale, vectors, sums_in, first_delta,
    branch, sums, total,
):
    length, width = total.shape
    delta_far, up_far = ready(delta_far, up_far)
    total[...] = dot_t(delta_far[...], up_far[...])
    delta_near, up_near = ready(delta_near, up_near)
    total[...] += dot_t(delta_near[...], up_near[...])
    second_delta, normed = ready(second_delta, normed)
    step = length // 4
    zero = jnp.zeros((1, width), f32)
    bias_sum = gain_sum = shift_sum = zero
    for start in range(0, length, step):
        at = pl.ds(start, step)
        out_delta = second_delta[at] + total[at]
        n = normed[at].astype(f32)
        delta = norm_back(out_delta, n, scale[at], vectors[FG : FG + 1])
        branch[at] = delta.astype(bf16)
        first_delta[at] = delta
        bias_sum += jnp.sum(delta, 0, keepdims=True)
        gain_sum += jnp.sum(out_delta * n, 0, keepdims=True)
        shift_sum += jnp.sum(out_delta, 0, keepdims=True)
    sums[...] = sums_in[...] + jnp.concatenate(
        [bias_sum, gain_sum, shift_sum, jnp.zeros((7 - FS, width), f32)], 0
    )


def shards(
    tokens,
    upper_delta,
    segments,
    summary_index,
    validity,
    queries,
    positives,
    query_weight,
    key_weight,
    value_weight,
    query_bias,
    value_bias,
    output_weight,
    output_bias,
    first_gain,
    first_shift,
    up_weight,
    up_bias,
    down_weight,
    down_bias,
    second_gain,
):
    row_count, length = segments.shape
    token_count = row_count * length
    members = lax.axis_size("tensor")
    place = lax.axis_index("tensor")
    own_count = token_count // members
    width_local = query_weight.shape[1]
    heads_local = width_local // HD
    at_dp = lax.axis_index("dp")
    half_rows = D // 2

    def own(value):
        part = value.shape[0] // members
        return lax.dynamic_slice_in_dim(value, place * part, part, 0)

    info = jnp.concatenate(
        [
            jnp.stack([at_dp & 1, (at_dp >> 1) & 1, (at_dp >> 2) & 3, place, at_dp]).astype(jnp.int32),
            own(summary_index).reshape(-1),
        ]
    )
    vectors = jnp.stack([output_bias, first_gain, first_shift, down_bias, second_gain]).astype(f32)
    vectors = jnp.concatenate([vectors, jnp.zeros((3, D), f32)], 0)
    output_far = swap(output_weight)
    up_far = swap(up_weight)
    bias_far = swap(up_bias.reshape(1, -1))
    down_far = swap(down_weight)

    context_shape = ((length, width_local), bf16)

    def attention(far):
        return call(
            functools.partial(attend, far=far),
            "attend_far" if far else "attend_near",
            [((width_local, length), bf16)] + [context_shape] * 3
            + [((heads_local, length, length), bf16), ((heads_local + -heads_local % 8, length), f32)],
            info, tokens, query_weight, key_weight, value_weight, query_bias, value_bias, segments, validity,
            scratch=[pltpu.VMEM((length, length), f32)],
            late=(1, 2, 3, 4, 5, 6, 7, 8) if far else (),
            early=(1, 2, 3, 4, 5),
        )

    context_far, query_far, key_far, value_far, raised_far, shares_far = attention(True)
    context_in = swap(context_far)
    context, query, key, value, raised, shares = attention(False)

    row, units = ((length, D), bf16), ((length, up_weight.shape[1]), bf16)
    scale_shape = ((length, 1), f32)
    own_passages = summary_index.shape[1]
    (
        first_low, first_normed, first_scale, active, active_far, slope, slope_far, second_normed, second_scale,
        summary,
    ) = call(
        forward, "forward",
        [row, row, scale_shape, units, units, units, units, row, scale_shape, ((own_passages, D), bf16)],
        info, context, output_weight, tokens, context_in, output_far, up_far, down_far, up_weight, down_weight,
        vectors, up_bias.reshape(1, -1).astype(f32), bias_far.astype(f32),
        late=(8, 9), early=(0, 1, 2, 3, 4, 5, 6, 7, 8), grant=30,
        scratch=[pltpu.VMEM((length, D), f32)],
    )
    first_in = swap(first_low)
    active_in = swap(active_far)

    pairs = jnp.concatenate([summary, swap(summary)], 0)
    pairs = jnp.where(place == 0, pairs, jnp.roll(pairs, own_passages, 0))
    column = (positives // 8) * 16 + positives % 8
    digits = jnp.stack([column // 16, column % 16], 1).astype(bf16)
    bundle = jnp.concatenate(
        [
            jnp.pad(pairs, ((0, 0), (0, LANES))),
            jnp.concatenate([queries, jnp.pad(digits, ((0, 0), (0, LANES - 2)))], 1),
        ],
        0,
    )
    for bit in (0, 1):
        bundle = join(bundle, flip_by(bundle, "dp", 1 << bit), own_bit("dp", bit))
    pieces = [bundle, *[flip_by(bundle, "dp", 4 * k) for k in (1, 2, 3)]]
    if bits_of("dp") > 4:
        place_z = (at_dp >> 2) & 3
        joined = jnp.zeros((4, *bundle.shape), bf16)
        for k, piece in enumerate(pieces):
            joined = lax.dynamic_update_slice(joined, piece[None], (place_z ^ k, 0, 0))
        bundle = joined.reshape(-1, bundle.shape[1])
        for bit in range(4, bits_of("dp")):
            bundle = join(bundle, flip_by(bundle, "dp", 1 << bit), own_bit("dp", bit))
        pieces = [bundle]
    gathered = 16 * lax.axis_size("dp")
    query_count = queries.shape[0]
    losses, query_gradient, second_delta, unit_delta, sums = call(
        functools.partial(loss_back, pieces=len(pieces)), "loss_back",
        [((query_count, 1), f32), ((query_count, D), f32), ((length, D), f32), row, ((8, D), f32)],
        info, *pieces, upper_delta, second_normed, second_scale, vectors,

        late=range(len(pieces) + 1, len(pieces) + 4), final=(0, 1), grant=20 if gathered <= 256 else 40,
        scratch=[
            pltpu.VMEM((gathered, D + LANES), bf16),
            pltpu.VMEM((gathered, gathered), bf16),
            pltpu.VMEM((gathered, 1), f32),
            pltpu.VMEM((length, D), f32),
        ],
    )
    unit_in = swap(unit_delta)
    order = []

    def through_units(name, weight, slope):
        return call(
            unit_back, name, [units], info, unit_delta, weight, slope, order=order
        )[0]

    delta_far = through_units("unit_back_far", down_far, slope_far)
    delta_in = swap(delta_far)
    half = ((half_rows, D), bf16)
    down = Reduction(
        info, order,
        call(
            down_gradient, "down_gradient", [half] * 4, info, unit_delta, active, unit_in, active_in,
            order=order,
        ),
    )
    hidden_delta = through_units("unit_back_near", down_weight, slope)
    *halves, up_bias_sum = call(
        up_gradient, "up_gradient", [half] * 4 + [((8, up_weight.shape[1]), f32)], info, hidden_delta, first_low,
        delta_in, first_in, order=order,
    )
    up = Reduction(info, order, halves)
    down.quarters()
    first_delta, branch, shared = call(
        first_back, "first_back", [((length, D), f32), row, ((8, D), f32)], info, delta_far, up_far,
        hidden_delta, up_weight, second_delta, first_normed, first_scale, vectors, sums,
        scratch=[pltpu.VMEM((length, D), f32)], order=order,
    )
    branch_far = swap(branch)
    shared_in = swap(shared)

    def attention_back(name, branch, shares, raised, query, key, value, context, kind):
        return call(
            attend_back,
            name,
            [context_shape] * 3 + [((length, D), kind)],
            info, branch, output_weight, shares, value, context, raised, key, query, query_weight, key_weight,
            value_weight,
            scratch=[pltpu.VMEM((width_local, length), bf16)],
            order=order,
        )

    query_delta, key_delta, value_delta, part = attention_back(
        "attend_back_near", branch, shares, raised, query, key, value, context, f32
    )
    down.eighths()
    up.quarters()
    query_delta_far, key_delta_far, value_delta_far, part_far = attention_back(
        "attend_back_far", branch_far, shares_far, raised_far, query_far, key_far, value_far, context_far, bf16,
    )
    part_in = swap(part_far)
    down.pieces()
    up.eighths()

    tall = ((half_rows + SMALL, D), bf16)
    heads = Reduction(
        info, order,
        call(
            head_gradients, "head_gradients", [tall, half, tall, half], info, tokens, query_delta, query_delta_far,
            key_delta, key_delta_far, value_delta, value_delta_far, branch, branch_far, context, context_far,
            shared, shared_in, up_bias_sum, order=order,
        ),
    )
    mark = ((8, LANES), f32)
    down.total()
    up.pieces()
    heads.quarters()
    down.join_two_z()
    up.total()
    heads.eighths()
    down.join_z()
    up.join_two_z()
    heads.pieces()
    down.join_two()
    up.join_z()
    heads.total()
    down_total = down.finish(finish_down, [(down_weight.shape, f32), mark])[0]
    up.join_two()
    heads.join_two_z()
    up_total = up.finish(finish_up, [(up_weight.shape, f32), mark])[0]
    heads.join_z()
    heads.join_two()
    wide = (query_weight.shape, f32)
    heads_total = heads.finish(finish_heads, [wide] * 3 + [(output_weight.shape, f32)])
    small_total = heads.small.astype(f32)
    token_gradient = (first_delta + part + part_in.astype(f32)).astype(bf16)

    return (
        losses.reshape(-1),
        query_gradient,
        token_gradient,
        heads_total[0],
        heads_total[1],
        heads_total[2],
        small_total[7, :width_local],
        small_total[7, width_local:],
        heads_total[3],
        small_total[OB],
        small_total[FG],
        small_total[FS],
        up_total,
        small_total[5:7].reshape(-1),
        down_total,
        small_total[DB],
        small_total[SG],
    )


def solution(mesh):
    in_specs = (
        P("dp", None),
        P(("dp", "tensor"), None),
        P("dp", None),
        P("dp", None),
        P("dp", None),
        P("dp", None),
        P("dp"),
        P(None, "tensor"),
        P(None, "tensor"),
        P(None, "tensor"),
        P("tensor"),
        P("tensor"),
        P("tensor", None),
        P(),
        P(),
        P(),
        P(None, "tensor"),
        P("tensor"),
        P("tensor", None),
        P(),
        P(),
    )
    out_specs = (
        P("dp"),
        P("dp", None),
        P(("dp", "tensor"), None),
        P(None, "tensor"),
        P(None, "tensor"),
        P(None, "tensor"),
        P("tensor"),
        P("tensor"),
        P("tensor", None),
        P(),
        P(),
        P(),
        P(None, "tensor"),
        P("tensor"),
        P("tensor", None),
        P(),
        P(),
    )
    return jax.shard_map(shards, mesh=mesh, in_specs=in_specs, out_specs=out_specs, check_vma=False)
```

```python
import functools
import math

import jax
import jax.numpy as jnp
from jax import lax
from jax.experimental import pallas as pl
from jax.experimental.pallas import tpu as pltpu
from jax.sharding import PartitionSpec as P

D = 768
HD = 64
LANES = 128

norm_eps = 1e-05
neg_large = -1e30
root_half = 0.7071067811865476
inv_root_tau = 0.3989422804014327
log2_e = 1.4426950408889634

f32, bf16 = jnp.float32, jnp.bfloat16
COSTS = dict(
    attend_far=8, attend_near=7, forward=15, loss_back=4,
    unit_back_far=4, unit_back_near=0.4, down_gradient=3, up_gradient=0.16,
    first_back=1.8, attend_back_near=3.5, attend_back_far=3.5, head_gradients=5,
    down_add_halves=2, down_add_quarters=2, down_add_eighths=2, down_add_last=2,
    down_join_pieces=2, down_join_eighths=2, down_join_quarters=2, down_finish_down=6,
    up_add_halves=2, up_add_quarters=2, up_add_eighths=2, up_add_last=2,
    up_join_pieces=2, up_join_eighths=2, up_join_quarters=2, up_finish_up=6,
    heads_add_halves=2, heads_add_quarters=2, heads_add_eighths=2, heads_add_last=2,
    heads_join_pieces=2, heads_join_eighths=6, heads_join_quarters=2, heads_finish_heads=8,
)
FLOPS = int(1.15e+09)
SMALL = 16


def bits_of(axis):
    return lax.axis_size(axis).bit_length() - 1


def flip_by(value, axis, mask):
    size = lax.axis_size(axis)
    return lax.ppermute(value, axis, [(i, i ^ mask) for i in range(size)])


def swap(value):
    return flip_by(value, "tensor", 1)


def dot(left, right):
    return jnp.dot(left, right, preferred_element_type=f32)


def dot_t(left, right):
    return lax.dot_general(left, right, (((1,), (1,)), ((), ())), preferred_element_type=f32)


def t_dot(left, right):
    return lax.dot_general(left, right, (((0,), (0,)), ((), ())), preferred_element_type=f32)


class Late:
    def __init__(self, source, held, semaphore):
        self.held, self.waited = held, False
        self.shape, self.dtype = held.shape, held.dtype
        self.copy = pltpu.make_async_copy(source, held, semaphore)
        self.copy.start()

    def wait(self):
        if not self.waited:
            self.copy.wait()
        self.waited = True
        return self.held


class Early:
    def __init__(self, held, target, semaphore):
        self.held, self.target, self.semaphore, self.sent = held, target, semaphore, False
        self.shape, self.dtype = held.shape, held.dtype

    def __getitem__(self, at):
        return self.held[at]

    def __setitem__(self, at, value):
        self.held[at] = value

    def send(self, *at):
        source, target = (self.held.at[at], self.target.at[at]) if at else (self.held, self.target)
        pltpu.make_async_copy(source, target, self.semaphore).start()
        self.sent = True

    def finish(self):
        if not self.sent:
            self.send()
        pltpu.make_async_copy(self.held, self.target, self.semaphore).wait()


def ready(*values):
    return [value.wait() if isinstance(value, Late) else value for value in values]


def call(kernel, name, outs, *args, scratch=(), late=(), early=(), order=None, grant=20, final=()):
    after = order or []
    count, waits, made = len(args), len(after), len(outs)
    held = [pltpu.VMEM(args[i].shape, args[i].dtype) for i in late] + [pltpu.VMEM(*outs[i]) for i in early]
    args = [pltpu.with_memory_space_constraint(a, pltpu.HBM) if i in late else a for i, a in enumerate(args)]

    def body(*refs):
        inputs = list(refs[:count])
        results = list(refs[count + waits : count + waits + made])
        rest = refs[count + waits + made :]
        scratches, rest = rest[: len(scratch)], rest[len(scratch) :]
        for k, i in enumerate(late):
            inputs[i] = Late(inputs[i], rest[k], rest[-1].at[k])
        for k, i in enumerate(early, len(late)):
            results[i] = Early(rest[k], results[i], rest[-1].at[k])
        kernel(*inputs, *results, *scratches)
        for i in early:
            results[i].finish()

    specs = [pl.BlockSpec(memory_space=pltpu.SMEM)]
    specs += [pl.BlockSpec(memory_space=pltpu.HBM if i in late else pltpu.VMEM) for i in range(1, count)]
    specs += [pl.BlockSpec(memory_space=pl.ANY)] * waits
    own = [pltpu.SemaphoreType.DMA((len(held),))] if held else []
    made_by = pl.pallas_call(
        body,
        name=name,
        out_shape=[
            jax.ShapeDtypeStruct(*out) if i in final else (pltpu.HBM if i in early else pltpu.VMEM)(*out)
            for i, out in enumerate(outs)
        ],
        in_specs=specs,
        out_specs=[pl.BlockSpec(memory_space=pltpu.HBM if i in early else pltpu.VMEM) for i in range(made)],
        scratch_shapes=[*scratch, *held, *own],
        compiler_params=pltpu.CompilerParams(vmem_limit_bytes=grant << 20),
        cost_estimate=pl.CostEstimate(
            flops=int(COSTS[name] * FLOPS), bytes_accessed=1, transcendentals=0
        ),
    )(*args, *after)
    if order is not None:
        order[:] = [made_by[-1]]
    return made_by


def rows_at(index, size):
    return pl.ds(pl.multiple_of(index * size, size), size)


def add_low(left, right):
    return (left.astype(f32) + right.astype(f32)).astype(bf16)


BX, BY, BZ, BT, BD, PLACES = range(6)


def add_halves(info, keep_a, came_a, keep_b, came_b, send_a, kept_a, send_b, kept_b):
    quarter = keep_b.shape[0] // 2
    for bit, keep, came, send, kept in (
        (info[BY], keep_a, came_a, send_a, kept_a),
        (info[BX], keep_b, came_b, send_b, kept_b),
    ):
        mine, other = rows_at(bit, quarter), rows_at(1 - bit, quarter)
        send[:quarter] = add_low(keep[other], came[other])
        kept[:quarter] = add_low(keep[mine], came[mine])
        if keep.shape[0] > 2 * quarter:
            extra = add_low(keep[2 * quarter :], came[2 * quarter :])
            send[quarter:] = extra
            kept[quarter:] = extra


def add_quarters(info, keep_a, came_a, keep_b, came_b, send, kept):
    quarter, width = keep_b.shape[0], keep_a.shape[1]
    half = quarter // 2
    bit = info[BZ] & 1
    for out, side in ((send, 1 - bit), (kept, bit)):
        at = rows_at(side, half)
        out[:half, :width] = add_low(keep_a[at], came_a[at])
        out[:half, width:] = add_low(keep_b[at], came_b[at])
        if keep_a.shape[0] > quarter:
            out[half:, :width] = add_low(keep_a[quarter:], came_a[quarter:])
            out[half:, width:] = jnp.zeros((out.shape[0] - half, out.shape[1] - width), bf16)


def add_eighths(info, keep, came, send, kept, *, half):
    bit = info[BZ] >> 1
    for out, side in ((send, 1 - bit), (kept, bit)):
        at = rows_at(side, half)
        out[:half] = add_low(keep[at], came[at])
        if kept.shape[0] > half:
            out[half:] = add_low(keep[2 * half :], came[2 * half :])


def add_last(info, keep, came, total, *small):
    size = total.shape[0]
    total[...] = add_low(keep[:size], came[:size])
    if small:
        small[0][...] = add_low(keep[size:], came[size:])


def join_pieces(info, own, came, eighth):
    size = own.shape[0]
    bit = info[BZ] >> 1
    eighth[rows_at(bit, size)] = own[...]
    eighth[rows_at(1 - bit, size)] = came[...]


def join_eighths(info, own, came, quarter_a, quarter_b):
    size, width = own.shape[0], quarter_a.shape[1]
    bit = info[BZ] & 1
    for source, side in ((own, bit), (came, 1 - bit)):
        quarter_a[rows_at(side, size)] = source[:, :width]
        quarter_b[rows_at(side, size)] = source[:, width:]


def join_quarters(info, own_a, came_a, own_b, came_b, half_a, half_b):
    size = own_a.shape[0]
    for bit, own, came, half in (
        (info[BY], own_a, came_a, half_a),
        (info[BX], own_b, came_b, half_b),
    ):
        half[rows_at(bit, size)] = own[...]
        half[rows_at(1 - bit, size)] = came[...]


def finish_down(info, own_a, came_a, own_b, came_b, out, mark):
    mark[...] = jnp.zeros_like(mark)
    size = own_a.shape[0]
    for part, bit, own, came in ((0, info[BX], own_a, came_a), (1, info[BY], own_b, came_b)):
        for side, source in ((bit, own), (1 - bit, came)):
            at = rows_at(2 * part + side, size)
            out[at] = source[...].astype(f32)
            out.send(at)


def put(out, rows, columns, value):
    at = rows, pl.ds(columns, value.shape[1])
    out[at] = value.astype(f32)
    out.send(*at)


def finish_up(info, own_a, came_a, own_b, came_b, up, output, mark):
    mark[...] = jnp.zeros_like(mark)
    size, width = own_a.shape
    rest = up.shape[1] - width
    for side, source in ((info[BX], own_a), (1 - info[BX], came_a)):
        put(up, rows_at(side, size), 0, source[...])
    for side, source in ((info[BY], own_b), (1 - info[BY], came_b)):
        put(up, rows_at(side, size), width, source[:, :rest])
        at = slice(None), rows_at(side, size)
        output[at] = source[:, rest:].astype(f32)
        output.send(*at)


def finish_heads(info, own_a, came_a, own_b, came_b, query, key, value):
    size, width = own_a.shape
    own = query.shape[1]
    rest = width - own
    for side, source in ((info[BX], own_a), (1 - info[BX], came_a)):
        put(query, rows_at(side, size), 0, source[:, :own])
        put(key, rows_at(side, size), 0, source[:, own:])
    for side, source in ((info[BY], own_b), (1 - info[BY], came_b)):
        put(key, rows_at(side, size), rest, source[:, : own - rest])
        put(value, rows_at(side, size), 0, source[:, own - rest :])


class Reduction:
    def __init__(self, name, info, order):
        self.name, self.info, self.order = name, info, order

    def begin(self, halves):
        self.made = halves
        send_a, send_b, self.keep_a, self.keep_b = halves
        self.came = [flip_by(send_a, "dp", 1), flip_by(send_b, "dp", 2)]

    def staged(self, kernel, outs, *args, early=(), **fixed):
        bound = functools.partial(kernel, **fixed) if fixed else kernel
        self.made = call(bound, self.name + kernel.__name__, outs, self.info, *args, order=self.order, early=early)
        return self.made

    def quarters(self):
        (first, self.wide), (half, self.narrow) = self.keep_a.shape, self.keep_b.shape
        self.extra, self.quarter = first - half, half // 2
        a, b = ((self.quarter + self.extra, self.wide), bf16), ((self.quarter, self.narrow), bf16)
        send_a, self.keep_a, send_b, self.keep_b = self.staged(
            add_halves, [a, a, b, b], self.keep_a, self.came[0], self.keep_b, self.came[1]
        )
        self.came = [flip_by(send_a, "dp", 2), flip_by(send_b, "dp", 1)]

    def eighths(self):
        self.both = self.wide + self.narrow
        piece = ((self.quarter // 2 + self.extra, self.both), bf16)
        send, self.own = self.staged(
            add_quarters, [piece] * 2, self.keep_a, self.came[0], self.keep_b, self.came[1]
        )
        self.came = flip_by(send, "dp", 4)

    def pieces(self):
        size = self.quarter // 4
        piece = ((size + self.extra, self.both), bf16)
        send, self.own = self.staged(add_eighths, [piece] * 2, self.own, self.came, half=size)
        self.came = flip_by(send, "dp", 8)

    def total(self):
        outs = [((self.quarter // 4, self.both), bf16)]
        outs += [((self.extra, self.both), bf16)] if self.extra else []
        self.own, *small = [
            functools.reduce(
                lambda value, bit: add_low(value, flip_by(value, "dp", 1 << bit)),
                range(4, bits_of("dp")),
                made,
            )
            for made in self.staged(add_last, outs, self.own, self.came)
        ]
        self.small = small[0] if small else None
        self.came = flip_by(self.own, "dp", 8)

    def join_two_z(self):
        piece = ((self.quarter // 2, self.both), bf16)
        (self.own,) = self.staged(join_pieces, [piece], self.own, self.came)
        self.came = flip_by(self.own, "dp", 4)

    def join_z(self):
        outs = [((self.quarter, self.wide), bf16), ((self.quarter, self.narrow), bf16)]
        self.keep_a, self.keep_b = self.staged(join_eighths, outs, self.own, self.came)
        self.came = [flip_by(self.keep_a, "dp", 2), flip_by(self.keep_b, "dp", 1)]

    def join_two(self):
        outs = [((2 * self.quarter, self.wide), bf16), ((2 * self.quarter, self.narrow), bf16)]
        self.keep_a, self.keep_b = self.staged(
            join_quarters, outs, self.keep_a, self.came[0], self.keep_b, self.came[1]
        )
        self.came = [flip_by(self.keep_a, "dp", 1), flip_by(self.keep_b, "dp", 2)]

    def finish(self, kernel, outs):
        return self.staged(
            kernel, outs, self.keep_a, self.came[0], self.keep_b, self.came[1],
            early=[i for i, out in enumerate(outs) if out[0][0] > 8],
        )


def down_gradient(info, unit, active, unit_in, active_in, send_a, send_b, keep_a, keep_b):
    size = send_a.shape[0]
    unit, active, unit_in, active_in = ready(unit, active, unit_in, active_in)
    for side in range(2):
        for part, bit, outs in ((0, info[BX], (send_a, keep_a)), (1, info[BY], (send_b, keep_b))):
            at = rows_at(2 * part + (bit if side else 1 - bit), size)
            outs[side][...] = (
                t_dot(active[:, at], unit[...]) + t_dot(active_in[:, at], unit_in[...])
            ).astype(bf16)


def up_gradient(
    info, delta, first, delta_in, first_in, branch, branch_far, context, context_far, send_a, send_b, keep_a, keep_b,
    bias,
):
    size, width = send_a.shape
    rest = delta.shape[1] - width
    for side in range(2):
        for bit, outs, columns in (
            (info[BX], (send_a, keep_a), pl.ds(0, width)),
            (info[BY], (send_b, keep_b), pl.ds(width, rest)),
        ):
            at = rows_at(bit if side else 1 - bit, size)
            out = outs[side]
            out[:, : columns.size] = (
                t_dot(first[:, at], delta[:, columns]) + t_dot(first_in[:, at], delta_in[:, columns])
            ).astype(bf16)
            if columns.size == rest:
                out[:, rest:] = (dot(context[...], branch[:, at]) + dot(context_far[...], branch_far[:, at])).astype(
                    bf16
                )
    ones = jnp.ones((8, delta.shape[0]), bf16)
    bias[...] = dot(ones, delta[...]) + dot(ones, delta_in[...])


def head_gradients(
    info, tokens, query, query_far, key, key_far, value, value_far, shared, shared_in, bias, send_a, send_b, keep_a,
    keep_b,
):
    half, width = send_b.shape[0], send_a.shape[1]
    length, narrow = query.shape
    rest = width - narrow
    near, far = rows_at(info[BT], length), rows_at(1 - info[BT], length)
    for side in range(2):
        for bit, outs, sources in (
            (info[BX], (send_a, keep_a), ((query, query_far, 0, narrow), (key, key_far, 0, rest))),
            (info[BY], (send_b, keep_b), ((key, key_far, rest, narrow - rest), (value, value_far, 0, narrow))),
        ):
            at = rows_at(bit if side else 1 - bit, half)
            tokens_near, tokens_far = tokens[near, at], tokens[far, at]
            put_at = 0
            for left, right, first, count in sources:
                columns = pl.ds(first, count)
                outs[side][:half, pl.ds(put_at, count)] = (
                    t_dot(tokens_near, left[:, columns]) + t_dot(tokens_far, right[:, columns])
                ).astype(bf16)
                put_at += count
    ones = jnp.ones((8, length), bf16)
    query_sum = dot(ones, query[...]) + dot(ones, query_far[...])
    value_sum = dot(ones, value[...]) + dot(ones, value_far[...])
    sums = shared[...] + shared_in[...]
    pairs = [(sums[k : k + 1, :narrow], sums[k : k + 1, narrow:]) for k in range(5)]
    pairs += [(bias[:1, k * narrow : (k + 1) * narrow], bias[:1, (k + 1) * narrow : (k + 2) * narrow]) for k in (0, 2)]
    pairs += [(query_sum[:1], value_sum[:1])]
    block = jnp.concatenate([piece for pair in pairs for piece in pair], 0)
    block = jnp.concatenate([block, jnp.zeros((SMALL, rest), f32)], 1).astype(bf16)
    send_a[half:] = block
    keep_a[half:] = block


def attend(
    info, tokens, query_weight, key_weight, value_weight, query_bias, value_bias, segments, validity,
    context, query, key, value, raised, shares, shade, *, far,
):
    length = context.shape[1]
    row = 1 - info[BT] if far else info[BT]
    segments, validity = ready(segments, validity)
    mark = segments[pl.ds(row, 1)]
    seen = jnp.where(validity[pl.ds(row, 1)] > 0, mark, -1)
    column = jnp.broadcast_to(seen.astype(f32), (8, length)).T[:, :1]
    shade[...] = jnp.where(column == mark.astype(f32), 0.0, neg_large)
    tokens, query_weight, query_bias, value_bias = ready(tokens, query_weight, query_bias, value_bias)
    x = tokens[rows_at(row, length)]
    scale = 1.0 / math.sqrt(HD)
    query[...] = (
        (dot(x, query_weight[...]) + query_bias[...].astype(f32)[None]).astype(bf16) * bf16(scale)
    )
    query.send()
    (key_weight,) = ready(key_weight)
    key[...] = dot(x, key_weight[...]).astype(bf16)
    key.send()
    (value_weight,) = ready(value_weight)
    value[...] = (dot(x, value_weight[...]) + value_bias[...].astype(f32)[None]).astype(bf16)
    value.send()
    low = lax.broadcasted_iota(jnp.int32, (length, LANES), 1) < HD

    heads = [(pl.ds(start, LANES), member) for start in range(0, context.shape[0], LANES) for member in range(2)]

    def logits_of(head):
        at, member = head
        q = query[:, at]
        return dot_t(key[:, at], jnp.where(low if member == 0 else ~low, q, jnp.zeros_like(q))) + shade[...]

    coming = logits_of(heads[0])
    for number, (at, member) in enumerate(heads):
        logits, coming = coming, logits_of(heads[number + 1]) if number + 1 < len(heads) else None
        v = value[:, at]
        peak = jnp.max(logits, 0, keepdims=True)
        lifted = jnp.exp(logits - peak).astype(bf16)
        raised[number] = lifted
        raised.send(number)
        sums = t_dot(jnp.where(low if member == 0 else ~low, v, jnp.ones_like(v)), lifted)
        other = (1 - member) * HD
        share = 1.0 / sums[other : other + 1]
        shares[number : number + 1] = share
        rows = pl.ds(number * HD, HD)
        part = (sums[member * HD : member * HD + HD] * share).astype(bf16)
        context[rows] = part
        context.send(rows)


def attend_back(
    info, branch, output_weight, shares, value, context, raised, key, query, query_weight, key_weight, value_weight,
    query_delta, key_delta, value_delta, part, context_delta,
):
    length = part.shape[0]
    branch, output_weight = ready(branch, output_weight)
    context_delta[...] = dot_t(output_weight[...], branch[...]).astype(bf16)
    value, context, raised, key, query = ready(value, context, raised, key, query)
    low = lax.broadcasted_iota(jnp.int32, (length, LANES), 1) < HD
    scale = 1.0 / math.sqrt(HD)

    heads = [(pl.ds(start, LANES), member) for start in range(0, query.shape[1], LANES) for member in range(2)]

    def begin(number):
        at, member = heads[number]
        rows = pl.ds(number * HD, HD)
        delta = context_delta[rows].astype(f32) * shares[number : number + 1]
        inner = jnp.sum(delta * context[rows].astype(f32), 0, keepdims=True)
        delta = delta.astype(bf16)
        none = jnp.zeros_like(delta)
        delta = jnp.concatenate([none, delta] if member else [delta, none], 0)
        return delta, inner, dot(value[:, at], delta)

    coming = begin(0)
    for number, (at, member) in enumerate(heads):
        (delta, inner, weight_delta), coming = coming, begin(number + 1) if number + 1 < len(heads) else None
        if member == 0:
            queries, keys, values = [], [], []
        lifted = raised[number]
        logit_delta = (lifted.astype(f32) * (weight_delta - inner)).astype(bf16)
        values.append(dot_t(lifted, delta))
        keys.append(dot(logit_delta, query[:, at]))
        queries.append(t_dot(key[:, at], logit_delta)[member * HD : member * HD + HD])
        if member == 1:
            query_delta[:, at] = (jnp.concatenate(queries, 0) * scale).T.astype(bf16)
            key_delta[:, at] = jnp.where(low, keys[0], keys[1]).astype(bf16)
            value_delta[:, at] = (values[0] + values[1]).astype(bf16)
    query_weight, key_weight, value_weight = ready(query_weight, key_weight, value_weight)
    part[...] = (
        dot_t(query_delta[...], query_weight[...])
        + dot_t(key_delta[...], key_weight[...])
        + dot_t(value_delta[...], value_weight[...])
    ).astype(part.dtype)


OB, FG, FS, DB, SG = range(5)


def center(inputs):
    shifted = inputs - jnp.mean(inputs, -1, keepdims=True)
    spread = jnp.mean(shifted * shifted, -1, keepdims=True)
    row_scale = lax.rsqrt(spread + norm_eps)
    return shifted * row_scale, row_scale


def norm_back(out_delta, normed, row_scale, norm_gain):
    scaled = out_delta * norm_gain
    first_mean = jnp.mean(scaled, -1, keepdims=True)
    second_mean = jnp.mean(scaled * normed, -1, keepdims=True)
    return row_scale * (scaled - first_mean - normed * second_mean)


def forward(
    info, context, output_near, tokens, context_in, output_far, up_far, down_far, up_near, down_near, vectors,
    bias_near, bias_far, first_low, first_normed, first_scale, active_near, active_far, slope_near, slope_far,
    second_normed, second_scale, summary, total,
):
    length = total.shape[0]
    step = length // 2
    halves = (pl.ds(0, step), pl.ds(step, step))
    base = info[BT] * length
    context, output_near, tokens = ready(context, output_near, tokens)
    for at in halves:
        heads = t_dot(context[:, at], output_near[...]) + t_dot(context_in[:, at], output_far[...])
        x = tokens[pl.ds(pl.multiple_of(base + at.start, step), step)].astype(f32)
        normed, scale = center(x + (heads + vectors[OB : OB + 1]))
        out = normed * vectors[FG : FG + 1] + vectors[FS : FS + 1]
        first_normed[at] = normed.astype(bf16)
        first_scale[at] = scale
        first_low[at] = out.astype(bf16)
        total[at] = out + vectors[DB : DB + 1]
    first_low.send()
    first_normed.send()
    first_scale.send()

    width = 6 * LANES
    groups = (
        (up_far, down_far, bias_far, active_far, slope_far),
        (up_near, down_near, bias_near, active_near, slope_near),
    )
    tasks = [
        (group, pl.ds(start, width), at)
        for group in groups
        for start in range(0, bias_near.shape[1], width)
        for at in halves
    ]

    def hidden_of(task):
        (up, _, bias, _, _), units, at = task
        (up,) = ready(up)
        return dot(first_low[at], up[:, units]) + bias[:, units]

    coming = hidden_of(tasks[0])
    for task, later in zip(tasks, [*tasks[1:], None]):
        hidden, coming = coming, None if later is None else hidden_of(later)
        (_, down, _, active, slope), units, at = task
        share = 0.5 * (1.0 + lax.erf(hidden * root_half))
        low = (hidden * share).astype(bf16)
        active[at, units] = low
        slope[at, units] = (share + hidden * jnp.exp(-0.5 * hidden * hidden) * inv_root_tau).astype(bf16)
        (down,) = ready(down)
        total[at] += dot(low, down[units])
        if at is halves[-1]:
            active.send(slice(None), units)
            slope.send(slice(None), units)

    for at in halves:
        normed, scale = center(total[at])
        second_normed[at] = normed.astype(bf16)
        second_scale[at] = scale
        total[at] = normed * vectors[SG : SG + 1]
    rows = [total[pl.ds(info[PLACES + k], 1)] for k in range(summary.shape[0])]
    summary[...] = jnp.concatenate(rows, 0).astype(bf16)


def loss_back(
    info, near, far, upper, normed, scale, vectors, losses, query_gradient, second_delta, unit_delta, sums, all_rows,
    out_delta,
):
    width = upper.shape[1]
    all_rows[: near.shape[0]] = near[...]
    all_rows[near.shape[0] :] = far[...]
    here = info[BT] * near.shape[0] + info[BD] * 8
    places = near.shape[0] // 8
    count = all_rows.shape[0]
    block = min(256, count)
    score_scale = 1.0 / math.sqrt(width)
    own_passages = 4

    def body(index, sums_in):
        at = rows_at(index, block)
        rows = all_rows[at, :width]
        digits = all_rows[at, width:].astype(f32)
        scores = dot_t(rows, all_rows[:, :width]) * score_scale
        columns = lax.broadcasted_iota(jnp.int32, (block, count), 1) ^ here
        numbers = (lax.broadcasted_iota(jnp.int32, (block, 1), 0) + index * block) ^ here
        scores = jnp.where((columns & 7) < own_passages, scores, neg_large)
        peak = jnp.max(scores, -1, keepdims=True)
        raised = jnp.exp(scores - peak)
        total = jnp.sum(raised, -1, keepdims=True)
        target = (digits[:, 0:1] * 16.0 + digits[:, 1:2]).astype(jnp.int32)
        chosen = columns == target
        lost = peak + jnp.log(total) - jnp.sum(jnp.where(chosen, scores, 0.0), -1, keepdims=True)
        delta = raised / total - chosen.astype(f32)
        delta = jnp.where((numbers & 7) >= own_passages, delta, 0.0).astype(bf16)
        wide = delta.astype(f32)
        places_here = lax.broadcasted_iota(jnp.int32, (block, 8), 1)
        wanted = ((places_here >> 2) * places + info[BD]) * 8 + own_passages + (places_here & 3)
        mine = (numbers == wanted).astype(f32)
        own_losses = sums_in[0] + jnp.sum(mine * lost, 0, keepdims=True)
        own_delta = sums_in[1] + t_dot(mine.astype(bf16), delta)
        results = []
        for k in range(own_passages):
            column = (info[BT] * places + info[BD]) * 8 + k
            share = jnp.sum(jnp.where(columns == column, wide, 0.0), -1, keepdims=True)
            results.append(sums_in[2 + k] + jnp.sum(share * rows.astype(f32), 0, keepdims=True))
        return own_losses, own_delta, *results

    zero = jnp.zeros((1, width), f32)
    first = (jnp.zeros((1, 8), f32), jnp.zeros((8, count), f32), *[zero] * own_passages)
    if count == block:
        own_losses, own_delta, *passage_delta = body(0, first)
    else:
        own_losses, own_delta, *passage_delta = lax.fori_loop(0, count // block, body, first)
    upper, normed, scale = ready(upper, normed, scale)
    out_delta[...] = upper[...].astype(f32)
    for k in range(own_passages):
        out_delta[pl.ds(info[PLACES + k], 1)] += passage_delta[k] * score_scale
    query_gradient[...] = dot(own_delta.astype(bf16), all_rows[:, :width]) * score_scale
    losses[...] = own_losses

    length = upper.shape[0]
    step = length // 4
    bias_sum = gain_sum = zero
    for start in range(0, length, step):
        at = pl.ds(start, step)
        n = normed[at].astype(f32)
        delta = norm_back(out_delta[at], n, scale[at], vectors[SG : SG + 1])
        unit_delta[at] = delta.astype(bf16)
        second_delta[at] = delta
        bias_sum += jnp.sum(delta, 0, keepdims=True)
        gain_sum += jnp.sum(out_delta[at] * n, 0, keepdims=True)
    sums[...] = jnp.concatenate(
        [jnp.zeros((DB, width), f32), bias_sum, gain_sum, jnp.zeros((7 - SG, width), f32)], 0
    )


def unit_back(info, unit_delta, down_weight, slope, hidden_delta):
    width = 6 * LANES
    for start in range(0, down_weight.shape[0], width):
        units = pl.ds(start, width)
        delta = dot_t(unit_delta[...], down_weight[units])
        hidden_delta[:, units] = (delta * slope[:, units].astype(f32)).astype(bf16)


def first_back(
    info, delta_far, up_far, delta_near, up_near, second_delta, normed, scale, vectors, sums_in, first_delta,
    branch, sums, total,
):
    length, width = total.shape
    delta_far, up_far = ready(delta_far, up_far)
    total[...] = dot_t(delta_far[...], up_far[...])
    delta_near, up_near = ready(delta_near, up_near)
    total[...] += dot_t(delta_near[...], up_near[...])
    second_delta, normed = ready(second_delta, normed)
    step = length // 4
    zero = jnp.zeros((1, width), f32)
    bias_sum = gain_sum = shift_sum = zero
    for start in range(0, length, step):
        at = pl.ds(start, step)
        out_delta = second_delta[at] + total[at]
        n = normed[at].astype(f32)
        delta = norm_back(out_delta, n, scale[at], vectors[FG : FG + 1])
        branch[at] = delta.astype(bf16)
        first_delta[at] = delta
        bias_sum += jnp.sum(delta, 0, keepdims=True)
        gain_sum += jnp.sum(out_delta * n, 0, keepdims=True)
        shift_sum += jnp.sum(out_delta, 0, keepdims=True)
    sums[...] = sums_in[...] + jnp.concatenate(
        [bias_sum, gain_sum, shift_sum, jnp.zeros((7 - FS, width), f32)], 0
    )


def shards(
    tokens,
    upper_delta,
    segments,
    summary_index,
    validity,
    queries,
    positives,
    query_weight,
    key_weight,
    value_weight,
    query_bias,
    value_bias,
    output_weight,
    output_bias,
    first_gain,
    first_shift,
    up_weight,
    up_bias,
    down_weight,
    down_bias,
    second_gain,
):
    row_count, length = segments.shape
    token_count = row_count * length
    members = lax.axis_size("tensor")
    place = lax.axis_index("tensor")
    own_count = token_count // members
    width_local = query_weight.shape[1]
    heads_local = width_local // HD
    at_dp = lax.axis_index("dp")
    half_rows = D // 2

    def own(value):
        part = value.shape[0] // members
        return lax.dynamic_slice_in_dim(value, place * part, part, 0)

    info = jnp.concatenate(
        [
            jnp.stack([at_dp & 1, (at_dp >> 1) & 1, (at_dp >> 2) & 3, place, at_dp]).astype(jnp.int32),
            own(summary_index).reshape(-1),
        ]
    )
    vectors = jnp.stack([output_bias, first_gain, first_shift, down_bias, second_gain]).astype(f32)
    vectors = jnp.concatenate([vectors, jnp.zeros((3, D), f32)], 0)
    output_far = swap(output_weight)
    up_far = swap(up_weight)
    bias_far = swap(up_bias.reshape(1, -1))
    down_far = swap(down_weight)

    context_shape = ((length, width_local), bf16)

    def attention(far):
        return call(
            functools.partial(attend, far=far),
            "attend_far" if far else "attend_near",
            [((width_local, length), bf16)] + [context_shape] * 3
            + [((heads_local, length, length), bf16), ((heads_local + -heads_local % 8, length), f32)],
            info, tokens, query_weight, key_weight, value_weight, query_bias, value_bias, segments, validity,
            scratch=[pltpu.VMEM((length, length), f32)],
            late=(1, 2, 3, 4, 5, 6, 7, 8) if far else (),
            early=(0, 1, 2, 3, 4, 5),
        )

    context_far, query_far, key_far, value_far, raised_far, shares_far = attention(True)
    context_in = swap(context_far)
    context, query, key, value, raised, shares = attention(False)

    row, units = ((length, D), bf16), ((length, up_weight.shape[1]), bf16)
    scale_shape = ((length, 1), f32)
    own_passages = summary_index.shape[1]
    (
        first_low, first_normed, first_scale, active, active_far, slope, slope_far, second_normed, second_scale,
        summary,
    ) = call(
        forward, "forward",
        [row, row, scale_shape, units, units, units, units, row, scale_shape, ((own_passages, D), bf16)],
        info, context, output_weight, tokens, context_in, output_far, up_far, down_far, up_weight, down_weight,
        vectors, up_bias.reshape(1, -1).astype(f32), bias_far.astype(f32),
        late=(1, 2, 3, 7, 8, 9), early=(0, 1, 2, 3, 4, 5, 6, 7, 8), grant=40,
        scratch=[pltpu.VMEM((length, D), f32)],
    )
    first_in = swap(first_low)
    active_in = swap(active_far)

    places = lax.axis_size("dp")
    row_of = ((positives % 8) // 4 * places + positives // 8) * 8 + positives % 4
    digits = jnp.stack([row_of // 16, row_of % 16], 1).astype(bf16)
    digits = jnp.pad(digits, ((0, 0), (0, LANES - 2)))
    bundle = jnp.concatenate(
        [jnp.pad(summary, ((0, 0), (0, LANES))), own(jnp.concatenate([queries, digits], 1))], 0
    )
    for low in (1, 4):
        bundle = jnp.concatenate([bundle, *[flip_by(bundle, "dp", low * k) for k in (1, 2, 3)]], 0)
    for bit in range(4, bits_of("dp")):
        bundle = jnp.concatenate([bundle, flip_by(bundle, "dp", 1 << bit)], 0)
    bundle_far = swap(bundle)
    gathered = 2 * bundle.shape[0]
    query_count = queries.shape[0]
    losses, query_gradient, second_delta, unit_delta, sums = call(
        loss_back, "loss_back",
        [((1, query_count), f32), ((query_count, D), f32), ((length, D), f32), row, ((8, D), f32)],
        info, bundle, bundle_far, upper_delta, second_normed, second_scale, vectors,
        late=(3, 4, 5), final=(0, 1), grant=20 if gathered <= 256 else 50,
        scratch=[pltpu.VMEM((gathered, D + LANES), bf16), pltpu.VMEM((length, D), f32)],
    )
    unit_in = swap(unit_delta)
    order = []

    def through_units(name, weight, slope):
        return call(
            unit_back, name, [units], info, unit_delta, weight, slope, order=order
        )[0]

    delta_far = through_units("unit_back_far", down_far, slope_far)
    delta_in = swap(delta_far)
    down, up, heads = [Reduction(name, info, order) for name in ("down_", "up_", "heads_")]
    held = {}
    wide_shape, mark = (query_weight.shape, f32), ((8, LANES), f32)
    down.begin(
        call(
            down_gradient, "down_gradient", [((half_rows, D), bf16)] * 4, info, unit_delta, active, unit_in, active_in,
            order=order,
        )
    )

    def two_parts(columns, extra=0):
        wide = (columns // 2 + LANES - 1) // LANES * LANES
        first, second = ((half_rows + extra, wide), bf16), ((half_rows, columns - wide), bf16)
        return [first, second, first, second]

    def near_units():
        held["delta"] = through_units("unit_back_near", down_weight, slope)

    def first_norm():
        held["first_delta"], held["branch"], held["shared"] = call(
            first_back, "first_back", [((length, D), f32), row, ((8, D), f32)], info, delta_far, up_far,
            held["delta"], up_weight, second_delta, first_normed, first_scale, vectors, sums,
            scratch=[pltpu.VMEM((length, D), f32)], order=order,
        )
        held["branch_far"], held["shared_in"] = swap(held["branch"]), swap(held["shared"])

    def up_begin():
        *halves, held["bias"] = call(
            up_gradient, "up_gradient",
            two_parts(up_weight.shape[1] + width_local) + [((8, up_weight.shape[1]), f32)],
            info, held["delta"], first_low, delta_in, first_in, held["branch"], held["branch_far"], context,
            context_far, order=order,
        )
        up.begin(halves)

    def attention_back(name, branch, shares, raised, query, key, value, context, kind):
        return call(
            attend_back,
            name,
            [context_shape] * 3 + [((length, D), kind)],
            info, branch, output_weight, shares, value, context, raised, key, query, query_weight, key_weight,
            value_weight,
            scratch=[pltpu.VMEM((width_local, length), bf16)],
            order=order,
        )

    def near_row():
        held["near"] = attention_back(
            "attend_back_near", held["branch"], shares, raised, query, key, value, context, f32
        )

    def far_row():
        held["far"] = attention_back(
            "attend_back_far", held["branch_far"], shares_far, raised_far, query_far, key_far, value_far, context_far,
            bf16,
        )
        held["part_in"] = swap(held["far"][3])

    def heads_begin():
        near, far = held["near"], held["far"]
        heads.begin(
            call(
                head_gradients, "head_gradients", two_parts(3 * width_local, SMALL), info, tokens, near[0], far[0],
                near[1], far[1], near[2], far[2], held["shared"], held["shared_in"], held["bias"], order=order,
            )
        )

    up_outs = [(up_weight.shape, f32), (output_weight.shape, f32), mark]
    stages = [
        near_units, first_norm, up_begin, down.quarters, near_row, down.eighths,
        far_row, up.quarters, down.pieces, heads_begin, down.total, up.eighths,
        heads.quarters, down.join_two_z, up.pieces, heads.eighths, down.join_z, up.total,
        heads.pieces, up.join_two_z, down.join_two, heads.total, up.join_z, heads.join_two_z,
        up.join_two, heads.join_z, down.finish, heads.join_two, up.finish,
    ]
    for stage in stages:
        if stage == down.finish:
            down_total = stage(finish_down, [(down_weight.shape, f32), mark])[0]
        elif stage == up.finish:
            up_total, output_total, _ = stage(finish_up, up_outs)
        else:
            stage()
    heads_total = heads.finish(finish_heads, [wide_shape] * 3)
    small_total = heads.small[:, :width_local].astype(f32).reshape(8, -1)
    token_gradient = (held["first_delta"] + held["near"][3] + held["part_in"].astype(f32)).astype(bf16)

    return (
        losses.reshape(-1),
        query_gradient,
        token_gradient,
        heads_total[0],
        heads_total[1],
        heads_total[2],
        small_total[7, :width_local],
        small_total[7, width_local:],
        output_total,
        small_total[OB],
        small_total[FG],
        small_total[FS],
        up_total,
        small_total[5:7].reshape(-1),
        down_total,
        small_total[DB],
        small_total[SG],
    )


def solution(mesh):
    in_specs = (
        P("dp", None),
        P(("dp", "tensor"), None),
        P("dp", None),
        P("dp", None),
        P("dp", None),
        P("dp", None),
        P("dp"),
        P(None, "tensor"),
        P(None, "tensor"),
        P(None, "tensor"),
        P("tensor"),
        P("tensor"),
        P("tensor", None),
        P(),
        P(),
        P(),
        P(None, "tensor"),
        P("tensor"),
        P("tensor", None),
        P(),
        P(),
    )
    out_specs = (
        P("dp"),
        P("dp", None),
        P(("dp", "tensor"), None),
        P(None, "tensor"),
        P(None, "tensor"),
        P(None, "tensor"),
        P("tensor"),
        P("tensor"),
        P("tensor", None),
        P(),
        P(),
        P(),
        P(None, "tensor"),
        P("tensor"),
        P("tensor", None),
        P(),
        P(),
    )
    return jax.shard_map(shards, mesh=mesh, in_specs=in_specs, out_specs=out_specs, check_vma=False)
```

```python
import functools
import math

import jax
import jax.numpy as jnp
from jax import lax
from jax.experimental import pallas as pl
from jax.experimental.pallas import tpu as pltpu
from jax.sharding import PartitionSpec as P

D = 768
HD = 64
LANES = 128

norm_eps = 1e-05
neg_large = -1e30
root_half = 0.7071067811865476
inv_root_tau = 0.3989422804014327
log2_e = 1.4426950408889634

f32, bf16 = jnp.float32, jnp.bfloat16
COSTS = dict(
    attend_far=8, attend_near=7, forward=15, loss_back=4,
    unit_back_far=4, unit_back_near=0.4, down_gradient=3, up_gradient=0.16,
    first_back=1.8, attend_back_near=3.5, attend_back_far=3.5, head_gradients=5,
    down_add_halves=2, down_add_quarters=2, down_add_eighths=2, down_add_last=2,
    down_join_pieces=2, down_join_eighths=2, down_join_quarters=2, down_finish_down=6,
    up_add_halves=2, up_add_quarters=2, up_add_eighths=2, up_add_last=2,
    up_join_pieces=2, up_join_eighths=2, up_join_quarters=2, up_finish_up=6,
    heads_add_halves=2, heads_add_quarters=2, heads_add_eighths=2, heads_add_last=2,
    heads_join_pieces=2, heads_join_eighths=6, heads_join_quarters=2, heads_finish_heads=8,
)
FLOPS = int(1.15e+09)
SMALL = 16


def bits_of(axis):
    return lax.axis_size(axis).bit_length() - 1


def flip_by(value, axis, mask):
    size = lax.axis_size(axis)
    return lax.ppermute(value, axis, [(i, i ^ mask) for i in range(size)])


def swap(value):
    return flip_by(value, "tensor", 1)


def dot(left, right):
    return jnp.dot(left, right, preferred_element_type=f32)


def dot_t(left, right):
    return lax.dot_general(left, right, (((1,), (1,)), ((), ())), preferred_element_type=f32)


def t_dot(left, right):
    return lax.dot_general(left, right, (((0,), (0,)), ((), ())), preferred_element_type=f32)


class Late:
    def __init__(self, source, held, semaphore):
        self.held, self.waited = held, False
        self.shape, self.dtype = held.shape, held.dtype
        self.copy = pltpu.make_async_copy(source, held, semaphore)
        self.copy.start()

    def wait(self):
        if not self.waited:
            self.copy.wait()
        self.waited = True
        return self.held


class Early:
    def __init__(self, held, target, semaphore):
        self.held, self.target, self.semaphore, self.sent = held, target, semaphore, False
        self.shape, self.dtype = held.shape, held.dtype

    def __getitem__(self, at):
        return self.held[at]

    def __setitem__(self, at, value):
        self.held[at] = value

    def send(self, *at):
        source, target = (self.held.at[at], self.target.at[at]) if at else (self.held, self.target)
        pltpu.make_async_copy(source, target, self.semaphore).start()
        self.sent = True

    def finish(self):
        if not self.sent:
            self.send()
        pltpu.make_async_copy(self.held, self.target, self.semaphore).wait()


def ready(*values):
    return [value.wait() if isinstance(value, Late) else value for value in values]


def call(kernel, name, outs, *args, scratch=(), late=(), early=(), order=None, grant=20, final=()):
    after = order or []
    count, waits, made = len(args), len(after), len(outs)
    held = [pltpu.VMEM(args[i].shape, args[i].dtype) for i in late] + [pltpu.VMEM(*outs[i]) for i in early]
    args = [pltpu.with_memory_space_constraint(a, pltpu.HBM) if i in late else a for i, a in enumerate(args)]

    def body(*refs):
        inputs = list(refs[:count])
        results = list(refs[count + waits : count + waits + made])
        rest = refs[count + waits + made :]
        scratches, rest = rest[: len(scratch)], rest[len(scratch) :]
        for k, i in enumerate(late):
            inputs[i] = Late(inputs[i], rest[k], rest[-1].at[k])
        for k, i in enumerate(early, len(late)):
            results[i] = Early(rest[k], results[i], rest[-1].at[k])
        kernel(*inputs, *results, *scratches)
        for i in early:
            results[i].finish()

    specs = [pl.BlockSpec(memory_space=pltpu.SMEM)]
    specs += [pl.BlockSpec(memory_space=pltpu.HBM if i in late else pltpu.VMEM) for i in range(1, count)]
    specs += [pl.BlockSpec(memory_space=pl.ANY)] * waits
    own = [pltpu.SemaphoreType.DMA((len(held),))] if held else []
    made_by = pl.pallas_call(
        body,
        name=name,
        out_shape=[
            jax.ShapeDtypeStruct(*out) if i in final else (pltpu.HBM if i in early else pltpu.VMEM)(*out)
            for i, out in enumerate(outs)
        ],
        in_specs=specs,
        out_specs=[pl.BlockSpec(memory_space=pltpu.HBM if i in early else pltpu.VMEM) for i in range(made)],
        scratch_shapes=[*scratch, *held, *own],
        compiler_params=pltpu.CompilerParams(vmem_limit_bytes=grant << 20),
        cost_estimate=pl.CostEstimate(
            flops=int(COSTS[name] * FLOPS), bytes_accessed=1, transcendentals=0
        ),
    )(*args, *after)
    if order is not None:
        order[:] = [made_by[-1]]
    return made_by


def rows_at(index, size):
    return pl.ds(pl.multiple_of(index * size, size), size)


def add_low(left, right):
    return (left.astype(f32) + right.astype(f32)).astype(bf16)


BX, BY, BZ, BT, BD, PLACES = range(6)


def add_halves(info, keep_a, came_a, keep_b, came_b, send_a, kept_a, send_b, kept_b):
    quarter = keep_b.shape[0] // 2
    for bit, keep, came, send, kept in (
        (info[BY], keep_a, came_a, send_a, kept_a),
        (info[BX], keep_b, came_b, send_b, kept_b),
    ):
        mine, other = rows_at(bit, quarter), rows_at(1 - bit, quarter)
        send[:quarter] = add_low(keep[other], came[other])
        kept[:quarter] = add_low(keep[mine], came[mine])
        if keep.shape[0] > 2 * quarter:
            extra = add_low(keep[2 * quarter :], came[2 * quarter :])
            send[quarter:] = extra
            kept[quarter:] = extra


def add_quarters(info, keep_a, came_a, keep_b, came_b, send, kept):
    quarter, width = keep_b.shape[0], keep_a.shape[1]
    half = quarter // 2
    bit = info[BZ] & 1
    for out, side in ((send, 1 - bit), (kept, bit)):
        at = rows_at(side, half)
        out[:half, :width] = add_low(keep_a[at], came_a[at])
        out[:half, width:] = add_low(keep_b[at], came_b[at])
        if keep_a.shape[0] > quarter:
            out[half:, :width] = add_low(keep_a[quarter:], came_a[quarter:])
            out[half:, width:] = jnp.zeros((out.shape[0] - half, out.shape[1] - width), bf16)


def add_eighths(info, keep, came, send, kept, *, half):
    bit = info[BZ] >> 1
    for out, side in ((send, 1 - bit), (kept, bit)):
        at = rows_at(side, half)
        out[:half] = add_low(keep[at], came[at])
        if kept.shape[0] > half:
            out[half:] = add_low(keep[2 * half :], came[2 * half :])


def add_last(info, keep, came, total, *small):
    size = total.shape[0]
    total[...] = add_low(keep[:size], came[:size])
    if small:
        small[0][...] = add_low(keep[size:], came[size:])


def join_pieces(info, own, came, eighth):
    size = own.shape[0]
    bit = info[BZ] >> 1
    eighth[rows_at(bit, size)] = own[...]
    eighth[rows_at(1 - bit, size)] = came[...]


def join_eighths(info, own, came, quarter_a, quarter_b):
    size, width = own.shape[0], quarter_a.shape[1]
    bit = info[BZ] & 1
    for source, side in ((own, bit), (came, 1 - bit)):
        quarter_a[rows_at(side, size)] = source[:, :width]
        quarter_b[rows_at(side, size)] = source[:, width:]


def join_quarters(info, own_a, came_a, own_b, came_b, half_a, half_b):
    size = own_a.shape[0]
    for bit, own, came, half in (
        (info[BY], own_a, came_a, half_a),
        (info[BX], own_b, came_b, half_b),
    ):
        half[rows_at(bit, size)] = own[...]
        half[rows_at(1 - bit, size)] = came[...]


def finish_down(info, own_a, came_a, own_b, came_b, out, mark):
    mark[...] = jnp.zeros_like(mark)
    size = own_a.shape[0]
    for part, bit, own, came in ((0, info[BX], own_a, came_a), (1, info[BY], own_b, came_b)):
        for side, source in ((bit, own), (1 - bit, came)):
            at = rows_at(2 * part + side, size)
            out[at] = source[...].astype(f32)
            out.send(at)


def put(out, rows, columns, value):
    at = rows, pl.ds(columns, value.shape[1])
    out[at] = value.astype(f32)
    out.send(*at)


def finish_up(info, own_a, came_a, own_b, came_b, up, output, mark):
    mark[...] = jnp.zeros_like(mark)
    size, width = own_a.shape
    rest = up.shape[1] - width
    for side, source in ((info[BX], own_a), (1 - info[BX], came_a)):
        put(up, rows_at(side, size), 0, source[...])
    for side, source in ((info[BY], own_b), (1 - info[BY], came_b)):
        put(up, rows_at(side, size), width, source[:, :rest])
        at = slice(None), rows_at(side, size)
        output[at] = source[:, rest:].astype(f32)
        output.send(*at)


def finish_heads(info, own_a, came_a, own_b, came_b, query, key, value):
    size, width = own_a.shape
    own = query.shape[1]
    rest = width - own
    for side, source in ((info[BX], own_a), (1 - info[BX], came_a)):
        put(query, rows_at(side, size), 0, source[:, :own])
        put(key, rows_at(side, size), 0, source[:, own:])
    for side, source in ((info[BY], own_b), (1 - info[BY], came_b)):
        put(key, rows_at(side, size), rest, source[:, : own - rest])
        put(value, rows_at(side, size), 0, source[:, own - rest :])


class Reduction:
    def __init__(self, name, info, order):
        self.name, self.info, self.order = name, info, order

    def begin(self, halves):
        self.made = halves
        send_a, send_b, self.keep_a, self.keep_b = halves
        self.came = [flip_by(send_a, "dp", 1), flip_by(send_b, "dp", 2)]

    def staged(self, kernel, outs, *args, early=(), **fixed):
        bound = functools.partial(kernel, **fixed) if fixed else kernel
        self.made = call(bound, self.name + kernel.__name__, outs, self.info, *args, order=self.order, early=early)
        return self.made

    def quarters(self):
        (first, self.wide), (half, self.narrow) = self.keep_a.shape, self.keep_b.shape
        self.extra, self.quarter = first - half, half // 2
        a, b = ((self.quarter + self.extra, self.wide), bf16), ((self.quarter, self.narrow), bf16)
        send_a, self.keep_a, send_b, self.keep_b = self.staged(
            add_halves, [a, a, b, b], self.keep_a, self.came[0], self.keep_b, self.came[1]
        )
        self.came = [flip_by(send_a, "dp", 2), flip_by(send_b, "dp", 1)]

    def eighths(self):
        self.both = self.wide + self.narrow
        piece = ((self.quarter // 2 + self.extra, self.both), bf16)
        send, self.own = self.staged(
            add_quarters, [piece] * 2, self.keep_a, self.came[0], self.keep_b, self.came[1]
        )
        self.came = flip_by(send, "dp", 4)

    def pieces(self):
        size = self.quarter // 4
        piece = ((size + self.extra, self.both), bf16)
        send, self.own = self.staged(add_eighths, [piece] * 2, self.own, self.came, half=size)
        self.came = flip_by(send, "dp", 8)

    def total(self):
        outs = [((self.quarter // 4, self.both), bf16)]
        outs += [((self.extra, self.both), bf16)] if self.extra else []
        self.own, *small = [
            functools.reduce(
                lambda value, bit: add_low(value, flip_by(value, "dp", 1 << bit)),
                range(4, bits_of("dp")),
                made,
            )
            for made in self.staged(add_last, outs, self.own, self.came)
        ]
        self.small = small[0] if small else None
        self.came = flip_by(self.own, "dp", 8)

    def join_two_z(self):
        piece = ((self.quarter // 2, self.both), bf16)
        (self.own,) = self.staged(join_pieces, [piece], self.own, self.came)
        self.came = flip_by(self.own, "dp", 4)

    def join_z(self):
        outs = [((self.quarter, self.wide), bf16), ((self.quarter, self.narrow), bf16)]
        self.keep_a, self.keep_b = self.staged(join_eighths, outs, self.own, self.came)
        self.came = [flip_by(self.keep_a, "dp", 2), flip_by(self.keep_b, "dp", 1)]

    def join_two(self):
        outs = [((2 * self.quarter, self.wide), bf16), ((2 * self.quarter, self.narrow), bf16)]
        self.keep_a, self.keep_b = self.staged(
            join_quarters, outs, self.keep_a, self.came[0], self.keep_b, self.came[1]
        )
        self.came = [flip_by(self.keep_a, "dp", 1), flip_by(self.keep_b, "dp", 2)]

    def finish(self, kernel, outs):
        return self.staged(
            kernel, outs, self.keep_a, self.came[0], self.keep_b, self.came[1],
            early=[i for i, out in enumerate(outs) if out[0][0] > 8],
        )


def down_gradient(info, unit, active, unit_in, active_in, send_a, send_b, keep_a, keep_b):
    size = send_a.shape[0]
    unit, active, unit_in, active_in = ready(unit, active, unit_in, active_in)
    for side in range(2):
        for part, bit, outs in ((0, info[BX], (send_a, keep_a)), (1, info[BY], (send_b, keep_b))):
            at = rows_at(2 * part + (bit if side else 1 - bit), size)
            outs[side][...] = (
                t_dot(active[:, at], unit[...]) + t_dot(active_in[:, at], unit_in[...])
            ).astype(bf16)


def up_gradient(
    info, delta, first, delta_in, first_in, branch, branch_far, context, context_far, send_a, send_b, keep_a, keep_b,
    bias,
):
    size, width = send_a.shape
    rest = delta.shape[1] - width
    for side in range(2):
        for bit, outs, columns in (
            (info[BX], (send_a, keep_a), pl.ds(0, width)),
            (info[BY], (send_b, keep_b), pl.ds(width, rest)),
        ):
            at = rows_at(bit if side else 1 - bit, size)
            out = outs[side]
            out[:, : columns.size] = (
                t_dot(first[:, at], delta[:, columns]) + t_dot(first_in[:, at], delta_in[:, columns])
            ).astype(bf16)
            if columns.size == rest:
                out[:, rest:] = (dot(context[...], branch[:, at]) + dot(context_far[...], branch_far[:, at])).astype(
                    bf16
                )
    ones = jnp.ones((8, delta.shape[0]), bf16)
    bias[...] = dot(ones, delta[...]) + dot(ones, delta_in[...])


def head_gradients(
    info, tokens, query, query_far, key, key_far, value, value_far, shared, shared_in, bias, send_a, send_b, keep_a,
    keep_b,
):
    half, width = send_b.shape[0], send_a.shape[1]
    length, narrow = query.shape
    rest = width - narrow
    near, far = rows_at(info[BT], length), rows_at(1 - info[BT], length)
    for side in range(2):
        for bit, outs, sources in (
            (info[BX], (send_a, keep_a), ((query, query_far, 0, narrow), (key, key_far, 0, rest))),
            (info[BY], (send_b, keep_b), ((key, key_far, rest, narrow - rest), (value, value_far, 0, narrow))),
        ):
            at = rows_at(bit if side else 1 - bit, half)
            tokens_near, tokens_far = tokens[near, at], tokens[far, at]
            put_at = 0
            for left, right, first, count in sources:
                columns = pl.ds(first, count)
                outs[side][:half, pl.ds(put_at, count)] = (
                    t_dot(tokens_near, left[:, columns]) + t_dot(tokens_far, right[:, columns])
                ).astype(bf16)
                put_at += count
    ones = jnp.ones((8, length), bf16)
    query_sum = dot(ones, query[...]) + dot(ones, query_far[...])
    value_sum = dot(ones, value[...]) + dot(ones, value_far[...])
    sums = shared[...] + shared_in[...]
    pairs = [(sums[k : k + 1, :narrow], sums[k : k + 1, narrow:]) for k in range(5)]
    pairs += [(bias[:1, k * narrow : (k + 1) * narrow], bias[:1, (k + 1) * narrow : (k + 2) * narrow]) for k in (0, 2)]
    pairs += [(query_sum[:1], value_sum[:1])]
    block = jnp.concatenate([piece for pair in pairs for piece in pair], 0)
    block = jnp.concatenate([block, jnp.zeros((SMALL, rest), f32)], 1).astype(bf16)
    send_a[half:] = block
    keep_a[half:] = block


def attend(
    info, tokens, query_weight, key_weight, value_weight, query_bias, value_bias, segments, validity,
    context, query, key, value, raised, shares, shade, *, far,
):
    length = context.shape[1]
    row = 1 - info[BT] if far else info[BT]
    segments, validity = ready(segments, validity)
    mark = segments[pl.ds(row, 1)]
    seen = jnp.where(validity[pl.ds(row, 1)] > 0, mark, -1)
    column = jnp.broadcast_to(seen.astype(f32), (8, length)).T[:, :1]
    shade[...] = jnp.where(column == mark.astype(f32), 0.0, neg_large)
    tokens, query_weight, query_bias, value_bias = ready(tokens, query_weight, query_bias, value_bias)
    x = tokens[rows_at(row, length)]
    scale = 1.0 / math.sqrt(HD)
    query[...] = (
        (dot(x, query_weight[...]) + query_bias[...].astype(f32)[None]).astype(bf16) * bf16(scale)
    )
    query.send()
    (key_weight,) = ready(key_weight)
    key[...] = dot(x, key_weight[...]).astype(bf16)
    key.send()
    (value_weight,) = ready(value_weight)
    value[...] = (dot(x, value_weight[...]) + value_bias[...].astype(f32)[None]).astype(bf16)
    value.send()
    low = lax.broadcasted_iota(jnp.int32, (length, LANES), 1) < HD

    def body(pair, _):
        at = pl.ds(pl.multiple_of(pair * LANES, LANES), LANES)
        q, k, v = query[:, at], key[:, at], value[:, at]

        def logits_of(member):
            return dot_t(k, jnp.where(low if member == 0 else ~low, q, jnp.zeros_like(q))) + shade[...]

        coming = logits_of(0)
        for member in range(2):
            logits, coming = coming, logits_of(1) if member == 0 else None
            number = 2 * pair + member
            peak = jnp.max(logits, 0, keepdims=True)
            lifted = jnp.exp(logits - peak).astype(bf16)
            raised[number] = lifted
            raised.send(number)
            sums = t_dot(jnp.where(low if member == 0 else ~low, v, jnp.ones_like(v)), lifted)
            other = (1 - member) * HD
            share = 1.0 / sums[other : other + 1]
            shares[pl.ds(number, 1)] = share
            rows = pl.ds(pl.multiple_of(number * HD, HD), HD)
            context[rows] = (sums[member * HD : member * HD + HD] * share).astype(bf16)
            context.send(rows)
        return 0

    lax.fori_loop(0, context.shape[0] // LANES, body, 0)


def attend_back(
    info, branch, output_weight, shares, value, context, raised, key, query, query_weight, key_weight, value_weight,
    query_delta, key_delta, value_delta, part, context_delta,
):
    length = part.shape[0]
    branch, output_weight = ready(branch, output_weight)
    context_delta[...] = dot_t(output_weight[...], branch[...]).astype(bf16)
    value, context, raised, key, query = ready(value, context, raised, key, query)
    low = lax.broadcasted_iota(jnp.int32, (length, LANES), 1) < HD
    scale = 1.0 / math.sqrt(HD)

    def body(pair, _):
        at = pl.ds(pl.multiple_of(pair * LANES, LANES), LANES)
        queries, keys, values = [], [], []
        for member in range(2):
            rows = pl.ds(pl.multiple_of(pair * LANES + member * HD, HD), HD)
            delta = context_delta[rows].astype(f32) * shares[pl.ds(2 * pair + member, 1)]
            inner = jnp.sum(delta * context[rows].astype(f32), 0, keepdims=True)
            delta = delta.astype(bf16)
            none = jnp.zeros_like(delta)
            delta = jnp.concatenate([none, delta] if member else [delta, none], 0)
            lifted = raised[2 * pair + member]
            logit_delta = (lifted.astype(f32) * (dot(value[:, at], delta) - inner)).astype(bf16)
            values.append(dot_t(lifted, delta))
            keys.append(dot(logit_delta, query[:, at]))
            queries.append(t_dot(key[:, at], logit_delta)[member * HD : member * HD + HD])
        query_delta[:, at] = (jnp.concatenate(queries, 0) * scale).T.astype(bf16)
        key_delta[:, at] = jnp.where(low, keys[0], keys[1]).astype(bf16)
        value_delta[:, at] = (values[0] + values[1]).astype(bf16)
        return 0

    lax.fori_loop(0, query.shape[1] // LANES, body, 0)
    query_weight, key_weight, value_weight = ready(query_weight, key_weight, value_weight)
    part[...] = (
        dot_t(query_delta[...], query_weight[...])
        + dot_t(key_delta[...], key_weight[...])
        + dot_t(value_delta[...], value_weight[...])
    ).astype(part.dtype)


OB, FG, FS, DB, SG = range(5)


def center(inputs):
    shifted = inputs - jnp.mean(inputs, -1, keepdims=True)
    spread = jnp.mean(shifted * shifted, -1, keepdims=True)
    row_scale = lax.rsqrt(spread + norm_eps)
    return shifted * row_scale, row_scale


def norm_back(out_delta, normed, row_scale, norm_gain):
    scaled = out_delta * norm_gain
    first_mean = jnp.mean(scaled, -1, keepdims=True)
    second_mean = jnp.mean(scaled * normed, -1, keepdims=True)
    return row_scale * (scaled - first_mean - normed * second_mean)


def forward(
    info, context, output_near, tokens, context_in, output_far, up_far, down_far, up_near, down_near, vectors,
    bias_near, bias_far, first_low, first_normed, first_scale, active_near, active_far, slope_near, slope_far,
    second_normed, second_scale, summary, total,
):
    length = total.shape[0]
    step = length // 2
    halves = (pl.ds(0, step), pl.ds(step, step))
    base = info[BT] * length
    context, output_near, tokens = ready(context, output_near, tokens)
    for at in halves:
        heads = t_dot(context[:, at], output_near[...]) + t_dot(context_in[:, at], output_far[...])
        x = tokens[pl.ds(pl.multiple_of(base + at.start, step), step)].astype(f32)
        normed, scale = center(x + (heads + vectors[OB : OB + 1]))
        out = normed * vectors[FG : FG + 1] + vectors[FS : FS + 1]
        first_normed[at] = normed.astype(bf16)
        first_scale[at] = scale
        first_low[at] = out.astype(bf16)
        total[at] = out + vectors[DB : DB + 1]
    first_low.send()
    first_normed.send()
    first_scale.send()

    width = 6 * LANES
    groups = (
        (up_far, down_far, bias_far, active_far, slope_far),
        (up_near, down_near, bias_near, active_near, slope_near),
    )
    for up, down, bias, active, slope in groups:
        up, down = ready(up, down)

        def body(index, _, up=up, down=down, bias=bias, active=active, slope=slope):
            units = rows_at(index, width)

            def hidden_of(at):
                return dot(first_low[at], up[:, units]) + bias[:, units]

            coming = hidden_of(halves[0])
            for at in halves:
                hidden, coming = coming, hidden_of(halves[1]) if at is halves[0] else None
                share = 0.5 * (1.0 + lax.erf(hidden * root_half))
                low = (hidden * share).astype(bf16)
                active[at, units] = low
                slope[at, units] = (share + hidden * jnp.exp(-0.5 * hidden * hidden) * inv_root_tau).astype(bf16)
                total[at] += dot(low, down[units])
            active.send(slice(None), units)
            slope.send(slice(None), units)
            return 0

        lax.fori_loop(0, bias.shape[1] // width, body, 0)

    for at in halves:
        normed, scale = center(total[at])
        second_normed[at] = normed.astype(bf16)
        second_scale[at] = scale
        total[at] = normed * vectors[SG : SG + 1]
    rows = [total[pl.ds(info[PLACES + k], 1)] for k in range(summary.shape[0])]
    summary[...] = jnp.concatenate(rows, 0).astype(bf16)


def loss_back(
    info, near, far, upper, normed, scale, vectors, losses, query_gradient, second_delta, unit_delta, sums, all_rows,
    out_delta,
):
    width = upper.shape[1]
    all_rows[: near.shape[0]] = near[...]
    all_rows[near.shape[0] :] = far[...]
    here = info[BT] * near.shape[0] + info[BD] * 8
    places = near.shape[0] // 8
    count = all_rows.shape[0]
    block = min(256, count)
    score_scale = 1.0 / math.sqrt(width)
    own_passages = 4

    def body(index, sums_in):
        at = rows_at(index, block)
        rows = all_rows[at, :width]
        digits = all_rows[at, width:].astype(f32)
        scores = dot_t(rows, all_rows[:, :width]) * score_scale
        columns = lax.broadcasted_iota(jnp.int32, (block, count), 1) ^ here
        numbers = (lax.broadcasted_iota(jnp.int32, (block, 1), 0) + index * block) ^ here
        scores = jnp.where((columns & 7) < own_passages, scores, neg_large)
        peak = jnp.max(scores, -1, keepdims=True)
        raised = jnp.exp(scores - peak)
        total = jnp.sum(raised, -1, keepdims=True)
        target = (digits[:, 0:1] * 16.0 + digits[:, 1:2]).astype(jnp.int32)
        chosen = columns == target
        lost = peak + jnp.log(total) - jnp.sum(jnp.where(chosen, scores, 0.0), -1, keepdims=True)
        delta = raised / total - chosen.astype(f32)
        delta = jnp.where((numbers & 7) >= own_passages, delta, 0.0).astype(bf16)
        wide = delta.astype(f32)
        places_here = lax.broadcasted_iota(jnp.int32, (block, 8), 1)
        wanted = ((places_here >> 2) * places + info[BD]) * 8 + own_passages + (places_here & 3)
        mine = (numbers == wanted).astype(f32)
        own_losses = sums_in[0] + jnp.sum(mine * lost, 0, keepdims=True)
        own_delta = sums_in[1] + t_dot(mine.astype(bf16), delta)
        results = []
        for k in range(own_passages):
            column = (info[BT] * places + info[BD]) * 8 + k
            share = jnp.sum(jnp.where(columns == column, wide, 0.0), -1, keepdims=True)
            results.append(sums_in[2 + k] + jnp.sum(share * rows.astype(f32), 0, keepdims=True))
        return own_losses, own_delta, *results

    zero = jnp.zeros((1, width), f32)
    first = (jnp.zeros((1, 8), f32), jnp.zeros((8, count), f32), *[zero] * own_passages)
    if count == block:
        own_losses, own_delta, *passage_delta = body(0, first)
    else:
        own_losses, own_delta, *passage_delta = lax.fori_loop(0, count // block, body, first)
    upper, normed, scale = ready(upper, normed, scale)
    out_delta[...] = upper[...].astype(f32)
    for k in range(own_passages):
        out_delta[pl.ds(info[PLACES + k], 1)] += passage_delta[k] * score_scale
    query_gradient[...] = dot(own_delta.astype(bf16), all_rows[:, :width]) * score_scale
    losses[...] = own_losses

    length = upper.shape[0]
    step = length // 4
    bias_sum = gain_sum = zero
    for start in range(0, length, step):
        at = pl.ds(start, step)
        n = normed[at].astype(f32)
        delta = norm_back(out_delta[at], n, scale[at], vectors[SG : SG + 1])
        unit_delta[at] = delta.astype(bf16)
        second_delta[at] = delta
        bias_sum += jnp.sum(delta, 0, keepdims=True)
        gain_sum += jnp.sum(out_delta[at] * n, 0, keepdims=True)
    sums[...] = jnp.concatenate(
        [jnp.zeros((DB, width), f32), bias_sum, gain_sum, jnp.zeros((7 - SG, width), f32)], 0
    )


def unit_back(info, unit_delta, down_weight, slope, hidden_delta):
    width = 6 * LANES

    def body(index, _):
        units = rows_at(index, width)
        delta = dot_t(unit_delta[...], down_weight[units])
        hidden_delta[:, units] = (delta * slope[:, units].astype(f32)).astype(bf16)
        return 0

    lax.fori_loop(0, down_weight.shape[0] // width, body, 0)


def first_back(
    info, delta_far, up_far, delta_near, up_near, second_delta, normed, scale, vectors, sums_in, first_delta,
    branch, sums, total,
):
    length, width = total.shape
    delta_far, up_far = ready(delta_far, up_far)
    total[...] = dot_t(delta_far[...], up_far[...])
    delta_near, up_near = ready(delta_near, up_near)
    total[...] += dot_t(delta_near[...], up_near[...])
    second_delta, normed = ready(second_delta, normed)
    step = length // 4
    zero = jnp.zeros((1, width), f32)
    bias_sum = gain_sum = shift_sum = zero
    for start in range(0, length, step):
        at = pl.ds(start, step)
        out_delta = second_delta[at] + total[at]
        n = normed[at].astype(f32)
        delta = norm_back(out_delta, n, scale[at], vectors[FG : FG + 1])
        branch[at] = delta.astype(bf16)
        first_delta[at] = delta
        bias_sum += jnp.sum(delta, 0, keepdims=True)
        gain_sum += jnp.sum(out_delta * n, 0, keepdims=True)
        shift_sum += jnp.sum(out_delta, 0, keepdims=True)
    sums[...] = sums_in[...] + jnp.concatenate(
        [bias_sum, gain_sum, shift_sum, jnp.zeros((7 - FS, width), f32)], 0
    )


def shards(
    tokens,
    upper_delta,
    segments,
    summary_index,
    validity,
    queries,
    positives,
    query_weight,
    key_weight,
    value_weight,
    query_bias,
    value_bias,
    output_weight,
    output_bias,
    first_gain,
    first_shift,
    up_weight,
    up_bias,
    down_weight,
    down_bias,
    second_gain,
):
    row_count, length = segments.shape
    token_count = row_count * length
    members = lax.axis_size("tensor")
    place = lax.axis_index("tensor")
    own_count = token_count // members
    width_local = query_weight.shape[1]
    heads_local = width_local // HD
    at_dp = lax.axis_index("dp")
    half_rows = D // 2

    def own(value):
        part = value.shape[0] // members
        return lax.dynamic_slice_in_dim(value, place * part, part, 0)

    info = jnp.concatenate(
        [
            jnp.stack([at_dp & 1, (at_dp >> 1) & 1, (at_dp >> 2) & 3, place, at_dp]).astype(jnp.int32),
            own(summary_index).reshape(-1),
        ]
    )
    vectors = jnp.stack([output_bias, first_gain, first_shift, down_bias, second_gain]).astype(f32)
    vectors = jnp.concatenate([vectors, jnp.zeros((3, D), f32)], 0)
    output_far = swap(output_weight)
    up_far = swap(up_weight)
    bias_far = swap(up_bias.reshape(1, -1))
    down_far = swap(down_weight)

    context_shape = ((length, width_local), bf16)

    def attention(far):
        return call(
            functools.partial(attend, far=far),
            "attend_far" if far else "attend_near",
            [((width_local, length), bf16)] + [context_shape] * 3
            + [((heads_local, length, length), bf16), ((heads_local + -heads_local % 8, length), f32)],
            info, tokens, query_weight, key_weight, value_weight, query_bias, value_bias, segments, validity,
            scratch=[pltpu.VMEM((length, length), f32)],
            late=(1, 2, 3, 4, 5, 6, 7, 8) if far else (),
            early=(0, 1, 2, 3, 4, 5),
        )

    context_far, query_far, key_far, value_far, raised_far, shares_far = attention(True)
    context_in = swap(context_far)
    context, query, key, value, raised, shares = attention(False)

    row, units = ((length, D), bf16), ((length, up_weight.shape[1]), bf16)
    scale_shape = ((length, 1), f32)
    own_passages = summary_index.shape[1]
    (
        first_low, first_normed, first_scale, active, active_far, slope, slope_far, second_normed, second_scale,
        summary,
    ) = call(
        forward, "forward",
        [row, row, scale_shape, units, units, units, units, row, scale_shape, ((own_passages, D), bf16)],
        info, context, output_weight, tokens, context_in, output_far, up_far, down_far, up_weight, down_weight,
        vectors, up_bias.reshape(1, -1).astype(f32), bias_far.astype(f32),
        late=(1, 2, 3, 7, 8, 9), early=(0, 1, 2, 3, 4, 5, 6, 7, 8), grant=40,
        scratch=[pltpu.VMEM((length, D), f32)],
    )
    first_in = swap(first_low)
    active_in = swap(active_far)

    places = lax.axis_size("dp")
    row_of = ((positives % 8) // 4 * places + positives // 8) * 8 + positives % 4
    digits = jnp.stack([row_of // 16, row_of % 16], 1).astype(bf16)
    digits = jnp.pad(digits, ((0, 0), (0, LANES - 2)))
    bundle = jnp.concatenate(
        [jnp.pad(summary, ((0, 0), (0, LANES))), own(jnp.concatenate([queries, digits], 1))], 0
    )
    for low in (1, 4):
        bundle = jnp.concatenate([bundle, *[flip_by(bundle, "dp", low * k) for k in (1, 2, 3)]], 0)
    for bit in range(4, bits_of("dp")):
        bundle = jnp.concatenate([bundle, flip_by(bundle, "dp", 1 << bit)], 0)
    bundle_far = swap(bundle)
    gathered = 2 * bundle.shape[0]
    query_count = queries.shape[0]
    losses, query_gradient, second_delta, unit_delta, sums = call(
        loss_back, "loss_back",
        [((1, query_count), f32), ((query_count, D), f32), ((length, D), f32), row, ((8, D), f32)],
        info, bundle, bundle_far, upper_delta, second_normed, second_scale, vectors,
        late=(3, 4, 5), final=(0, 1), grant=20 if gathered <= 256 else 50,
        scratch=[pltpu.VMEM((gathered, D + LANES), bf16), pltpu.VMEM((length, D), f32)],
    )
    unit_in = swap(unit_delta)
    order = []

    def through_units(name, weight, slope):
        return call(
            unit_back, name, [units], info, unit_delta, weight, slope, order=order
        )[0]

    delta_far = through_units("unit_back_far", down_far, slope_far)
    delta_in = swap(delta_far)
    down, up, heads = [Reduction(name, info, order) for name in ("down_", "up_", "heads_")]
    held = {}
    wide_shape, mark = (query_weight.shape, f32), ((8, LANES), f32)
    down.begin(
        call(
            down_gradient, "down_gradient", [((half_rows, D), bf16)] * 4, info, unit_delta, active, unit_in, active_in,
            order=order,
        )
    )

    def two_parts(columns, extra=0):
        wide = (columns // 2 + LANES - 1) // LANES * LANES
        first, second = ((half_rows + extra, wide), bf16), ((half_rows, columns - wide), bf16)
        return [first, second, first, second]

    def near_units():
        held["delta"] = through_units("unit_back_near", down_weight, slope)

    def first_norm():
        held["first_delta"], held["branch"], held["shared"] = call(
            first_back, "first_back", [((length, D), f32), row, ((8, D), f32)], info, delta_far, up_far,
            held["delta"], up_weight, second_delta, first_normed, first_scale, vectors, sums,
            scratch=[pltpu.VMEM((length, D), f32)], order=order,
        )
        held["branch_far"], held["shared_in"] = swap(held["branch"]), swap(held["shared"])

    def up_begin():
        *halves, held["bias"] = call(
            up_gradient, "up_gradient",
            two_parts(up_weight.shape[1] + width_local) + [((8, up_weight.shape[1]), f32)],
            info, held["delta"], first_low, delta_in, first_in, held["branch"], held["branch_far"], context,
            context_far, order=order,
        )
        up.begin(halves)

    def attention_back(name, branch, shares, raised, query, key, value, context, kind):
        return call(
            attend_back,
            name,
            [context_shape] * 3 + [((length, D), kind)],
            info, branch, output_weight, shares, value, context, raised, key, query, query_weight, key_weight,
            value_weight,
            scratch=[pltpu.VMEM((width_local, length), bf16)],
            order=order,
        )

    def near_row():
        held["near"] = attention_back(
            "attend_back_near", held["branch"], shares, raised, query, key, value, context, f32
        )

    def far_row():
        held["far"] = attention_back(
            "attend_back_far", held["branch_far"], shares_far, raised_far, query_far, key_far, value_far, context_far,
            bf16,
        )
        held["part_in"] = swap(held["far"][3])

    def heads_begin():
        near, far = held["near"], held["far"]
        heads.begin(
            call(
                head_gradients, "head_gradients", two_parts(3 * width_local, SMALL), info, tokens, near[0], far[0],
                near[1], far[1], near[2], far[2], held["shared"], held["shared_in"], held["bias"], order=order,
            )
        )

    up_outs = [(up_weight.shape, f32), (output_weight.shape, f32), mark]
    stages = [
        near_units, first_norm, up_begin, down.quarters, near_row, down.eighths,
        far_row, up.quarters, down.pieces, heads_begin, down.total, up.eighths,
        heads.quarters, down.join_two_z, up.pieces, heads.eighths, down.join_z, up.total,
        heads.pieces, up.join_two_z, down.join_two, heads.total, up.join_z, heads.join_two_z,
        up.join_two, heads.join_z, down.finish, heads.join_two, up.finish,
    ]
    for stage in stages:
        if stage == down.finish:
            down_total = stage(finish_down, [(down_weight.shape, f32), mark])[0]
        elif stage == up.finish:
            up_total, output_total, _ = stage(finish_up, up_outs)
        else:
            stage()
    heads_total = heads.finish(finish_heads, [wide_shape] * 3)
    small_total = heads.small[:, :width_local].astype(f32).reshape(8, -1)
    token_gradient = (held["first_delta"] + held["near"][3] + held["part_in"].astype(f32)).astype(bf16)

    return (
        losses.reshape(-1),
        query_gradient,
        token_gradient,
        heads_total[0],
        heads_total[1],
        heads_total[2],
        small_total[7, :width_local],
        small_total[7, width_local:],
        output_total,
        small_total[OB],
        small_total[FG],
        small_total[FS],
        up_total,
        small_total[5:7].reshape(-1),
        down_total,
        small_total[DB],
        small_total[SG],
    )


def solution(mesh):
    in_specs = (
        P("dp", None),
        P(("dp", "tensor"), None),
        P("dp", None),
        P("dp", None),
        P("dp", None),
        P("dp", None),
        P("dp"),
        P(None, "tensor"),
        P(None, "tensor"),
        P(None, "tensor"),
        P("tensor"),
        P("tensor"),
        P("tensor", None),
        P(),
        P(),
        P(),
        P(None, "tensor"),
        P("tensor"),
        P("tensor", None),
        P(),
        P(),
    )
    out_specs = (
        P("dp"),
        P("dp", None),
        P(("dp", "tensor"), None),
        P(None, "tensor"),
        P(None, "tensor"),
        P(None, "tensor"),
        P("tensor"),
        P("tensor"),
        P("tensor", None),
        P(),
        P(),
        P(),
        P(None, "tensor"),
        P("tensor"),
        P("tensor", None),
        P(),
        P(),
    )
    return jax.shard_map(shards, mesh=mesh, in_specs=in_specs, out_specs=out_specs, check_vma=False)
```

```python
import functools
import math

import jax
import jax.numpy as jnp
from jax import lax
from jax.experimental import pallas as pl
from jax.experimental.pallas import tpu as pltpu
from jax.sharding import PartitionSpec as P

D = 768
HD = 64
LANES = 128

norm_eps = 1e-05
neg_large = -1e30
root_half = 0.7071067811865476
inv_root_tau = 0.3989422804014327
log2_e = 1.4426950408889634

f32, bf16 = jnp.float32, jnp.bfloat16
COSTS = dict(
    attend_far=8, attend_near=7, forward=15, loss_back=4,
    unit_back_far=4, unit_back_near=0.4, down_gradient=3, up_gradient=0.16,
    first_back=1.8, attend_back_near=3.5, attend_back_far=3.5, head_gradients=5,
    down_add_halves=2, down_add_quarters=2, down_add_eighths=2, down_add_last=2,
    down_join_pieces=2, down_join_eighths=2, down_join_quarters=2, down_finish_down=6,
    up_add_halves=2, up_add_quarters=2, up_add_eighths=2, up_add_last=2,
    up_join_pieces=2, up_join_eighths=2, up_join_quarters=2, up_finish_up=6,
    heads_add_halves=2, heads_add_quarters=2, heads_add_eighths=2, heads_add_last=2,
    heads_join_pieces=2, heads_join_eighths=6, heads_join_quarters=2, heads_finish_heads=8,
)
FLOPS = int(1.15e+09)
SMALL = 16


def bits_of(axis):
    return lax.axis_size(axis).bit_length() - 1


def flip_by(value, axis, mask):
    size = lax.axis_size(axis)
    return lax.ppermute(value, axis, [(i, i ^ mask) for i in range(size)])


def swap(value):
    return flip_by(value, "tensor", 1)


def dot(left, right):
    return jnp.dot(left, right, preferred_element_type=f32)


def dot_t(left, right):
    return lax.dot_general(left, right, (((1,), (1,)), ((), ())), preferred_element_type=f32)


def t_dot(left, right):
    return lax.dot_general(left, right, (((0,), (0,)), ((), ())), preferred_element_type=f32)


class Late:
    def __init__(self, source, held, semaphore):
        self.held, self.waited = held, False
        self.shape, self.dtype = held.shape, held.dtype
        self.copy = pltpu.make_async_copy(source, held, semaphore)
        self.copy.start()

    def wait(self):
        if not self.waited:
            self.copy.wait()
        self.waited = True
        return self.held


class Early:
    def __init__(self, held, target, semaphore):
        self.held, self.target, self.semaphore, self.sent = held, target, semaphore, False
        self.shape, self.dtype = held.shape, held.dtype

    def __getitem__(self, at):
        return self.held[at]

    def __setitem__(self, at, value):
        self.held[at] = value

    def send(self, *at):
        source, target = (self.held.at[at], self.target.at[at]) if at else (self.held, self.target)
        pltpu.make_async_copy(source, target, self.semaphore).start()
        self.sent = True

    def finish(self):
        if not self.sent:
            self.send()
        pltpu.make_async_copy(self.held, self.target, self.semaphore).wait()


def ready(*values):
    return [value.wait() if isinstance(value, Late) else value for value in values]


def call(kernel, name, outs, *args, scratch=(), late=(), early=(), order=None, grant=20, final=()):
    after = order or []
    count, waits, made = len(args), len(after), len(outs)
    held = [pltpu.VMEM(args[i].shape, args[i].dtype) for i in late] + [pltpu.VMEM(*outs[i]) for i in early]
    args = [pltpu.with_memory_space_constraint(a, pltpu.HBM) if i in late else a for i, a in enumerate(args)]

    def body(*refs):
        inputs = list(refs[:count])
        results = list(refs[count + waits : count + waits + made])
        rest = refs[count + waits + made :]
        scratches, rest = rest[: len(scratch)], rest[len(scratch) :]
        for k, i in enumerate(late):
            inputs[i] = Late(inputs[i], rest[k], rest[-1].at[k])
        for k, i in enumerate(early, len(late)):
            results[i] = Early(rest[k], results[i], rest[-1].at[k])
        kernel(*inputs, *results, *scratches)
        for i in early:
            results[i].finish()

    specs = [pl.BlockSpec(memory_space=pltpu.SMEM)]
    specs += [pl.BlockSpec(memory_space=pltpu.HBM if i in late else pltpu.VMEM) for i in range(1, count)]
    specs += [pl.BlockSpec(memory_space=pl.ANY)] * waits
    own = [pltpu.SemaphoreType.DMA((len(held),))] if held else []
    made_by = pl.pallas_call(
        body,
        name=name,
        out_shape=[
            jax.ShapeDtypeStruct(*out) if i in final else (pltpu.HBM if i in early else pltpu.VMEM)(*out)
            for i, out in enumerate(outs)
        ],
        in_specs=specs,
        out_specs=[pl.BlockSpec(memory_space=pltpu.HBM if i in early else pltpu.VMEM) for i in range(made)],
        scratch_shapes=[*scratch, *held, *own],
        compiler_params=pltpu.CompilerParams(vmem_limit_bytes=grant << 20),
        cost_estimate=pl.CostEstimate(
            flops=int(COSTS[name] * FLOPS), bytes_accessed=1, transcendentals=0
        ),
    )(*args, *after)
    if order is not None:
        order[:] = [made_by[-1]]
    return made_by


def rows_at(index, size):
    return pl.ds(pl.multiple_of(index * size, size), size)


def add_low(left, right):
    return (left.astype(f32) + right.astype(f32)).astype(bf16)


BX, BY, BZ, BT, BD, PLACES = range(6)


def add_halves(info, keep_a, came_a, keep_b, came_b, send_a, kept_a, send_b, kept_b):
    quarter = keep_b.shape[0] // 2
    for bit, keep, came, send, kept in (
        (info[BY], keep_a, came_a, send_a, kept_a),
        (info[BX], keep_b, came_b, send_b, kept_b),
    ):
        mine, other = rows_at(bit, quarter), rows_at(1 - bit, quarter)
        send[:quarter] = add_low(keep[other], came[other])
        kept[:quarter] = add_low(keep[mine], came[mine])
        if keep.shape[0] > 2 * quarter:
            extra = add_low(keep[2 * quarter :], came[2 * quarter :])
            send[quarter:] = extra
            kept[quarter:] = extra


def add_quarters(info, keep_a, came_a, keep_b, came_b, send, kept):
    quarter, width = keep_b.shape[0], keep_a.shape[1]
    half = quarter // 2
    bit = info[BZ] & 1
    for out, side in ((send, 1 - bit), (kept, bit)):
        at = rows_at(side, half)
        out[:half, :width] = add_low(keep_a[at], came_a[at])
        out[:half, width:] = add_low(keep_b[at], came_b[at])
        if keep_a.shape[0] > quarter:
            out[half:, :width] = add_low(keep_a[quarter:], came_a[quarter:])
            out[half:, width:] = jnp.zeros((out.shape[0] - half, out.shape[1] - width), bf16)


def add_eighths(info, keep, came, send, kept, *, half):
    bit = info[BZ] >> 1
    for out, side in ((send, 1 - bit), (kept, bit)):
        at = rows_at(side, half)
        out[:half] = add_low(keep[at], came[at])
        if kept.shape[0] > half:
            out[half:] = add_low(keep[2 * half :], came[2 * half :])


def add_last(info, keep, came, total, *small):
    size = total.shape[0]
    total[...] = add_low(keep[:size], came[:size])
    if small:
        small[0][...] = add_low(keep[size:], came[size:])


def join_pieces(info, own, came, eighth):
    size = own.shape[0]
    bit = info[BZ] >> 1
    eighth[rows_at(bit, size)] = own[...]
    eighth[rows_at(1 - bit, size)] = came[...]


def join_eighths(info, own, came, quarter_a, quarter_b):
    size, width = own.shape[0], quarter_a.shape[1]
    bit = info[BZ] & 1
    for source, side in ((own, bit), (came, 1 - bit)):
        quarter_a[rows_at(side, size)] = source[:, :width]
        quarter_b[rows_at(side, size)] = source[:, width:]


def join_quarters(info, own_a, came_a, own_b, came_b, half_a, half_b):
    size = own_a.shape[0]
    for bit, own, came, half in (
        (info[BY], own_a, came_a, half_a),
        (info[BX], own_b, came_b, half_b),
    ):
        half[rows_at(bit, size)] = own[...]
        half[rows_at(1 - bit, size)] = came[...]


def finish_down(info, own_a, came_a, own_b, came_b, out, mark):
    mark[...] = jnp.zeros_like(mark)
    size = own_a.shape[0]
    for part, bit, own, came in ((0, info[BX], own_a, came_a), (1, info[BY], own_b, came_b)):
        for side, source in ((bit, own), (1 - bit, came)):
            at = rows_at(2 * part + side, size)
            out[at] = source[...].astype(f32)
            out.send(at)


def put(out, rows, columns, value):
    at = rows, pl.ds(columns, value.shape[1])
    out[at] = value.astype(f32)
    out.send(*at)


def finish_up(info, own_a, came_a, own_b, came_b, up, output, mark):
    mark[...] = jnp.zeros_like(mark)
    size, width = own_a.shape
    rest = up.shape[1] - width
    for side, source in ((info[BX], own_a), (1 - info[BX], came_a)):
        put(up, rows_at(side, size), 0, source[...])
    for side, source in ((info[BY], own_b), (1 - info[BY], came_b)):
        put(up, rows_at(side, size), width, source[:, :rest])
        at = slice(None), rows_at(side, size)
        output[at] = source[:, rest:].astype(f32)
        output.send(*at)


def finish_heads(info, own_a, came_a, own_b, came_b, query, key, value):
    size, width = own_a.shape
    own = query.shape[1]
    rest = width - own
    for side, source in ((info[BX], own_a), (1 - info[BX], came_a)):
        put(query, rows_at(side, size), 0, source[:, :own])
        put(key, rows_at(side, size), 0, source[:, own:])
    for side, source in ((info[BY], own_b), (1 - info[BY], came_b)):
        put(key, rows_at(side, size), rest, source[:, : own - rest])
        put(value, rows_at(side, size), 0, source[:, own - rest :])


class Reduction:
    def __init__(self, name, info, order):
        self.name, self.info, self.order = name, info, order

    def begin(self, halves):
        self.made = halves
        send_a, send_b, self.keep_a, self.keep_b = halves
        self.came = [flip_by(send_a, "dp", 1), flip_by(send_b, "dp", 2)]

    def staged(self, kernel, outs, *args, early=(), **fixed):
        bound = functools.partial(kernel, **fixed) if fixed else kernel
        self.made = call(bound, self.name + kernel.__name__, outs, self.info, *args, order=self.order, early=early)
        return self.made

    def quarters(self):
        (first, self.wide), (half, self.narrow) = self.keep_a.shape, self.keep_b.shape
        self.extra, self.quarter = first - half, half // 2
        a, b = ((self.quarter + self.extra, self.wide), bf16), ((self.quarter, self.narrow), bf16)
        send_a, self.keep_a, send_b, self.keep_b = self.staged(
            add_halves, [a, a, b, b], self.keep_a, self.came[0], self.keep_b, self.came[1]
        )
        self.came = [flip_by(send_a, "dp", 2), flip_by(send_b, "dp", 1)]

    def eighths(self):
        self.both = self.wide + self.narrow
        piece = ((self.quarter // 2 + self.extra, self.both), bf16)
        send, self.own = self.staged(
            add_quarters, [piece] * 2, self.keep_a, self.came[0], self.keep_b, self.came[1]
        )
        self.came = flip_by(send, "dp", 4)

    def pieces(self):
        size = self.quarter // 4
        piece = ((size + self.extra, self.both), bf16)
        send, self.own = self.staged(add_eighths, [piece] * 2, self.own, self.came, half=size)
        self.came = flip_by(send, "dp", 8)

    def total(self):
        outs = [((self.quarter // 4, self.both), bf16)]
        outs += [((self.extra, self.both), bf16)] if self.extra else []
        self.own, *small = [
            functools.reduce(
                lambda value, bit: add_low(value, flip_by(value, "dp", 1 << bit)),
                range(4, bits_of("dp")),
                made,
            )
            for made in self.staged(add_last, outs, self.own, self.came)
        ]
        self.small = small[0] if small else None
        self.came = flip_by(self.own, "dp", 8)

    def join_two_z(self):
        piece = ((self.quarter // 2, self.both), bf16)
        (self.own,) = self.staged(join_pieces, [piece], self.own, self.came)
        self.came = flip_by(self.own, "dp", 4)

    def join_z(self):
        outs = [((self.quarter, self.wide), bf16), ((self.quarter, self.narrow), bf16)]
        self.keep_a, self.keep_b = self.staged(join_eighths, outs, self.own, self.came)
        self.came = [flip_by(self.keep_a, "dp", 2), flip_by(self.keep_b, "dp", 1)]

    def join_two(self):
        outs = [((2 * self.quarter, self.wide), bf16), ((2 * self.quarter, self.narrow), bf16)]
        self.keep_a, self.keep_b = self.staged(
            join_quarters, outs, self.keep_a, self.came[0], self.keep_b, self.came[1]
        )
        self.came = [flip_by(self.keep_a, "dp", 1), flip_by(self.keep_b, "dp", 2)]

    def finish(self, kernel, outs):
        return self.staged(
            kernel, outs, self.keep_a, self.came[0], self.keep_b, self.came[1],
            early=[i for i, out in enumerate(outs) if out[0][0] > 8],
        )


def down_gradient(info, unit, active, unit_in, active_in, send_a, send_b, keep_a, keep_b):
    size = send_a.shape[0]
    unit, active, unit_in, active_in = ready(unit, active, unit_in, active_in)
    for side in range(2):
        for part, bit, outs in ((0, info[BX], (send_a, keep_a)), (1, info[BY], (send_b, keep_b))):
            at = rows_at(2 * part + (bit if side else 1 - bit), size)
            outs[side][...] = (
                t_dot(active[:, at], unit[...]) + t_dot(active_in[:, at], unit_in[...])
            ).astype(bf16)


def up_gradient(
    info, delta, first, delta_in, first_in, branch, branch_far, context, context_far, send_a, send_b, keep_a, keep_b,
    bias,
):
    size, width = send_a.shape
    rest = delta.shape[1] - width
    for side in range(2):
        for bit, outs, columns in (
            (info[BX], (send_a, keep_a), pl.ds(0, width)),
            (info[BY], (send_b, keep_b), pl.ds(width, rest)),
        ):
            at = rows_at(bit if side else 1 - bit, size)
            out = outs[side]
            out[:, : columns.size] = (
                t_dot(first[:, at], delta[:, columns]) + t_dot(first_in[:, at], delta_in[:, columns])
            ).astype(bf16)
            if columns.size == rest:
                out[:, rest:] = (dot(context[...], branch[:, at]) + dot(context_far[...], branch_far[:, at])).astype(
                    bf16
                )
    ones = jnp.ones((8, delta.shape[0]), bf16)
    bias[...] = dot(ones, delta[...]) + dot(ones, delta_in[...])


def head_gradients(
    info, tokens, query, query_far, key, key_far, value, value_far, shared, shared_in, bias, send_a, send_b, keep_a,
    keep_b,
):
    half, width = send_b.shape[0], send_a.shape[1]
    length, narrow = query.shape
    rest = width - narrow
    near, far = rows_at(info[BT], length), rows_at(1 - info[BT], length)
    for side in range(2):
        for bit, outs, sources in (
            (info[BX], (send_a, keep_a), ((query, query_far, 0, narrow), (key, key_far, 0, rest))),
            (info[BY], (send_b, keep_b), ((key, key_far, rest, narrow - rest), (value, value_far, 0, narrow))),
        ):
            at = rows_at(bit if side else 1 - bit, half)
            tokens_near, tokens_far = tokens[near, at], tokens[far, at]
            put_at = 0
            for left, right, first, count in sources:
                columns = pl.ds(first, count)
                outs[side][:half, pl.ds(put_at, count)] = (
                    t_dot(tokens_near, left[:, columns]) + t_dot(tokens_far, right[:, columns])
                ).astype(bf16)
                put_at += count
    ones = jnp.ones((8, length), bf16)
    query_sum = dot(ones, query[...]) + dot(ones, query_far[...])
    value_sum = dot(ones, value[...]) + dot(ones, value_far[...])
    sums = shared[...] + shared_in[...]
    pairs = [(sums[k : k + 1, :narrow], sums[k : k + 1, narrow:]) for k in range(5)]
    pairs += [(bias[:1, k * narrow : (k + 1) * narrow], bias[:1, (k + 1) * narrow : (k + 2) * narrow]) for k in (0, 2)]
    pairs += [(query_sum[:1], value_sum[:1])]
    block = jnp.concatenate([piece for pair in pairs for piece in pair], 0)
    block = jnp.concatenate([block, jnp.zeros((SMALL, rest), f32)], 1).astype(bf16)
    send_a[half:] = block
    keep_a[half:] = block


def attend(
    info, tokens, query_weight, key_weight, value_weight, query_bias, value_bias, segments, validity,
    context, query, key, value, raised, shares, shade, *, far,
):
    length = context.shape[1]
    row = 1 - info[BT] if far else info[BT]
    segments, validity = ready(segments, validity)
    mark = segments[pl.ds(row, 1)]
    seen = jnp.where(validity[pl.ds(row, 1)] > 0, mark, -1)
    column = jnp.broadcast_to(seen.astype(f32), (8, length)).T[:, :1]
    shade[...] = jnp.where(column == mark.astype(f32), 0.0, neg_large)
    tokens, query_weight, query_bias, value_bias = ready(tokens, query_weight, query_bias, value_bias)
    x = tokens[rows_at(row, length)]
    scale = 1.0 / math.sqrt(HD)
    query[...] = (
        (dot(x, query_weight[...]) + query_bias[...].astype(f32)[None]).astype(bf16) * bf16(scale)
    )
    query.send()
    (key_weight,) = ready(key_weight)
    key[...] = dot(x, key_weight[...]).astype(bf16)
    key.send()
    (value_weight,) = ready(value_weight)
    value[...] = (dot(x, value_weight[...]) + value_bias[...].astype(f32)[None]).astype(bf16)
    value.send()
    low = lax.broadcasted_iota(jnp.int32, (length, LANES), 1) < HD

    def body(pair, _):
        at = pl.ds(pl.multiple_of(pair * LANES, LANES), LANES)
        q, k, v = query[:, at], key[:, at], value[:, at]

        def logits_of(member):
            return dot_t(k, jnp.where(low if member == 0 else ~low, q, jnp.zeros_like(q))) + shade[...]

        coming = logits_of(0)
        for member in range(2):
            logits, coming = coming, logits_of(1) if member == 0 else None
            number = 2 * pair + member
            peak = jnp.max(logits, 0, keepdims=True)
            lifted = jnp.exp(logits - peak).astype(bf16)
            raised[number] = lifted
            raised.send(number)
            sums = t_dot(jnp.where(low if member == 0 else ~low, v, jnp.ones_like(v)), lifted)
            other = (1 - member) * HD
            share = 1.0 / sums[other : other + 1]
            shares[pl.ds(number, 1)] = share
            rows = pl.ds(pl.multiple_of(number * HD, HD), HD)
            context[rows] = (sums[member * HD : member * HD + HD] * share).astype(bf16)
            context.send(rows)
        return 0

    lax.fori_loop(0, context.shape[0] // LANES, body, 0)


def attend_back(
    info, branch, output_weight, shares, value, context, raised, key, query, query_weight, key_weight, value_weight,
    query_delta, key_delta, value_delta, part, context_delta,
):
    length = part.shape[0]
    branch, output_weight = ready(branch, output_weight)
    context_delta[...] = dot_t(output_weight[...], branch[...]).astype(bf16)
    value, context, raised, key, query = ready(value, context, raised, key, query)
    low = lax.broadcasted_iota(jnp.int32, (length, LANES), 1) < HD
    scale = 1.0 / math.sqrt(HD)

    def body(pair, _):
        at = pl.ds(pl.multiple_of(pair * LANES, LANES), LANES)
        queries, keys, values = [], [], []
        for member in range(2):
            rows = pl.ds(pl.multiple_of(pair * LANES + member * HD, HD), HD)
            delta = context_delta[rows].astype(f32) * shares[pl.ds(2 * pair + member, 1)]
            inner = jnp.sum(delta * context[rows].astype(f32), 0, keepdims=True)
            delta = delta.astype(bf16)
            none = jnp.zeros_like(delta)
            delta = jnp.concatenate([none, delta] if member else [delta, none], 0)
            lifted = raised[2 * pair + member]
            logit_delta = (lifted.astype(f32) * (dot(value[:, at], delta) - inner)).astype(bf16)
            values.append(dot_t(lifted, delta))
            keys.append(dot(logit_delta, query[:, at]))
            queries.append(t_dot(key[:, at], logit_delta)[member * HD : member * HD + HD])
        query_delta[:, at] = (jnp.concatenate(queries, 0) * scale).T.astype(bf16)
        key_delta[:, at] = jnp.where(low, keys[0], keys[1]).astype(bf16)
        value_delta[:, at] = (values[0] + values[1]).astype(bf16)
        return 0

    lax.fori_loop(0, query.shape[1] // LANES, body, 0)
    query_weight, key_weight, value_weight = ready(query_weight, key_weight, value_weight)
    part[...] = (
        dot_t(query_delta[...], query_weight[...])
        + dot_t(key_delta[...], key_weight[...])
        + dot_t(value_delta[...], value_weight[...])
    ).astype(part.dtype)


OB, FG, FS, DB, SG = range(5)


def center(inputs):
    shifted = inputs - jnp.mean(inputs, -1, keepdims=True)
    spread = jnp.mean(shifted * shifted, -1, keepdims=True)
    row_scale = lax.rsqrt(spread + norm_eps)
    return shifted * row_scale, row_scale


def norm_back(out_delta, normed, row_scale, norm_gain):
    scaled = out_delta * norm_gain
    first_mean = jnp.mean(scaled, -1, keepdims=True)
    second_mean = jnp.mean(scaled * normed, -1, keepdims=True)
    return row_scale * (scaled - first_mean - normed * second_mean)


def forward(
    info, context, output_near, tokens, context_in, output_far, up_far, down_far, up_near, down_near, vectors,
    bias_near, bias_far, first_low, first_normed, first_scale, active_near, active_far, slope_near, slope_far,
    second_normed, second_scale, summary, total,
):
    length = total.shape[0]
    step = length // 2
    halves = (pl.ds(0, step), pl.ds(step, step))
    base = info[BT] * length
    context, output_near = ready(context, output_near)
    for at in halves:
        heads = t_dot(context[:, at], output_near[...]) + t_dot(context_in[:, at], output_far[...])
        (tokens,) = ready(tokens)
        x = tokens[pl.ds(pl.multiple_of(base + at.start, step), step)].astype(f32)
        normed, scale = center(x + (heads + vectors[OB : OB + 1]))
        out = normed * vectors[FG : FG + 1] + vectors[FS : FS + 1]
        first_normed[at] = normed.astype(bf16)
        first_scale[at] = scale
        first_low[at] = out.astype(bf16)
        total[at] = out + vectors[DB : DB + 1]
    first_low.send()
    first_normed.send()
    first_scale.send()

    width = 6 * LANES
    groups = (
        (up_far, down_far, bias_far, active_far, slope_far),
        (up_near, down_near, bias_near, active_near, slope_near),
    )
    for up, down, bias, active, slope in groups:
        up, down = ready(up, down)

        def body(index, _, up=up, down=down, bias=bias, active=active, slope=slope):
            units = rows_at(index, width)

            def hidden_of(at):
                return dot(first_low[at], up[:, units]) + bias[:, units]

            coming = hidden_of(halves[0])
            for at in halves:
                hidden, coming = coming, hidden_of(halves[1]) if at is halves[0] else None
                share = 0.5 * (1.0 + lax.erf(hidden * root_half))
                low = (hidden * share).astype(bf16)
                active[at, units] = low
                slope[at, units] = (share + hidden * jnp.exp(-0.5 * hidden * hidden) * inv_root_tau).astype(bf16)
                total[at] += dot(low, down[units])
            active.send(slice(None), units)
            slope.send(slice(None), units)
            return 0

        lax.fori_loop(0, bias.shape[1] // width, body, 0)

    for at in halves:
        normed, scale = center(total[at])
        second_normed[at] = normed.astype(bf16)
        second_scale[at] = scale
        total[at] = normed * vectors[SG : SG + 1]
    rows = [total[pl.ds(info[PLACES + k], 1)] for k in range(summary.shape[0])]
    summary[...] = jnp.concatenate(rows, 0).astype(bf16)


def loss_back(
    info, near, far, upper, normed, scale, vectors, losses, query_gradient, second_delta, unit_delta, sums, all_rows,
    out_delta,
):
    width = upper.shape[1]
    all_rows[: near.shape[0]] = near[...]
    all_rows[near.shape[0] :] = far[...]
    here = info[BT] * near.shape[0] + info[BD] * 8
    places = near.shape[0] // 8
    count = all_rows.shape[0]
    block = min(256, count)
    score_scale = 1.0 / math.sqrt(width)
    own_passages = 4

    def body(index, sums_in):
        at = rows_at(index, block)
        rows = all_rows[at, :width]
        digits = all_rows[at, width:].astype(f32)
        scores = dot_t(rows, all_rows[:, :width]) * score_scale
        columns = lax.broadcasted_iota(jnp.int32, (block, count), 1) ^ here
        numbers = (lax.broadcasted_iota(jnp.int32, (block, 1), 0) + index * block) ^ here
        scores = jnp.where((columns & 7) < own_passages, scores, neg_large)
        peak = jnp.max(scores, -1, keepdims=True)
        raised = jnp.exp(scores - peak)
        total = jnp.sum(raised, -1, keepdims=True)
        target = (digits[:, 0:1] * 16.0 + digits[:, 1:2]).astype(jnp.int32)
        chosen = columns == target
        lost = peak + jnp.log(total) - jnp.sum(jnp.where(chosen, scores, 0.0), -1, keepdims=True)
        delta = raised / total - chosen.astype(f32)
        delta = jnp.where((numbers & 7) >= own_passages, delta, 0.0).astype(bf16)
        wide = delta.astype(f32)
        places_here = lax.broadcasted_iota(jnp.int32, (block, 8), 1)
        wanted = ((places_here >> 2) * places + info[BD]) * 8 + own_passages + (places_here & 3)
        mine = (numbers == wanted).astype(f32)
        own_losses = sums_in[0] + jnp.sum(mine * lost, 0, keepdims=True)
        own_delta = sums_in[1] + t_dot(mine.astype(bf16), delta)
        results = []
        for k in range(own_passages):
            column = (info[BT] * places + info[BD]) * 8 + k
            share = jnp.sum(jnp.where(columns == column, wide, 0.0), -1, keepdims=True)
            results.append(sums_in[2 + k] + jnp.sum(share * rows.astype(f32), 0, keepdims=True))
        return own_losses, own_delta, *results

    zero = jnp.zeros((1, width), f32)
    first = (jnp.zeros((1, 8), f32), jnp.zeros((8, count), f32), *[zero] * own_passages)
    if count == block:
        own_losses, own_delta, *passage_delta = body(0, first)
    else:
        own_losses, own_delta, *passage_delta = lax.fori_loop(0, count // block, body, first)
    upper, normed, scale = ready(upper, normed, scale)
    out_delta[...] = upper[...].astype(f32)
    for k in range(own_passages):
        out_delta[pl.ds(info[PLACES + k], 1)] += passage_delta[k] * score_scale
    query_gradient[...] = dot(own_delta.astype(bf16), all_rows[:, :width]) * score_scale
    losses[...] = own_losses

    length = upper.shape[0]
    step = length // 4
    bias_sum = gain_sum = zero
    for start in range(0, length, step):
        at = pl.ds(start, step)
        n = normed[at].astype(f32)
        delta = norm_back(out_delta[at], n, scale[at], vectors[SG : SG + 1])
        unit_delta[at] = delta.astype(bf16)
        second_delta[at] = delta
        bias_sum += jnp.sum(delta, 0, keepdims=True)
        gain_sum += jnp.sum(out_delta[at] * n, 0, keepdims=True)
    sums[...] = jnp.concatenate(
        [jnp.zeros((DB, width), f32), bias_sum, gain_sum, jnp.zeros((7 - SG, width), f32)], 0
    )


def unit_back(info, unit_delta, down_weight, slope, hidden_delta):
    width = 6 * LANES

    def body(index, _):
        units = rows_at(index, width)
        delta = dot_t(unit_delta[...], down_weight[units])
        hidden_delta[:, units] = (delta * slope[:, units].astype(f32)).astype(bf16)
        return 0

    lax.fori_loop(0, down_weight.shape[0] // width, body, 0)


def first_back(
    info, delta_far, up_far, delta_near, up_near, second_delta, normed, scale, vectors, sums_in, first_delta,
    branch, sums, total,
):
    length, width = total.shape
    delta_far, up_far = ready(delta_far, up_far)
    total[...] = dot_t(delta_far[...], up_far[...])
    delta_near, up_near = ready(delta_near, up_near)
    total[...] += dot_t(delta_near[...], up_near[...])
    second_delta, normed = ready(second_delta, normed)
    step = length // 4
    zero = jnp.zeros((1, width), f32)
    bias_sum = gain_sum = shift_sum = zero
    for start in range(0, length, step):
        at = pl.ds(start, step)
        out_delta = second_delta[at] + total[at]
        n = normed[at].astype(f32)
        delta = norm_back(out_delta, n, scale[at], vectors[FG : FG + 1])
        branch[at] = delta.astype(bf16)
        first_delta[at] = delta
        bias_sum += jnp.sum(delta, 0, keepdims=True)
        gain_sum += jnp.sum(out_delta * n, 0, keepdims=True)
        shift_sum += jnp.sum(out_delta, 0, keepdims=True)
    sums[...] = sums_in[...] + jnp.concatenate(
        [bias_sum, gain_sum, shift_sum, jnp.zeros((7 - FS, width), f32)], 0
    )


def shards(
    tokens,
    upper_delta,
    segments,
    summary_index,
    validity,
    queries,
    positives,
    query_weight,
    key_weight,
    value_weight,
    query_bias,
    value_bias,
    output_weight,
    output_bias,
    first_gain,
    first_shift,
    up_weight,
    up_bias,
    down_weight,
    down_bias,
    second_gain,
):
    row_count, length = segments.shape
    token_count = row_count * length
    members = lax.axis_size("tensor")
    place = lax.axis_index("tensor")
    own_count = token_count // members
    width_local = query_weight.shape[1]
    heads_local = width_local // HD
    at_dp = lax.axis_index("dp")
    half_rows = D // 2

    def own(value):
        part = value.shape[0] // members
        return lax.dynamic_slice_in_dim(value, place * part, part, 0)

    info = jnp.concatenate(
        [
            jnp.stack([at_dp & 1, (at_dp >> 1) & 1, (at_dp >> 2) & 3, place, at_dp]).astype(jnp.int32),
            own(summary_index).reshape(-1),
        ]
    )
    vectors = jnp.stack([output_bias, first_gain, first_shift, down_bias, second_gain]).astype(f32)
    vectors = jnp.concatenate([vectors, jnp.zeros((3, D), f32)], 0)
    output_far = swap(output_weight)
    up_far = swap(up_weight)
    bias_far = swap(up_bias.reshape(1, -1))
    down_far = swap(down_weight)

    context_shape = ((length, width_local), bf16)

    def attention(far):
        return call(
            functools.partial(attend, far=far),
            "attend_far" if far else "attend_near",
            [((width_local, length), bf16)] + [context_shape] * 3
            + [((heads_local, length, length), bf16), ((heads_local + -heads_local % 8, length), f32)],
            info, tokens, query_weight, key_weight, value_weight, query_bias, value_bias, segments, validity,
            scratch=[pltpu.VMEM((length, length), f32)],
            late=(7, 8, 1, 2, 5, 6, 3, 4) if far else (),
            early=(0, 1, 2, 3, 4, 5),
        )

    context_far, query_far, key_far, value_far, raised_far, shares_far = attention(True)
    context_in = swap(context_far)
    context, query, key, value, raised, shares = attention(False)

    row, units = ((length, D), bf16), ((length, up_weight.shape[1]), bf16)
    scale_shape = ((length, 1), f32)
    own_passages = summary_index.shape[1]
    (
        first_low, first_normed, first_scale, active, active_far, slope, slope_far, second_normed, second_scale,
        summary,
    ) = call(
        forward, "forward",
        [row, row, scale_shape, units, units, units, units, row, scale_shape, ((own_passages, D), bf16)],
        info, context, output_weight, tokens, context_in, output_far, up_far, down_far, up_weight, down_weight,
        vectors, up_bias.reshape(1, -1).astype(f32), bias_far.astype(f32),
        late=(1, 2, 3, 7, 8, 9), early=(0, 1, 2, 3, 4, 5, 6, 7, 8), grant=40,
        scratch=[pltpu.VMEM((length, D), f32)],
    )
    first_in = swap(first_low)
    active_in = swap(active_far)

    places = lax.axis_size("dp")
    row_of = ((positives % 8) // 4 * places + positives // 8) * 8 + positives % 4
    digits = jnp.stack([row_of // 16, row_of % 16], 1).astype(bf16)
    digits = jnp.pad(digits, ((0, 0), (0, LANES - 2)))
    bundle = jnp.concatenate(
        [jnp.pad(summary, ((0, 0), (0, LANES))), own(jnp.concatenate([queries, digits], 1))], 0
    )
    for low in (1, 4):
        bundle = jnp.concatenate([bundle, *[flip_by(bundle, "dp", low * k) for k in (1, 2, 3)]], 0)
    for bit in range(4, bits_of("dp")):
        bundle = jnp.concatenate([bundle, flip_by(bundle, "dp", 1 << bit)], 0)
    bundle_far = swap(bundle)
    gathered = 2 * bundle.shape[0]
    query_count = queries.shape[0]
    losses, query_gradient, second_delta, unit_delta, sums = call(
        loss_back, "loss_back",
        [((1, query_count), f32), ((query_count, D), f32), ((length, D), f32), row, ((8, D), f32)],
        info, bundle, bundle_far, upper_delta, second_normed, second_scale, vectors,
        late=(3, 4, 5), final=(0, 1), grant=20 if gathered <= 256 else 50,
        scratch=[pltpu.VMEM((gathered, D + LANES), bf16), pltpu.VMEM((length, D), f32)],
    )
    unit_in = swap(unit_delta)
    order = []

    def through_units(name, weight, slope):
        return call(
            unit_back, name, [units], info, unit_delta, weight, slope, order=order
        )[0]

    delta_far = through_units("unit_back_far", down_far, slope_far)
    delta_in = swap(delta_far)
    down, up, heads = [Reduction(name, info, order) for name in ("down_", "up_", "heads_")]
    held = {}
    wide_shape, mark = (query_weight.shape, f32), ((8, LANES), f32)
    down.begin(
        call(
            down_gradient, "down_gradient", [((half_rows, D), bf16)] * 4, info, unit_delta, active, unit_in, active_in,
            order=order,
        )
    )

    def two_parts(columns, extra=0):
        wide = (columns // 2 + LANES - 1) // LANES * LANES
        first, second = ((half_rows + extra, wide), bf16), ((half_rows, columns - wide), bf16)
        return [first, second, first, second]

    def near_units():
        held["delta"] = through_units("unit_back_near", down_weight, slope)

    def first_norm():
        held["first_delta"], held["branch"], held["shared"] = call(
            first_back, "first_back", [((length, D), f32), row, ((8, D), f32)], info, delta_far, up_far,
            held["delta"], up_weight, second_delta, first_normed, first_scale, vectors, sums,
            scratch=[pltpu.VMEM((length, D), f32)], order=order,
        )
        held["branch_far"], held["shared_in"] = swap(held["branch"]), swap(held["shared"])

    def up_begin():
        *halves, held["bias"] = call(
            up_gradient, "up_gradient",
            two_parts(up_weight.shape[1] + width_local) + [((8, up_weight.shape[1]), f32)],
            info, held["delta"], first_low, delta_in, first_in, held["branch"], held["branch_far"], context,
            context_far, order=order,
        )
        up.begin(halves)

    def attention_back(name, branch, shares, raised, query, key, value, context, kind):
        return call(
            attend_back,
            name,
            [context_shape] * 3 + [((length, D), kind)],
            info, branch, output_weight, shares, value, context, raised, key, query, query_weight, key_weight,
            value_weight,
            scratch=[pltpu.VMEM((width_local, length), bf16)],
            order=order,
        )

    def near_row():
        held["near"] = attention_back(
            "attend_back_near", held["branch"], shares, raised, query, key, value, context, f32
        )

    def far_row():
        held["far"] = attention_back(
            "attend_back_far", held["branch_far"], shares_far, raised_far, query_far, key_far, value_far, context_far,
            bf16,
        )
        held["part_in"] = swap(held["far"][3])

    def heads_begin():
        near, far = held["near"], held["far"]
        heads.begin(
            call(
                head_gradients, "head_gradients", two_parts(3 * width_local, SMALL), info, tokens, near[0], far[0],
                near[1], far[1], near[2], far[2], held["shared"], held["shared_in"], held["bias"], order=order,
            )
        )

    up_outs = [(up_weight.shape, f32), (output_weight.shape, f32), mark]
    stages = [
        near_units, first_norm, up_begin, down.quarters, near_row, down.eighths,
        far_row, up.quarters, down.pieces, heads_begin, down.total, up.eighths,
        heads.quarters, down.join_two_z, up.pieces, heads.eighths, down.join_z, up.total,
        heads.pieces, up.join_two_z, down.join_two, heads.total, up.join_z, heads.join_two_z,
        up.join_two, heads.join_z, down.finish, heads.join_two, up.finish,
    ]
    for stage in stages:
        if stage == down.finish:
            down_total = stage(finish_down, [(down_weight.shape, f32), mark])[0]
        elif stage == up.finish:
            up_total, output_total, _ = stage(finish_up, up_outs)
        else:
            stage()
    heads_total = heads.finish(finish_heads, [wide_shape] * 3)
    small_total = heads.small[:, :width_local].astype(f32).reshape(8, -1)
    token_gradient = (held["first_delta"] + held["near"][3] + held["part_in"].astype(f32)).astype(bf16)

    return (
        losses.reshape(-1),
        query_gradient,
        token_gradient,
        heads_total[0],
        heads_total[1],
        heads_total[2],
        small_total[7, :width_local],
        small_total[7, width_local:],
        output_total,
        small_total[OB],
        small_total[FG],
        small_total[FS],
        up_total,
        small_total[5:7].reshape(-1),
        down_total,
        small_total[DB],
        small_total[SG],
    )


def solution(mesh):
    in_specs = (
        P("dp", None),
        P(("dp", "tensor"), None),
        P("dp", None),
        P("dp", None),
        P("dp", None),
        P("dp", None),
        P("dp"),
        P(None, "tensor"),
        P(None, "tensor"),
        P(None, "tensor"),
        P("tensor"),
        P("tensor"),
        P("tensor", None),
        P(),
        P(),
        P(),
        P(None, "tensor"),
        P("tensor"),
        P("tensor", None),
        P(),
        P(),
    )
    out_specs = (
        P("dp"),
        P("dp", None),
        P(("dp", "tensor"), None),
        P(None, "tensor"),
        P(None, "tensor"),
        P(None, "tensor"),
        P("tensor"),
        P("tensor"),
        P("tensor", None),
        P(),
        P(),
        P(),
        P(None, "tensor"),
        P("tensor"),
        P("tensor", None),
        P(),
        P(),
    )
    return jax.shard_map(shards, mesh=mesh, in_specs=in_specs, out_specs=out_specs, check_vma=False)
```
